32 devices in a mesh: fsdp: 4 (over y, x), expert: 8 (over z, core).
Axes of the slice: x: 2, y: 2, z: 4, core: 2. Of those that a mesh axis runs over, the one named last changes fastest.
Arguments:
- patches: bfloat16 [64, 197, 768], P(('fsdp', 'expert')), may hold values from -6 to 6
- dense_gains: bfloat16 [2, 768], P(None, ('fsdp', 'expert')), may hold values from 0.25 to 1.75
- dense_shifts: bfloat16 [6, 768], P(None, ('fsdp', 'expert')), may hold values from -1.796875 to 1.796875
- dense_qkv: bfloat16 [768, 2304], P(('fsdp', 'expert')), may hold values from -0.3125 to 0.3125
- dense_proj: bfloat16 [768, 768], P(('fsdp', 'expert')), may hold values from -0.75 to 0.75
- dense_fc_in: bfloat16 [768, 3072], P(('fsdp', 'expert')), may hold values from -0.21875 to 0.21875
- dense_fc_bias: bfloat16 [3072], P(('fsdp', 'expert')), may hold values from -1.796875 to 1.796875
- dense_fc_out: bfloat16 [3072, 768], P(('fsdp', 'expert')), may hold values from -0.15625 to 0.15625
- moe_gains: bfloat16 [2, 768], P(None, ('fsdp', 'expert')), may hold values from 0.25 to 1.75
- moe_shifts: bfloat16 [5, 768], P(None, ('fsdp', 'expert')), may hold values from -1.796875 to 1.796875
- moe_qkv: bfloat16 [768, 2304], P(('fsdp', 'expert')), may hold values from -0.3125 to 0.3125
- moe_proj: bfloat16 [768, 768], P(('fsdp', 'expert')), may hold values from -0.75 to 0.75
- router: bfloat16 [768, 8], P(('fsdp', 'expert')), may hold values from -0.15625 to 0.15625
- expert_in: bfloat16 [8, 768, 3072], P('expert', 'fsdp'), may hold values from -0.21875 to 0.21875
- expert_in_bias: bfloat16 [8, 3072], P('expert', 'fsdp'), may hold values from -1.1953125 to 1.1953125
- expert_out: bfloat16 [8, 3072, 768], P('expert', 'fsdp'), may hold values from -0.4375 to 0.4375
- expert_out_bias: bfloat16 [8, 768], P('expert', 'fsdp'), may hold values from -1.796875 to 1.796875
- routes: int32 [64, 197, 2], P(('fsdp', 'expert')), may hold values from 0 to 7, as said below
- slot_pos: int32 [64, 197, 2], P(('fsdp', 'expert')), may hold values from -1 to 93, as said below
- image_counts: int32 [32], P(('fsdp', 'expert')), may hold values from 1 to 2, as said below
- cotangent: bfloat16 [64, 197, 768], P(('fsdp', 'expert')), may hold values from -6 to 6
Outputs:
- output_tokens: bfloat16 [64, 197, 768], P(('fsdp', 'expert'))
- patches_grad: float32 [64, 197, 768], P(('fsdp', 'expert'))
- dense_gains_grad: float32 [2, 768], P(None, ('fsdp', 'expert'))
- dense_shifts_grad: float32 [6, 768], P(None, ('fsdp', 'expert'))
- dense_qkv_grad: float32 [768, 2304], P(('fsdp', 'expert'))
- dense_proj_grad: float32 [768, 768], P(('fsdp', 'expert'))
- dense_fc_in_grad: float32 [768, 3072], P(('fsdp', 'expert'))
- dense_fc_bias_grad: float32 [3072], P(('fsdp', 'expert'))
- dense_fc_out_grad: float32 [3072, 768], P(('fsdp', 'expert'))
- moe_gains_grad: float32 [2, 768], P(None, ('fsdp', 'expert'))
- moe_shifts_grad: float32 [5, 768], P(None, ('fsdp', 'expert'))
- moe_qkv_grad: float32 [768, 2304], P(('fsdp', 'expert'))
- moe_proj_grad: float32 [768, 768], P(('fsdp', 'expert'))
- router_grad: float32 [768, 8], P(('fsdp', 'expert'))
- expert_in_grad: float32 [8, 768, 3072], P('expert', 'fsdp')
- expert_in_bias_grad: float32 [8, 3072], P('expert', 'fsdp')
- expert_out_grad: float32 [8, 3072, 768], P('expert', 'fsdp')
- expert_out_bias_grad: float32 [8, 768], P('expert', 'fsdp')
The draws below stay inside these ranges and needn't reach their ends.
Inputs may be any that keep to these rules, and one draw needn't show every extreme that they name: `routes`: each token names two different experts. `slot_pos`: within one block of 2 images, the placed entries that name one expert hold distinct slots; entries of images beyond the block's live count are -1, and some live entries are -1 where an expert's slots run out. In every block some expert has all 94 slots filled. A device's live images are its first image_counts image slots.
All inputs are finite; a program needn't handle non-finite values.
Results may differ from the reference program's by a relative error of at most 0.02.
Values may be sent and summed in bfloat16 or wider, within the bound.
No kernel may reach another device: no remote copies, remote signals or barrier semaphores. Data moves between devices by JAX's collectives and lax.ppermute only.
A program may use at most 256 MiB of HBM per device.

```python
import math
import jax
import jax.numpy as jnp
from jax import lax

D = 768
HEADS = 12
HEAD = 64
FF = 3072
SEQ = 197
IMG_DEV = 2
TOK_DEV = 394
IMAGES = 64
EXPERTS = 8
CAP = 94
N_FSDP = 4
N_EXPERT = 8


def joint_plan(key):
    devices = IMAGES // IMG_DEV
    lowest = (IMG_DEV + 1) // 2
    tokens = IMG_DEV * SEQ
    entries = tokens * 2
    key_count, key_full, key_low, key_first, key_hot, key_second, key_order = jax.random.split(key, 7)
    counts = jax.random.randint(key_count, (devices,), lowest, IMG_DEV + 1)
    full_device = jax.random.randint(key_full, (), 0, devices)
    low_device = (full_device + 1 + jax.random.randint(key_low, (), 0, devices - 1)) % devices
    places = jnp.arange(devices)
    counts = jnp.where(places == full_device, IMG_DEV, jnp.where(places == low_device, lowest, counts))
    first_pick = jax.random.randint(key_first, (devices, tokens), 0, EXPERTS)
    hot_expert = jax.random.randint(key_hot, (), 0, EXPERTS)
    first_pick = jnp.where(jnp.arange(tokens)[None, :] < CAP + 4, hot_expert, first_pick)
    second_pick = (first_pick + 1 + jax.random.randint(key_second, (devices, tokens), 0, EXPERTS - 1)) % EXPERTS
    route_all = jnp.stack([first_pick, second_pick], axis=-1)
    live_mask = jnp.arange(tokens)[None, :] // SEQ < counts[:, None]
    flat_routes = route_all.reshape(devices, entries)
    flat_live = jnp.repeat(live_mask, 2, axis=1)
    orders = jax.vmap(lambda subkey: jax.random.permutation(subkey, entries))(jax.random.split(key_order, devices))

    def rank_one(perm_order, chosen, is_alive):
        onehot = ((chosen[:, None] == jnp.arange(EXPERTS)[None, :]) & is_alive[:, None]).astype(jnp.int32)
        sorted_hot = onehot[perm_order]
        before = jnp.cumsum(sorted_hot, axis=0) - sorted_hot
        position = jnp.zeros((entries,), jnp.int32).at[perm_order].set(jnp.arange(entries, dtype=jnp.int32))
        rank_now = jnp.sum(before[position] * onehot, axis=1)
        return jnp.where(is_alive & (rank_now < CAP), rank_now, -1)
    slot_all = jax.vmap(rank_one)(orders, flat_routes, flat_live)
    return (counts.astype(jnp.int32), route_all.reshape(IMAGES, SEQ, 2).astype(jnp.int32), slot_all.reshape(IMAGES, SEQ, 2).astype(jnp.int32))


def draw_routes(key, part):
    shared = joint_plan(key)
    return shared[1]


def draw_slot_pos(key, part):
    shared = joint_plan(key)
    return shared[2]


def draw_image_counts(key, part):
    shared = joint_plan(key)
    return shared[0]


def with_spikes(values, own_key, source, target, blocks, factor):
    owner, partner = [(jnp.arange(values.shape[dim]) // (values.shape[dim] // blocks)).reshape([-1 if axis == dim else 1 for axis in range(values.ndim)]) for dim in (source, target)]
    chosen = jax.random.permutation(own_key, blocks)[partner]
    strong = (owner == chosen) | (owner == (partner + blocks // 2) % blocks)
    return jnp.where(strong, factor * values, values)


def block_levels(key, shape, cuts, low, high):
    gain = 1.0
    for axis_at, shards_of in cuts:
        steps = jax.random.uniform(jax.random.fold_in(jax.random.fold_in(key, 6), axis_at), (shards_of,), jnp.float32, low / len(cuts), high / len(cuts))
        gain = gain * jnp.repeat(jnp.exp(steps), shape[axis_at] // shards_of).reshape((-1,) + (1,) * (len(shape) - 1 - axis_at))
    return gain


def noise(rng, dims, width, reach, pieces=(), kind=jnp.bfloat16):
    values = jax.random.normal(rng, dims, jnp.float32) * width
    if len(pieces) > 0:
        values = block_levels(rng, dims, pieces, -0.22, 0.18) * values
    return jnp.clip(values, min=-reach, max=reach).astype(kind)


def noise_with(rng, extent, width, most, shards, heavy, held_as=jnp.bfloat16):
    values = width * jax.random.normal(rng, extent, jnp.float32)
    if shards:
        values = values * block_levels(rng, extent, shards, -0.22, 0.18)
    return jnp.clip(with_spikes(values, jax.random.fold_in(rng, 3), *heavy), -most, most).astype(held_as)


def setup_inputs(seed: int = 0) -> dict:
    key_of = jax.random.split(jax.random.key(seed), 22)
    return {
        "patches": noise(key_of[0], (IMAGES, SEQ, D), 1.0, 6.0, ((0, 32),)),
        "dense_gains": jnp.clip(1.0 + 0.15 * jax.random.normal(key_of[1], (2, D), jnp.float32), 0.25, 1.75).astype(jnp.bfloat16),
        "dense_shifts": noise(key_of[2], (6, D), 0.3, 1.796875, ((1, 32),)),
        "dense_qkv": noise(key_of[3], (D, 3 * D), (D // 2) ** -0.5, 0.3125, ((0, 32),)),
        "dense_proj": noise(key_of[4], (D, D), (D // 12) ** -0.5, 0.75, ((0, 32),)),
        "dense_fc_in": noise(key_of[5], (D, FF), D ** -0.5, 0.21875, ((0, 32),)),
        "dense_fc_bias": noise(key_of[6], (FF,), 0.3, 1.796875, ((0, 32),)),
        "dense_fc_out": noise(key_of[7], (FF, D), (FF // 2) ** -0.5, 0.15625, ((0, 32),)),
        "moe_gains": jnp.clip(1.0 + 0.15 * jax.random.normal(key_of[8], (2, D), jnp.float32), 0.25, 1.75).astype(jnp.bfloat16),
        "moe_shifts": noise(key_of[9], (5, D), 0.3, 1.796875, ((1, 32),)),
        "moe_qkv": noise(key_of[10], (D, 3 * D), (D // 2) ** -0.5, 0.3125, ((0, 32),)),
        "moe_proj": noise(key_of[11], (D, D), (D // 12) ** -0.5, 0.75, ((0, 32),)),
        "router": noise(key_of[12], (D, EXPERTS), (2 * D) ** -0.5, 0.15625, ((0, 32),)),
        "expert_in": noise(key_of[13], (EXPERTS, D, FF), D ** -0.5, 0.21875, ((0, 8), (1, 4))),
        "expert_in_bias": noise(key_of[14], (EXPERTS, FF), 0.2, 1.1953125, ((0, 8), (1, 4))),
        "expert_out": noise(key_of[15], (EXPERTS, FF, D), (max(1, 4 * FF // (EXPERTS * EXPERTS))) ** -0.5, 0.4375, ((0, 8), (1, 4))),
        "expert_out_bias": noise(key_of[16], (EXPERTS, D), 0.3, 1.796875, ((0, 8), (1, 4))),
        "routes": draw_routes(jax.random.fold_in(key_of[21], 71), 0),
        "slot_pos": draw_slot_pos(jax.random.fold_in(key_of[21], 71), 0),
        "image_counts": draw_image_counts(jax.random.fold_in(key_of[21], 71), 0),
        "cotangent": noise_with(key_of[20], (IMAGES, SEQ, D), 1.0, 6.0, ((0, 32),), (0, 2, 32, 2.75)),
    }


@jax.custom_vjp
def low(v):
    return lax.optimization_barrier(v.astype(jnp.bfloat16)).astype(jnp.float32)

@jax.custom_vjp
def low_back(v):
    return v

def low_keep(v):
    return (low(v), None)

def low_pass(kept, grad):
    return (grad,)

def back_keep(v):
    return (v, None)

def back_low(kept, grad):
    return (low(grad),)
low.defvjp(low_keep, low_pass)
low_back.defvjp(back_keep, back_low)
eps_norm = 1e-06
highest = lax.Precision.HIGHEST

def norm_rows(values, norm_gain, norm_shift):
    center = values - lax.optimization_barrier(jnp.mean(values, axis=-1, keepdims=True))
    spread = lax.optimization_barrier(jnp.mean(center * center, axis=-1, keepdims=True))
    return center * lax.rsqrt(spread + eps_norm) * norm_gain + norm_shift

def attend(resid_in, norm_gain, norm_shift, qkv_full, q_bias, v_bias, proj_full, out_bias):
    images = resid_in.shape[0]
    normed = low(norm_rows(resid_in, norm_gain, norm_shift))
    proj_all = jnp.einsum('isd,de->ise', normed, qkv_full, precision=highest)
    split_heads = (images, SEQ, HEADS, HEAD)
    query_low = low(low_back(proj_all[..., :D] + q_bias)).reshape(split_heads)
    key_low = low(low_back(proj_all[..., D:2 * D])).reshape(split_heads)
    value_low = low(low_back(proj_all[..., 2 * D:] + v_bias)).reshape(split_heads)
    scores = low_back(jnp.einsum('ishd,ithd->ihst', query_low, key_low, precision=highest) * HEAD ** (-0.5))
    prob_full = jax.nn.softmax(scores, axis=-1)
    mixed_sum = jnp.einsum('ihst,ithd->ishd', low(prob_full), value_low, precision=highest)
    mixed_low = low(low_back(mixed_sum.reshape(images, SEQ, D)))
    branch = jnp.einsum('isd,de->ise', mixed_low, proj_full, precision=highest) + out_bias
    return low_back(branch)

def feed(resid_in, norm_gain, norm_shift, fc_in, fc_bias, fc_out, out_bias):
    normed = low(norm_rows(resid_in, norm_gain, norm_shift))
    pre_act = low_back(jnp.einsum('isd,df->isf', normed, fc_in, precision=highest) + fc_bias)
    act_low = low(jax.nn.gelu(pre_act, approximate=True))
    return low_back(jnp.einsum('isf,fd->isd', act_low, fc_out, precision=highest) + out_bias)

def experts_apply(resid_in, norm_gain, norm_shift, router, expert_in, expert_in_bias, expert_out, expert_out_bias, route_rows, slot_rows):
    normed = low(norm_rows(resid_in, norm_gain, norm_shift)).reshape(TOK_DEV, D)
    logits = jnp.dot(normed, router, precision=highest)
    gate_all = jax.nn.softmax(logits, axis=-1)
    picked = jnp.take_along_axis(gate_all, route_rows, axis=1)
    target = route_rows * CAP + slot_rows
    slot_table = ((target[:, :, None] == jnp.arange(EXPERTS * CAP, dtype=jnp.int32)[None, None, :]) & (slot_rows[:, :, None] >= 0)).astype(jnp.float32)
    buffer = low_back(jnp.einsum('tkc,td->cd', slot_table, normed, precision=highest)).reshape(EXPERTS, CAP, D)
    hidden = low_back(jnp.einsum('ecd,edf->ecf', buffer, expert_in, precision=highest) + expert_in_bias[:, None, :])
    act_low = low(jax.nn.gelu(hidden, approximate=True))
    result = low(low_back(jnp.einsum('ecf,efd->ecd', act_low, expert_out, precision=highest) + expert_out_bias[:, None, :]))
    fetched = jnp.einsum('tkc,cd->tkd', slot_table, result.reshape(EXPERTS * CAP, D), precision=highest)
    return lax.optimization_barrier(jnp.sum(picked[:, :, None] * fetched, axis=1)).reshape(resid_in.shape)

def device_forward(resid_in, live_mask, route_one, slot_one, params):
    dense_gains, dense_shifts, dense_qkv, dense_proj, dense_fc_in, dense_fc_bias, dense_fc_out, moe_gains, moe_shifts, moe_qkv, moe_proj, router, expert_in, expert_in_bias, expert_out, expert_out_bias = params
    resid_one = resid_in + attend(resid_in, dense_gains[0], dense_shifts[0], dense_qkv, dense_shifts[2], dense_shifts[3], dense_proj, dense_shifts[4])
    resid_two = resid_one + feed(resid_one, dense_gains[1], dense_shifts[1], dense_fc_in, dense_fc_bias, dense_fc_out, dense_shifts[5])
    resid_three = resid_two + attend(resid_two, moe_gains[0], moe_shifts[0], moe_qkv, moe_shifts[2], moe_shifts[3], moe_proj, moe_shifts[4])
    resid_four = resid_three + experts_apply(resid_three, moe_gains[1], moe_shifts[1], router, expert_in, expert_in_bias, expert_out, expert_out_bias, route_one, slot_one)
    return resid_four * live_mask[:, None, None]

def reference(patches, dense_gains, dense_shifts, dense_qkv, dense_proj, dense_fc_in, dense_fc_bias, dense_fc_out, moe_gains, moe_shifts, moe_qkv, moe_proj, router, expert_in, expert_in_bias, expert_out, expert_out_bias, routes, slot_pos, image_counts, cotangent):
    devices = N_FSDP * N_EXPERT
    together = math.gcd(8, devices)
    weights = tuple((array.astype(jnp.float32) for array in (dense_gains, dense_shifts, dense_qkv, dense_proj, dense_fc_in, dense_fc_bias, dense_fc_out, moe_gains, moe_shifts, moe_qkv, moe_proj, router, expert_in, expert_in_bias, expert_out, expert_out_bias)))
    resid_start = patches.astype(jnp.float32).reshape(devices, IMG_DEV, SEQ, D)
    live_mask = (jnp.arange(IMG_DEV, dtype=jnp.int32)[None, :] < image_counts[:, None]).astype(jnp.float32)
    route_dev = routes.reshape(devices, TOK_DEV, 2)
    slot_dev = slot_pos.reshape(devices, TOK_DEV, 2)

    def grouped(array):
        return array.reshape((devices // together, together) + array.shape[1:])

    def forward(resid_all, params):

        def one_device(resid_one, live_one, route_one, slot_one):
            return device_forward(resid_one, live_one, route_one, slot_one, params)

        def one_group(group_args):
            return jax.vmap(one_device)(*group_args)
        result = lax.map(jax.checkpoint(one_group), (grouped(resid_all), grouped(live_mask), grouped(route_dev), grouped(slot_dev)))
        return result.reshape(resid_all.shape)
    output_all, pullback = jax.vjp(forward, resid_start, weights)
    resid_grad, weight_grads = pullback(cotangent.astype(jnp.float32).reshape(resid_start.shape))
    whole_shape = (IMAGES, SEQ, D)
    return (output_all.reshape(whole_shape).astype(jnp.bfloat16), resid_grad.reshape(whole_shape), weight_grads[0], weight_grads[1], weight_grads[2], weight_grads[3], weight_grads[4], weight_grads[5], weight_grads[6], weight_grads[7], weight_grads[8], weight_grads[9], weight_grads[10], weight_grads[11], weight_grads[12], weight_grads[13], weight_grads[14], weight_grads[15])
```

```python
from functools import partial

import jax
import jax.numpy as jnp
from jax import lax
from jax.sharding import PartitionSpec as P

HEADS = 12


eps_norm = 1e-06
highest = lax.Precision.HIGHEST


def trade(value, axis_name, mask):
    count = lax.axis_size(axis_name)
    return lax.ppermute(value, axis_name, [(place, place ^ mask) for place in range(count)])


def in_order(pieces, place):
    level = 0
    while len(pieces) > 1:
        flip = ((place >> level) & 1) == 1
        pieces = [
            jnp.where(
                flip,
                jnp.concatenate([pieces[at + 1], pieces[at]], axis=0),
                jnp.concatenate([pieces[at], pieces[at + 1]], axis=0),
            )
            for at in range(0, len(pieces), 2)
        ]
        level += 1
    return pieces[0]


def plane_gather(piece):
    count = lax.axis_size("fsdp")
    place = lax.axis_index("fsdp")
    if count == 4:
        half = piece.shape[0] // 2
        from_x = trade(piece, "fsdp", 1)
        from_y = trade(piece, "fsdp", 2)
        far_low = trade(from_y[:half], "fsdp", 1)
        far_high = trade(from_x[half:], "fsdp", 2)
        pieces = [piece, from_x, from_y, jnp.concatenate([far_low, far_high], axis=0)]
    else:
        pieces = [piece] + [trade(piece, "fsdp", mask) for mask in range(1, count)]
    return in_order([part[None] for part in pieces], place)


def plane_sum(blocks):
    count = lax.axis_size("fsdp")
    place = lax.axis_index("fsdp")

    def part(mask):
        return lax.dynamic_index_in_dim(blocks, place ^ mask, 0, keepdims=False)

    if count == 4:
        half = blocks.shape[1] // 2
        far = part(3)
        near_x = part(1)
        near_y = part(2)
        got_low = trade(far[:half], "fsdp", 1)
        got_high = trade(far[half:], "fsdp", 2)
        mixed_x = (near_x[half:].astype(jnp.float32) + got_high.astype(jnp.float32)).astype(
            jnp.bfloat16
        )
        mixed_y = (near_y[:half].astype(jnp.float32) + got_low.astype(jnp.float32)).astype(
            jnp.bfloat16
        )
        from_x = trade(jnp.concatenate([near_x[:half], mixed_x], axis=0), "fsdp", 1)
        from_y = trade(jnp.concatenate([mixed_y, near_y[half:]], axis=0), "fsdp", 2)
        arrived = [from_x, from_y]
    else:
        arrived = [trade(part(mask), "fsdp", mask) for mask in range(1, count)]
    total = part(0).astype(jnp.float32)
    for term in arrived:
        total = total + term.astype(jnp.float32)
    return total


def shared_gather(shard, before):
    side = lax.axis_index("expert") % 2
    layer = lax.axis_index("expert") // 2
    layers = lax.axis_size("expert") // 2
    if before is not None:
        shard, _ = lax.optimization_barrier((shard, before))
    stacked = [shard] + [trade(shard, "expert", 2 * mask) for mask in range(1, layers)]
    block = in_order([part[None] for part in stacked], layer)
    mark = block
    block = plane_gather(block)
    other = trade(block, "expert", 1)
    full = jnp.where(
        side == 0, jnp.stack([block, other], axis=2), jnp.stack([other, block], axis=2)
    )
    return full.reshape(-1, shard.shape[-1]), mark


def shared_sum(half_grad):
    side = lax.axis_index("expert") % 2
    layer = lax.axis_index("expert") // 2
    layers = lax.axis_size("expert") // 2
    planes = lax.axis_size("fsdp")
    width = half_grad.shape[-1]
    held = plane_sum(half_grad.reshape(planes, layers, -1, width)).astype(jnp.bfloat16)

    def part(mask):
        return lax.dynamic_index_in_dim(held, layer ^ mask, 0, keepdims=False)

    total = part(0).astype(jnp.float32)
    for mask in range(1, layers):
        total = total + trade(part(mask), "expert", 2 * mask).astype(jnp.float32)
    rows = total.shape[0] // 2
    mine = lax.dynamic_slice_in_dim(total, side * rows, rows, 0)
    away = lax.dynamic_slice_in_dim(total, (1 - side) * rows, rows, 0).astype(jnp.bfloat16)
    came = trade(away, "expert", 1).astype(jnp.float32)
    return jnp.where(
        side == 0,
        jnp.concatenate([mine, came], axis=-1),
        jnp.concatenate([came, mine], axis=-1),
    )


def pair_product(left, right):
    side = lax.axis_index("expert") % 2
    half = right.shape[-1] // 2
    left_far = trade(left, "expert", 1)
    mine = lax.dynamic_slice_in_dim(right, side * half, half, 1)
    away = lax.dynamic_slice_in_dim(right, (1 - side) * half, half, 1)
    right_far = trade(away, "expert", 1)
    return jnp.dot(
        jnp.concatenate([left, left_far], axis=0).T,
        jnp.concatenate([mine, right_far], axis=0),
        preferred_element_type=jnp.float32,
    ).astype(jnp.bfloat16)


def half_of(whole):
    side = lax.axis_index("expert") % 2
    half = whole.shape[-1] // 2
    own = lax.dynamic_slice_in_dim(whole, side * half, half, 1)
    away = lax.dynamic_slice_in_dim(whole, (1 - side) * half, half, 1)
    return (own + trade(away, "expert", 1)).astype(jnp.bfloat16)


def norm_rows(values, norm_gain, norm_shift):
    center = values - jnp.mean(values, axis=-1, keepdims=True)
    spread = jnp.mean(center * center, axis=-1, keepdims=True)
    return center * lax.rsqrt(spread + eps_norm) * norm_gain + norm_shift


def norm_back(values, norm_gain, norm_shift, upstream):
    _, pullback = jax.vjp(norm_rows, values, norm_gain, norm_shift)
    return pullback(upstream)


def smooth_gate(values):
    return jax.nn.gelu(values, approximate=True)


def smooth_back(values, upstream):
    _, pullback = jax.vjp(smooth_gate, values)
    return pullback(upstream)[0]


def pick_gates(logits, route_rows):
    gate_all = jax.nn.softmax(logits, axis=-1)
    choose = route_rows[:, :, None] == jnp.arange(logits.shape[-1])[None, None, :]
    return jnp.sum(jnp.where(choose, gate_all[:, None, :], 0.0), axis=-1)


def attend_forward(resid_in, norm_gain, norm_shift, q_bias, v_bias, out_bias, qkv_full, proj_full):
    images, length, model_width = resid_in.shape
    normed_low = norm_rows(resid_in, norm_gain, norm_shift).astype(jnp.bfloat16)
    proj_all = jnp.einsum("isd,de->ise", normed_low, qkv_full, preferred_element_type=jnp.float32)
    split_heads = (images, length, HEADS, model_width // HEADS)
    query_low = (proj_all[..., :model_width] + q_bias).astype(jnp.bfloat16).reshape(split_heads)
    key_low = proj_all[..., model_width : 2 * model_width].astype(jnp.bfloat16).reshape(split_heads)
    value_low = (
        (proj_all[..., 2 * model_width :] + v_bias).astype(jnp.bfloat16).reshape(split_heads)
    )
    score_scale = (model_width // HEADS) ** (-0.5)
    scores = (
        jnp.einsum("ishd,ithd->ihst", query_low, key_low, preferred_element_type=jnp.float32)
        * score_scale
    )
    row_top = jnp.max(scores, axis=-1, keepdims=True)
    log_total = row_top + jnp.log(jnp.sum(jnp.exp(scores - row_top), axis=-1, keepdims=True))
    prob_low = jnp.exp(scores - log_total).astype(jnp.bfloat16)
    mixed_sum = jnp.einsum(
        "ihst,ithd->ishd", prob_low, value_low, preferred_element_type=jnp.float32
    )
    mixed_low = mixed_sum.reshape(images, length, model_width).astype(jnp.bfloat16)
    branch = (
        jnp.einsum("isd,de->ise", mixed_low, proj_full, preferred_element_type=jnp.float32)
        + out_bias
    )
    return (resid_in + branch, (normed_low, query_low, key_low, value_low, log_total, mixed_low))


def attend_backward(grad_in, resid_in, norm_gain, norm_shift, qkv_full, proj_full, kept_state):
    normed_low, query_low, key_low, value_low, log_total, mixed_low = kept_state
    images, length, model_width = resid_in.shape
    score_scale = (model_width // HEADS) ** (-0.5)
    grad_low = grad_in.astype(jnp.bfloat16)
    proj_grad = pair_product(
        mixed_low.reshape(-1, model_width), grad_low.reshape(-1, model_width)
    )
    out_bias_grad = jnp.sum(grad_low.astype(jnp.float32), axis=(0, 1))
    mixed_grad = jnp.einsum("ise,de->isd", grad_low, proj_full, preferred_element_type=jnp.float32)
    mixed_grad = mixed_grad.astype(jnp.bfloat16).reshape(query_low.shape)
    scores = (
        jnp.einsum("ishd,ithd->ihst", query_low, key_low, preferred_element_type=jnp.float32)
        * score_scale
    )
    prob_full = jnp.exp(scores - log_total)
    prob_grad = jnp.einsum(
        "ishd,ithd->ihst", mixed_grad, value_low, preferred_element_type=jnp.float32
    )
    value_grad = jnp.einsum(
        "ihst,ishd->ithd",
        prob_full.astype(jnp.bfloat16),
        mixed_grad,
        preferred_element_type=jnp.float32,
    )
    score_grad = prob_full * (prob_grad - jnp.sum(prob_grad * prob_full, axis=-1, keepdims=True))
    score_grad = score_grad.astype(jnp.bfloat16)
    query_grad = (
        jnp.einsum("ihst,ithd->ishd", score_grad, key_low, preferred_element_type=jnp.float32)
        * score_scale
    )
    key_grad = (
        jnp.einsum("ihst,ishd->ithd", score_grad, query_low, preferred_element_type=jnp.float32)
        * score_scale
    )
    whole_shape = (images, length, model_width)
    query_grad = query_grad.astype(jnp.bfloat16).reshape(whole_shape)
    key_grad = key_grad.astype(jnp.bfloat16).reshape(whole_shape)
    value_grad = value_grad.astype(jnp.bfloat16).reshape(whole_shape)
    proj_all_grad = jnp.concatenate([query_grad, key_grad, value_grad], axis=-1)
    qkv_grad = pair_product(
        normed_low.reshape(-1, model_width), proj_all_grad.reshape(-1, 3 * model_width)
    )
    normed_grad = jnp.einsum(
        "ise,de->isd", proj_all_grad, qkv_full, preferred_element_type=jnp.float32
    )
    resid_grad, gain_grad, shift_grad = norm_back(resid_in, norm_gain, norm_shift, normed_grad)
    q_bias_grad = jnp.sum(query_grad.astype(jnp.float32), axis=(0, 1))
    v_bias_grad = jnp.sum(value_grad.astype(jnp.float32), axis=(0, 1))
    return (
        grad_in + resid_grad,
        (gain_grad, shift_grad, q_bias_grad, v_bias_grad, out_bias_grad, qkv_grad, proj_grad),
    )


def feed_forward(resid_in, norm_gain, norm_shift, fc_in, fc_bias, fc_out, out_bias):
    normed_low = norm_rows(resid_in, norm_gain, norm_shift).astype(jnp.bfloat16)
    pre_act = (
        jnp.einsum("isd,df->isf", normed_low, fc_in, preferred_element_type=jnp.float32) + fc_bias
    )
    act_low = smooth_gate(pre_act).astype(jnp.bfloat16)
    branch = (
        jnp.einsum("isf,fd->isd", act_low, fc_out, preferred_element_type=jnp.float32) + out_bias
    )
    return (resid_in + branch, (normed_low, pre_act, act_low))


def feed_backward(grad_in, resid_in, norm_gain, norm_shift, fc_in, fc_out, kept_state):
    normed_low, pre_act, act_low = kept_state
    grad_low = grad_in.astype(jnp.bfloat16)
    fc_out_grad = pair_product(
        act_low.reshape(-1, act_low.shape[-1]), grad_low.reshape(-1, grad_low.shape[-1])
    )
    out_bias_grad = jnp.sum(grad_low.astype(jnp.float32), axis=(0, 1))
    act_grad = jnp.einsum("isd,fd->isf", grad_low, fc_out, preferred_element_type=jnp.float32)
    pre_grad = smooth_back(pre_act, act_grad).astype(jnp.bfloat16)
    fc_bias_grad = jnp.sum(pre_grad.astype(jnp.float32), axis=(0, 1))
    fc_in_grad = pair_product(
        normed_low.reshape(-1, normed_low.shape[-1]), pre_grad.reshape(-1, pre_grad.shape[-1])
    )
    normed_grad = jnp.einsum("isf,df->isd", pre_grad, fc_in, preferred_element_type=jnp.float32)
    resid_grad, gain_grad, shift_grad = norm_back(resid_in, norm_gain, norm_shift, normed_grad)
    return (
        grad_in + resid_grad,
        (gain_grad, shift_grad, fc_in_grad, fc_bias_grad, fc_out_grad, out_bias_grad),
    )


def expert_forward(arrived, expert_set):
    in_full, in_bias, out_full, out_bias = expert_set
    local_experts = in_full.shape[0]
    slot_count = arrived.shape[1]
    model_width = arrived.shape[2]
    grouped_rows = arrived.reshape(-1, local_experts, slot_count, model_width)
    hidden = jnp.einsum("nucd,udf->nucf", grouped_rows, in_full, preferred_element_type=jnp.float32)
    hidden = hidden + in_bias.astype(jnp.float32)[None, :, None, :]
    act_low = smooth_gate(hidden).astype(jnp.bfloat16)
    result = jnp.einsum("nucf,ufd->nucd", act_low, out_full, preferred_element_type=jnp.float32)
    result = result + out_bias.astype(jnp.float32)[None, :, None, :]
    return (
        result.astype(jnp.bfloat16).reshape(arrived.shape),
        hidden.reshape(arrived.shape[0], slot_count, hidden.shape[-1]),
        arrived,
    )


def per_device(
    patches,
    dense_gains,
    dense_shifts,
    dense_qkv,
    dense_proj,
    dense_fc_in,
    dense_fc_bias,
    dense_fc_out,
    moe_gains,
    moe_shifts,
    moe_qkv,
    moe_proj,
    router,
    expert_in,
    expert_in_bias,
    expert_out,
    expert_out_bias,
    routes,
    slot_pos,
    image_counts,
    cotangent,
):
    images, length, model_width = patches.shape
    row_count = images * length
    small_rows = jnp.concatenate(
        [
            dense_gains.T,
            dense_shifts.T,
            moe_gains.T,
            moe_shifts.T,
            router,
            dense_fc_bias.reshape(dense_gains.shape[1], -1),
        ],
        axis=1,
    )
    small_cols = small_rows.shape[1]
    small_rows = jnp.pad(small_rows, ((0, 0), (0, 256 - small_cols)))
    first_rows, mark = shared_gather(jnp.concatenate([dense_qkv, small_rows], axis=1), None)
    dense_qkv_full = first_rows[:, : dense_qkv.shape[1]]
    small_full = first_rows[:, dense_qkv.shape[1] :]
    dense_proj_full, mark = shared_gather(dense_proj, mark)
    fc_in_full, mark = shared_gather(dense_fc_in, mark)
    fc_out_full, mark = shared_gather(dense_fc_out, mark)
    moe_qkv_full, mark = shared_gather(moe_qkv, mark)
    moe_proj_full, mark = shared_gather(moe_proj, mark)
    experts_all = router.shape[1]
    small_turned = small_full[:, :15].astype(jnp.float32).T
    router_full = small_full[:, 15 : 15 + experts_all]
    fc_bias_full = small_full[:, 15 + experts_all : small_cols].reshape(-1)
    dense_full = (
        small_turned[0:2],
        small_turned[2:8],
        dense_qkv_full,
        dense_proj_full,
        fc_in_full,
        fc_bias_full,
        fc_out_full,
    )
    moe_full = (
        small_turned[8:10],
        small_turned[10:15],
        moe_qkv_full,
        moe_proj_full,
        router_full,
    )
    later_in, later_out, _ = lax.optimization_barrier((expert_in[0], expert_out[0], mark))
    expert_bias = jnp.concatenate([expert_in_bias[0], expert_out_bias[0]])
    expert_bias = in_order(
        [expert_bias[None]]
        + [trade(expert_bias, "fsdp", mask)[None] for mask in range(1, lax.axis_size("fsdp"))],
        lax.axis_index("fsdp"),
    )
    hidden_part = expert_in_bias.shape[1]
    expert_full = (
        plane_gather(later_in).reshape(1, -1, expert_in.shape[2]),
        expert_bias[:, :hidden_part].reshape(1, -1),
        plane_gather(later_out).reshape(1, -1, expert_out.shape[2]),
        expert_bias[:, hidden_part:].reshape(1, -1),
    )
    dense_gain = dense_full[0].astype(jnp.float32)
    dense_shift = dense_full[1].astype(jnp.float32)
    moe_gain = moe_full[0].astype(jnp.float32)
    moe_shift = moe_full[1].astype(jnp.float32)
    resid_zero = patches.astype(jnp.float32)
    resid_one, attend_dense = attend_forward(
        resid_zero,
        dense_gain[0],
        dense_shift[0],
        dense_shift[2],
        dense_shift[3],
        dense_shift[4],
        dense_full[2],
        dense_full[3],
    )
    resid_two, feed_state = feed_forward(
        resid_one,
        dense_gain[1],
        dense_shift[1],
        dense_full[4],
        dense_full[5].astype(jnp.float32),
        dense_full[6],
        dense_shift[5],
    )
    resid_three, attend_moe = attend_forward(
        resid_two,
        moe_gain[0],
        moe_shift[0],
        moe_shift[2],
        moe_shift[3],
        moe_shift[4],
        moe_full[2],
        moe_full[3],
    )
    normed_low = (
        norm_rows(resid_three, moe_gain[1], moe_shift[1])
        .reshape(row_count, model_width)
        .astype(jnp.bfloat16)
    )
    logits = jnp.dot(normed_low, moe_full[4], preferred_element_type=jnp.float32)
    route_rows = routes.reshape(row_count, 2)
    slot_rows = slot_pos.reshape(row_count, 2)
    local_experts = expert_in.shape[0]
    all_experts = local_experts * lax.axis_size("expert")
    lowest = (images + 1) // 2
    capacity = 5 * (images + lowest) * length // (4 * all_experts) + 2
    target = route_rows * capacity + slot_rows
    slot_table = (
        (target[:, :, None] == jnp.arange(all_experts * capacity, dtype=jnp.int32)[None, None, :])
        & (slot_rows[:, :, None] >= 0)
    ).astype(jnp.bfloat16)
    outgoing = jnp.einsum("tkc,td->cd", slot_table, normed_low, preferred_element_type=jnp.float32)
    outgoing = outgoing.astype(jnp.bfloat16).reshape(all_experts, capacity, model_width)
    returned, hidden, arrived = expert_forward(
        lax.all_to_all(outgoing, "expert", split_axis=0, concat_axis=0, tiled=True),
        expert_set=expert_full,
    )
    homecoming = lax.all_to_all(returned, "expert", split_axis=0, concat_axis=0, tiled=True)
    fetched = jnp.einsum(
        "tkc,cd->tkd",
        slot_table,
        homecoming.reshape(-1, model_width),
        preferred_element_type=jnp.float32,
    )
    picked = pick_gates(logits, route_rows)
    moe_branch = jnp.sum(picked[:, :, None] * fetched, axis=1)
    resid_four = resid_three + moe_branch.reshape(images, length, model_width)
    live_mask = (jnp.arange(images) < image_counts[0]).astype(jnp.float32)[:, None, None]
    output_tokens = (resid_four * live_mask).astype(jnp.bfloat16)
    moe_gain = moe_full[0].astype(jnp.float32)
    moe_shift = moe_full[1].astype(jnp.float32)
    in_full, in_bias, out_full, out_bias = expert_full
    grad_four = cotangent.astype(jnp.float32) * live_mask
    grad_rows = grad_four.reshape(row_count, model_width)
    gate_grad = jnp.sum(grad_rows[:, None, :] * fetched, axis=-1)
    _, gate_pull = jax.vjp(partial(pick_gates, route_rows=route_rows), logits)
    logit_grad = gate_pull(gate_grad)[0]
    router_grad = jnp.einsum(
        "td,te->de", normed_low.astype(jnp.float32), logit_grad, precision=highest
    )
    normed_grad = jnp.einsum(
        "te,de->td", logit_grad, moe_full[4].astype(jnp.float32), precision=highest
    )
    weighted = (picked[:, :, None] * grad_rows[:, None, :]).astype(jnp.bfloat16)
    returned_grad = jnp.einsum(
        "tkc,tkd->cd", slot_table, weighted, preferred_element_type=jnp.float32
    )
    returned_grad = returned_grad.astype(jnp.bfloat16).reshape(all_experts, capacity, model_width)
    arriving = lax.all_to_all(returned_grad, "expert", split_axis=0, concat_axis=0, tiled=True)
    grouped_grad = arriving.reshape(-1, local_experts, capacity, model_width)
    hidden_four = hidden.reshape(-1, local_experts, capacity, hidden.shape[-1])
    act_low = smooth_gate(hidden_four).astype(jnp.bfloat16)
    out_weight_grad = jnp.einsum(
        "nucf,nucd->ufd", act_low, grouped_grad, preferred_element_type=jnp.float32
    )
    out_bias_grad = jnp.sum(grouped_grad.astype(jnp.float32), axis=(0, 2))
    act_grad = jnp.einsum(
        "nucd,ufd->nucf", grouped_grad, out_full, preferred_element_type=jnp.float32
    )
    hidden_grad = smooth_back(hidden_four, act_grad).astype(jnp.bfloat16)
    in_bias_grad = jnp.sum(hidden_grad.astype(jnp.float32), axis=(0, 2))
    arrived_four = arrived.reshape(-1, local_experts, capacity, model_width)
    in_weight_grad = jnp.einsum(
        "nucd,nucf->udf", arrived_four, hidden_grad, preferred_element_type=jnp.float32
    )
    arrived_grad = jnp.einsum(
        "nucf,udf->nucd", hidden_grad, in_full, preferred_element_type=jnp.float32
    )
    arrived_grad = arrived_grad.astype(jnp.bfloat16).reshape(arrived.shape)
    dispatched_grad = lax.all_to_all(
        arrived_grad, "expert", split_axis=0, concat_axis=0, tiled=True
    )
    normed_grad = normed_grad + jnp.einsum(
        "tkc,cd->td",
        slot_table,
        dispatched_grad.reshape(-1, model_width),
        preferred_element_type=jnp.float32,
    )
    planes = lax.axis_size("fsdp")
    bias_grads = jnp.concatenate(
        [in_bias_grad.reshape(planes, -1), out_bias_grad.reshape(planes, -1)], axis=1
    )
    bias_sum = jnp.sum(
        jnp.concatenate(
            [
                trade(
                    lax.dynamic_index_in_dim(bias_grads, lax.axis_index("fsdp") ^ mask, 0),
                    "fsdp",
                    mask,
                )
                for mask in range(planes)
            ]
        ),
        axis=0,
    )
    expert_grads = (
        plane_sum(in_weight_grad.astype(jnp.bfloat16).reshape((planes,) + expert_in.shape[1:]))[
            None
        ],
        bias_sum[None, :hidden_part],
        plane_sum(out_weight_grad.astype(jnp.bfloat16).reshape((planes,) + expert_out.shape[1:]))[
            None
        ],
        bias_sum[None, hidden_part:],
    )
    resid_grad, moe_gain_last, moe_shift_last = norm_back(
        resid_three, moe_gain[1], moe_shift[1], normed_grad.reshape(images, length, model_width)
    )
    grad_three = grad_four + resid_grad
    grad_two, moe_attend = attend_backward(
        grad_three, resid_two, moe_gain[0], moe_shift[0], moe_full[2], moe_full[3], attend_moe
    )
    moe_vectors = jnp.stack(
        [
            moe_attend[0],
            moe_gain_last,
            moe_attend[1],
            moe_shift_last,
            moe_attend[2],
            moe_attend[3],
            moe_attend[4],
        ]
    )
    moe_grads = (shared_sum(moe_attend[5]), shared_sum(moe_attend[6]))
    grad_one, feed_grads = feed_backward(
        grad_two, resid_one, dense_gain[1], dense_shift[1], dense_full[4], dense_full[6], feed_state
    )
    grad_zero, dense_attend = attend_backward(
        grad_one,
        resid_zero,
        dense_gain[0],
        dense_shift[0],
        dense_full[2],
        dense_full[3],
        attend_dense,
    )
    vectors = jnp.concatenate(
        [
            jnp.stack(
                [
                    dense_attend[0],
                    feed_grads[0],
                    dense_attend[1],
                    feed_grads[1],
                    dense_attend[2],
                    dense_attend[3],
                    dense_attend[4],
                    feed_grads[5],
                ]
            ),
            moe_vectors,
        ]
    ).T
    vectors = jnp.concatenate(
        [vectors, router_grad, feed_grads[3].reshape(model_width, -1)], axis=1
    )
    vectors = jnp.pad(vectors, ((0, 0), (0, 256 - small_cols)))
    qkv_width = dense_qkv.shape[1]
    last_grad = shared_sum(jnp.concatenate([dense_attend[5], half_of(vectors)], axis=1))
    half_cols = qkv_width // 2
    dense_qkv_sum = jnp.concatenate(
        [last_grad[:, :half_cols], last_grad[:, half_cols + 128 : 2 * half_cols + 128]], axis=1
    )
    small_sum = jnp.concatenate(
        [last_grad[:, half_cols : half_cols + 128], last_grad[:, 2 * half_cols + 128 :]], axis=1
    )
    small_turn = small_sum[:, :15].T
    dense_grads = (
        small_turn[0:2],
        small_turn[2:8],
        dense_qkv_sum,
        shared_sum(dense_attend[6]),
        shared_sum(feed_grads[2]),
        small_sum[:, 15 + experts_all : small_cols].reshape(-1),
        shared_sum(feed_grads[4]),
    )
    moe_grads = (
        small_turn[8:10],
        small_turn[10:15],
        moe_grads[0],
        moe_grads[1],
        small_sum[:, 15 : 15 + experts_all],
    )
    return (
        output_tokens,
        grad_zero,
        dense_grads[0],
        dense_grads[1],
        dense_grads[2],
        dense_grads[3],
        dense_grads[4],
        dense_grads[5],
        dense_grads[6],
        moe_grads[0],
        moe_grads[1],
        moe_grads[2],
        moe_grads[3],
        moe_grads[4],
        expert_grads[0],
        expert_grads[1],
        expert_grads[2],
        expert_grads[3],
    )


def solution(mesh):
    return jax.shard_map(
        per_device,
        mesh=mesh,
        in_specs=(
            P(("fsdp", "expert"), None, None),
            P(None, ("fsdp", "expert")),
            P(None, ("fsdp", "expert")),
            P(("fsdp", "expert"), None),
            P(("fsdp", "expert"), None),
            P(("fsdp", "expert"), None),
            P(("fsdp", "expert")),
            P(("fsdp", "expert"), None),
            P(None, ("fsdp", "expert")),
            P(None, ("fsdp", "expert")),
            P(("fsdp", "expert"), None),
            P(("fsdp", "expert"), None),
            P(("fsdp", "expert"), None),
            P("expert", "fsdp", None),
            P("expert", "fsdp"),
            P("expert", "fsdp", None),
            P("expert", "fsdp"),
            P(("fsdp", "expert"), None, None),
            P(("fsdp", "expert"), None, None),
            P(("fsdp", "expert")),
            P(("fsdp", "expert"), None, None),
        ),
        out_specs=(
            P(("fsdp", "expert"), None, None),
            P(("fsdp", "expert"), None, None),
            P(None, ("fsdp", "expert")),
            P(None, ("fsdp", "expert")),
            P(("fsdp", "expert"), None),
            P(("fsdp", "expert"), None),
            P(("fsdp", "expert"), None),
            P(("fsdp", "expert")),
            P(("fsdp", "expert"), None),
            P(None, ("fsdp", "expert")),
            P(None, ("fsdp", "expert")),
            P(("fsdp", "expert"), None),
            P(("fsdp", "expert"), None),
            P(("fsdp", "expert"), None),
            P("expert", "fsdp", None),
            P("expert", "fsdp"),
            P("expert", "fsdp", None),
            P("expert", "fsdp"),
        ),
        check_vma=False,
    )
```

```python
from functools import partial

import jax
import jax.numpy as jnp
from jax import lax
from jax.experimental import pallas as pl
from jax.experimental.pallas import tpu as pltpu
from jax.sharding import PartitionSpec as P

TILE = 256
LOW = jnp.bfloat16
FULL = jnp.float32
eps_norm = 1e-06


def fit(count, step):
    return -(-count // step) * step


def whole(shape):
    return pl.BlockSpec(shape, lambda *at: (0,) * len(shape))


def shape_of(rows, cols, kind):
    return jax.ShapeDtypeStruct((rows, cols), kind)


def run_kernel(kernel, outs, arrays, micros, scalars=(), scratch=(), far=(), grid=None, in_blocks=None, out_blocks=None, ahead=False):
    nbytes = sum(a.size * a.dtype.itemsize for a in list(arrays) + list(far))
    nbytes += sum(o.size * o.dtype.itemsize for o in outs)
    if grid is None:
        in_blocks = [pl.BlockSpec(memory_space=pltpu.VMEM)] * len(arrays)
        out_blocks = [pl.BlockSpec(memory_space=pltpu.VMEM)] * len(outs)
    in_specs = [pl.BlockSpec(memory_space=pltpu.SMEM)] * len(scalars)
    in_specs += list(in_blocks) + [pl.BlockSpec(memory_space=pl.ANY)] * len(far)
    if ahead:
        more = {
            "grid_spec": pltpu.PrefetchScalarGridSpec(
                num_scalar_prefetch=len(scalars),
                grid=grid,
                in_specs=in_specs[len(scalars) :],
                out_specs=list(out_blocks),
                scratch_shapes=list(scratch),
            )
        }
    else:
        more = {
            "in_specs": in_specs,
            "out_specs": list(out_blocks),
            "scratch_shapes": list(scratch),
        }
        if grid is not None:
            more["grid"] = grid
    return pl.pallas_call(
        kernel,
        out_shape=list(outs),
        compiler_params=pltpu.CompilerParams(vmem_limit_bytes=56 * 1024 * 1024),
        cost_estimate=pl.CostEstimate(
            flops=int(micros * 1.15e9), bytes_accessed=nbytes, transcendentals=0
        ),
        **more,
    )(*scalars, *arrays, *far)


def mul(left, right):
    return jnp.dot(left, right, preferred_element_type=FULL)


def mul_turned(left, right):
    return lax.dot_general(left, right, (((1,), (1,)), ((), ())), preferred_element_type=FULL)


def turned_mul(left, right):
    return lax.dot_general(left, right, (((0,), (0,)), ((), ())), preferred_element_type=FULL)


def span(at, size):
    if isinstance(at, int):
        return slice(at * size, (at + 1) * size)
    return pl.ds(pl.multiple_of(at * size, size), size)


def norm_parts(values):
    center = values - jnp.mean(values, axis=-1, keepdims=True)
    spread = jnp.mean(center * center, axis=-1, keepdims=True)
    return center, lax.rsqrt(spread + eps_norm)


def norm_low(values, gain, shift):
    center, scale = norm_parts(values)
    return (center * scale * gain + shift).astype(LOW)


def norm_back(values, gain, upstream):
    center, scale = norm_parts(values)
    unit = center * scale
    inner = upstream * gain
    grad = scale * (
        inner
        - jnp.mean(inner, axis=-1, keepdims=True)
        - unit * jnp.mean(inner * unit, axis=-1, keepdims=True)
    )
    return (
        grad,
        jnp.sum(upstream * unit, axis=0, keepdims=True),
        jnp.sum(upstream, axis=0, keepdims=True),
    )


def gelu_parts(values):
    rate = 0.7978845608028654
    square = values * values
    bend = jnp.tanh(values * (rate + (rate * 0.044715) * square))
    half = 0.5 + 0.5 * bend
    slope = half + (values * (1.0 - bend * bend)) * (0.5 * rate + (1.5 * rate * 0.044715) * square)
    return (values * half).astype(LOW), slope.astype(LOW)


def split_low(values):
    high = values.astype(LOW)
    return high, (values - high.astype(FULL)).astype(LOW)


def head_masks():
    lane = lax.broadcasted_iota(jnp.int32, (1, 128), 1)
    first = (lane < 64).astype(FULL)
    return first, 1.0 - first


def near_copies(place_ref, own_ref, other_ref, target, sems):
    plane, side = place_ref[0], place_ref[1]
    count = sems.shape[0] // 2
    half_cols = own_ref.shape[1]
    lines = own_ref.shape[0] // count
    copies = []
    for core, source in enumerate((own_ref, other_ref)):
        cols = pl.ds(pl.multiple_of((side if core == 0 else 1 - side) * half_cols, 128), half_cols)
        for mask in range(count):
            start = pl.multiple_of((plane ^ mask) * lines, lines)
            copies.append(
                pltpu.make_async_copy(
                    source.at[pl.ds(mask * lines, lines), :],
                    target.at[pl.ds(start, lines), cols],
                    sems.at[core * count + mask],
                )
            )
    return copies


def pack_copies(pack_ref, target, sems):
    groups, cores, lines, wide = pack_ref.shape
    half_cols = target.shape[1] // cores
    return [
        pltpu.make_async_copy(
            pack_ref.at[group, core, :, wide - half_cols : wide],
            target.at[span(group, lines), span(core, half_cols)],
            sems.at[group * cores + core],
        )
        for group in range(groups)
        for core in range(cores)
    ]


def score_parts(query, key, mask, keep):
    scores = mul_turned(query * (0.125 * mask).astype(LOW), key)
    scores = jnp.where(keep, scores, -1e30)
    raised = jnp.exp(scores - jnp.max(scores, axis=-1, keepdims=True))
    return raised * (1.0 / jnp.sum(raised, axis=-1, keepdims=True))


def attend_forward_kernel(length, images, lines_of, own, experts, *refs):
    if own:
        (
            place_ref, x_ref, near_ref, other_ref,
            an_ref, qkv_ref, o_ref, out_ref, vec_ref, wide_ref, router_ref, w_ref, sems,
        ) = refs
        copies = near_copies(place_ref, near_ref, other_ref, w_ref, sems)
    else:
        place_ref, x_ref, vec_ref, pack_ref, an_ref, qkv_ref, o_ref, out_ref, w_ref, sems = refs
        copies = pack_copies(pack_ref, w_ref, sems)
    gain, shift, q_line, v_line, o_line = lines_of
    for copy in copies:
        copy.start()
    rows, width = x_ref.shape
    block = rows // images
    pairs = width // 128
    for copy in copies:
        copy.wait()
    if own:
        small = w_ref[:, 4 * width : 4 * width + 128]
        turned = small.astype(FULL).T
        vec_ref[...] = turned[0:32, :]
        spot = lax.broadcasted_iota(jnp.int32, (128, 128), 0) - lax.broadcasted_iota(
            jnp.int32, (128, 128), 1
        )
        lane = lax.broadcasted_iota(jnp.int32, (128, 128), 1)
        pick = jnp.where((spot == 15) & (lane < experts), 1.0, 0.0).astype(LOW)
        router_ref[...] = mul(small, pick).astype(LOW)
        depth = wide_ref.shape[1] // width
        near = lax.broadcasted_iota(jnp.int32, (128, 128 * depth), 0)
        place = lax.broadcasted_iota(jnp.int32, (128, 128 * depth), 1)
        spread = jnp.where(place // depth == near, 1.0, 0.0).astype(LOW)
        line = lax.broadcasted_iota(jnp.int32, (128, 128 * depth), 0)
        for at in range(width // 128):
            many = mul(turned[:, span(at, 128)].astype(LOW), spread)
            keep_line = line == place % depth + 15 + experts
            wide_ref[:, span(at, 128 * depth)] = jnp.sum(
                jnp.where(keep_line, many, 0.0), axis=0, keepdims=True
            )
    an_ref[...] = norm_low(x_ref[...], vec_ref[gain : gain + 1, :], vec_ref[shift : shift + 1, :])
    for at in range(3 * width // TILE):
        part = mul(an_ref[...], w_ref[:, span(at, TILE)])
        here = (at * TILE) % width
        if at * TILE < width:
            part = part + vec_ref[q_line : q_line + 1, here : here + TILE]
        elif at * TILE >= 2 * width:
            part = part + vec_ref[v_line : v_line + 1, here : here + TILE]
        qkv_ref[:, span(at, TILE)] = part.astype(LOW)

    first, second = head_masks()
    keep = lax.broadcasted_iota(jnp.int32, (1, block), 1) < length
    for image in range(images):
        for pair in range(pairs):
            lines = span(image, block)
            query = qkv_ref[lines, span(pair, 128)]
            key = qkv_ref[lines, span(pair + pairs, 128)]
            value = qkv_ref[lines, span(pair + 2 * pairs, 128)]
            mixed = [
                mul(score_parts(query, key, mask, keep).astype(LOW), value)
                for mask in (first, second)
            ]
            o_ref[lines, span(pair, 128)] = (mixed[0] * first + mixed[1] * second).astype(LOW)

    for at in range(width // TILE):
        cols = span(at, TILE)
        weight = w_ref[:, 3 * width + at * TILE : 3 * width + (at + 1) * TILE]
        out_ref[:, cols] = x_ref[:, cols] + (
            mul(o_ref[...], weight) + vec_ref[o_line : o_line + 1, cols]
        )


def weight_scratch(width, pieces, planes):
    if len(pieces) == 2:
        cols, count = 2 * pieces[0].shape[1], 2 * planes
    else:
        cols, count = 4 * width, pieces[0].shape[0] * pieces[0].shape[1]
    return [pltpu.VMEM((width, cols), LOW), pltpu.SemaphoreType.DMA((count,))]


def attend_forward(place, x, vec, pieces, planes, lines_of, length, images, experts, inner):
    rows, width = x.shape
    outs = [
        shape_of(rows, width, LOW),
        shape_of(rows, 3 * width, LOW),
        shape_of(rows, width, LOW),
        shape_of(rows, width, FULL),
    ]
    own = vec is None
    if own:
        outs += [shape_of(32, width, FULL), shape_of(1, inner, FULL), shape_of(width, 128, LOW)]
    return run_kernel(
        partial(attend_forward_kernel, length, images, lines_of, own, experts),
        outs,
        [x] if own else [x, vec],
        11,
        scalars=[place],
        far=pieces,
        scratch=weight_scratch(width, pieces, planes),
    )


def attend_backward_kernel(length, images, lines_of, own, experts, place_ref, up_ref, x_ref, vec_ref, qkv_ref, *refs):
    gain = lines_of[0]
    if own:
        (
            feed_ref, moe_ref, gate_ref, wide_ref, router_ref, near_ref, other_ref,
            din_ref, mine_ref, away_ref, low_mine_ref, low_away_ref, small_ref,
            dol_ref, mix_ref, grad_ref, sums_ref, w_ref, sems,
        ) = refs
        copies = near_copies(place_ref, near_ref, other_ref, w_ref, sems)
    else:
        (
            pack_ref, din_ref, mine_ref, away_ref, low_mine_ref, low_away_ref, sums_ref,
            dol_ref, mix_ref, grad_ref, w_ref, sems,
        ) = refs
        copies = pack_copies(pack_ref, w_ref, sems)
    for copy in copies:
        copy.start()
    rows, width = x_ref.shape
    block = rows // images
    pairs = width // 128
    side = place_ref[1]
    dol_ref[...] = up_ref[...].astype(LOW)
    for copy in copies:
        copy.wait()
    for at in range(width // TILE):
        cols = span(at, TILE)
        mix_ref[:, cols] = mul_turned(dol_ref[...], w_ref[cols, 3 * width : 4 * width]).astype(LOW)

    first, second = head_masks()
    keep = lax.broadcasted_iota(jnp.int32, (block, 1), 0) < length
    for image in range(images):
        for pair in range(pairs):
            lines = span(image, block)
            query = qkv_ref[lines, span(pair, 128)]
            key = qkv_ref[lines, span(pair + pairs, 128)]
            value = qkv_ref[lines, span(pair + 2 * pairs, 128)]
            mix = mix_ref[lines, span(pair, 128)]
            grads = []
            for mask in (first, second):
                scores = mul_turned(key * (0.125 * mask).astype(LOW), query)
                scores = jnp.where(keep, scores, -1e30)
                raised = jnp.exp(scores - jnp.max(scores, axis=0, keepdims=True))
                prob = raised * (1.0 / jnp.sum(raised, axis=0, keepdims=True))
                slope = mul_turned(value * mask.astype(LOW), mix)
                inner = jnp.sum(slope * prob, axis=0, keepdims=True)
                change = (prob * (slope - inner)).astype(LOW)
                grads.append(
                    (turned_mul(change, key), mul(change, query), mul(prob.astype(LOW), mix))
                )
            for part, rate in ((0, 0.125), (1, 0.125), (2, 1.0)):
                both = grads[0][part] * (rate * first) + grads[1][part] * (rate * second)
                grad_ref[lines, span(pair + part * pairs, 128)] = both.astype(LOW)

    for at in range(width // TILE):
        cols = span(at, TILE)
        din_ref[:, cols] = mul_turned(grad_ref[...], w_ref[cols, 0 : 3 * width])

    grad, gain_sum, shift_sum = norm_back(x_ref[...], vec_ref[gain : gain + 1, :], din_ref[...])
    din_ref[...] = up_ref[...] + grad
    sums_ref[0:1, :] = gain_sum
    sums_ref[1:2, :] = shift_sum
    sums_ref[2:3, :] = jnp.sum(grad_ref[:, 0:width].astype(FULL), axis=0, keepdims=True)
    sums_ref[3:4, :] = jnp.sum(
        grad_ref[:, 2 * width : 3 * width].astype(FULL), axis=0, keepdims=True
    )
    sums_ref[4:5, :] = jnp.sum(dol_ref[...].astype(FULL), axis=0, keepdims=True)
    sums_ref[5:8, :] = jnp.zeros((3, width), FULL)
    mine_ref[...] = grad_ref[:, span(side, 3 * width // 2)]
    away_ref[...] = grad_ref[:, span(1 - side, 3 * width // 2)]
    low_mine_ref[...] = dol_ref[:, span(side, width // 2)]
    low_away_ref[...] = dol_ref[:, span(1 - side, width // 2)]
    if not own:
        return
    depth = wide_ref.shape[1] // width
    line = lax.broadcasted_iota(jnp.int32, (8, 128 * depth), 0)
    place = lax.broadcasted_iota(jnp.int32, (8, 128 * depth), 1)
    near = lax.broadcasted_iota(jnp.int32, (128 * depth, 128), 1)
    spot = lax.broadcasted_iota(jnp.int32, (128 * depth, 128), 0)
    collect = jnp.where(spot // depth == near, 1.0, 0.0).astype(LOW)
    pieces = []
    for at in range(width // 128):
        many = jnp.where(place % depth == line, wide_ref[:, span(at, 128 * depth)], 0.0)
        high, rest = split_low(many)
        pieces.append(mul(high, collect) + mul(rest, collect))
    wide_rows = jnp.concatenate(pieces, axis=1)
    order = (
        (sums_ref, 0), (feed_ref, 0), (sums_ref, 1), (feed_ref, 1), (sums_ref, 2), (sums_ref, 3),
        (sums_ref, 4), (feed_ref, 2), (moe_ref, 0), (gate_ref, 0), (moe_ref, 1), (gate_ref, 1),
        (moe_ref, 2), (moe_ref, 3), (moe_ref, 4),
    )
    row = lax.broadcasted_iota(jnp.int32, (128, 1), 0)
    total = jnp.zeros((128, width), FULL)
    for at, (source, spot_line) in enumerate(order):
        total = jnp.where(row == at, source[spot_line : spot_line + 1, :], total)
    for at in range(depth):
        total = jnp.where(row == 15 + experts + at, wide_rows[at : at + 1, :], total)
    small_ref[...] = total.T + router_ref[...]


def attend_backward(place, up, x, vec, qkv, pieces, planes, gain, length, images, experts=0, more=()):
    rows, width = x.shape
    own = len(more) > 0
    return run_kernel(
        partial(attend_backward_kernel, length, images, (gain,), own, experts),
        [
            shape_of(rows, width, FULL),
            shape_of(rows, 3 * width // 2, LOW),
            shape_of(rows, 3 * width // 2, LOW),
            shape_of(rows, width // 2, LOW),
            shape_of(rows, width // 2, LOW),
            shape_of(width, 128, FULL) if own else shape_of(8, width, FULL),
        ],
        [up, x, vec, qkv] + list(more),
        19,
        scalars=[place],
        far=pieces,
        scratch=[
            pltpu.VMEM((rows, width), LOW),
            pltpu.VMEM((rows, width), LOW),
            pltpu.VMEM((rows, 3 * width), LOW),
        ]
        + ([pltpu.VMEM((8, width), FULL)] if own else [])
        + weight_scratch(width, pieces, planes),
    )


def unfold(source, target):
    groups, _, lines, wide = source.shape
    width = target.shape[1]
    fold = wide // width
    for group in range(groups):
        for at in range(fold):
            start = (group * fold + at) * lines
            target[start : start + lines, :] = source[group, 0, :, span(at, width)]


def feed_forward_kernel(
    lines_of, x_ref, vec_ref, bias_ref, in_ref, pack_ref, hn_ref, act_ref, slope_ref, out_ref, out_w_ref
):
    gain, shift, last = lines_of
    step = pl.program_id(0)

    @pl.when(step == 0)
    def _():
        hn_ref[...] = norm_low(
            x_ref[...], vec_ref[gain : gain + 1, :], vec_ref[shift : shift + 1, :]
        )
        out_ref[...] = x_ref[...] + vec_ref[last : last + 1, :]

    unfold(pack_ref, out_w_ref)
    for at in range(act_ref.shape[1] // TILE):
        cols = span(at, TILE)
        weight = in_ref[:, 0, :, cols].reshape(x_ref.shape[1], TILE)
        act, slope = gelu_parts(mul(hn_ref[...], weight) + bias_ref[:, cols])
        act_ref[:, cols] = act
        slope_ref[:, cols] = slope
    for at in range(out_ref.shape[1] // TILE):
        cols = span(at, TILE)
        out_ref[:, cols] += mul(act_ref[...], out_w_ref[:, cols])


def pack_blocks(pack, part, inner):
    groups, _, lines, _ = pack.shape
    return [
        pl.BlockSpec((groups, 1, lines, part), lambda at: (0, 0, 0, at)),
        pl.BlockSpec((part * groups // inner, 1, lines, inner), lambda at: (at, 1, 0, 0)),
    ]


def feed_forward(x, vec, bias, pack, lines_of):
    rows, width = x.shape
    inner = bias.shape[1]
    part = 768
    return run_kernel(
        partial(feed_forward_kernel, lines_of),
        [
            shape_of(rows, width, LOW),
            shape_of(rows, inner, LOW),
            shape_of(rows, inner, LOW),
            shape_of(rows, width, FULL),
        ],
        [x, vec, bias, pack, pack],
        11,
        scratch=[pltpu.VMEM((part, width), LOW)],
        grid=(inner // part,),
        in_blocks=[
            whole((rows, width)),
            whole(vec.shape),
            pl.BlockSpec((1, part), lambda at: (0, at)),
        ]
        + pack_blocks(pack, part, inner),
        out_blocks=[
            whole((rows, width)),
            pl.BlockSpec((rows, part), lambda at: (0, at)),
            pl.BlockSpec((rows, part), lambda at: (0, at)),
            whole((rows, width)),
        ],
    )


def feed_backward_kernel(
    gain, place_ref, up_ref, x_ref, vec_ref, slope_ref, in_ref, pack_ref,
    down_ref, mine_ref, away_ref, low_mine_ref, low_away_ref, sums_ref, bias_ref,
    dml_ref, du_ref, out_w_ref,
):
    step = pl.program_id(0)
    last = pl.num_programs(0) - 1
    width = x_ref.shape[1]
    part_cols = slope_ref.shape[1]

    @pl.when(step == 0)
    def _():
        dml_ref[...] = up_ref[...].astype(LOW)
        down_ref[...] = jnp.zeros(down_ref.shape, FULL)

    unfold(pack_ref, out_w_ref)
    for at in range(part_cols // TILE):
        cols = span(at, TILE)
        part = (
            mul_turned(dml_ref[...], out_w_ref[cols, :]) * slope_ref[:, cols].astype(FULL)
        ).astype(LOW)
        du_ref[step, :, cols] = part
        bias_ref[:, cols] = jnp.sum(part.astype(FULL), axis=0, keepdims=True)
    groups = in_ref.shape[0] // 2
    for at in range(2):
        weight = in_ref[span(at, groups), 0, :, :].reshape(width // 2, part_cols)
        down_ref[:, span(at, width // 2)] += mul_turned(du_ref[step, :, :], weight)

    @pl.when(step == last)
    def _():
        side = place_ref[1]
        grad, gain_sum, shift_sum = norm_back(x_ref[...], vec_ref[gain : gain + 1, :], down_ref[...])
        down_ref[...] = up_ref[...] + grad
        sums_ref[0:1, :] = gain_sum
        sums_ref[1:2, :] = shift_sum
        sums_ref[2:3, :] = jnp.sum(dml_ref[...].astype(FULL), axis=0, keepdims=True)
        sums_ref[3:8, :] = jnp.zeros((5, width), FULL)
        half = du_ref.shape[0] // 2
        for at in range(half):
            mine_ref[:, span(at, part_cols)] = du_ref[side * half + at, :, :]
            away_ref[:, span(at, part_cols)] = du_ref[(1 - side) * half + at, :, :]
        low_mine_ref[...] = dml_ref[:, span(side, width // 2)]
        low_away_ref[...] = dml_ref[:, span(1 - side, width // 2)]


def feed_backward(place, up, x, vec, slope, pack, gain):
    rows, width = x.shape
    inner = slope.shape[1]
    part = 768
    return run_kernel(
        partial(feed_backward_kernel, gain),
        [
            shape_of(rows, width, FULL),
            shape_of(rows, inner // 2, LOW),
            shape_of(rows, inner // 2, LOW),
            shape_of(rows, width // 2, LOW),
            shape_of(rows, width // 2, LOW),
            shape_of(8, width, FULL),
            shape_of(1, inner, FULL),
        ],
        [up, x, vec, slope, pack, pack],
        13,
        scalars=[place],
        scratch=[
            pltpu.VMEM((rows, width), LOW),
            pltpu.VMEM((inner // part, rows, part), LOW),
            pltpu.VMEM((part, width), LOW),
        ],
        grid=(inner // part,),
        in_blocks=[
            whole((rows, width)),
            whole((rows, width)),
            whole(vec.shape),
            pl.BlockSpec((rows, part), lambda at: (0, at)),
        ]
        + pack_blocks(pack, part, inner),
        out_blocks=[
            whole((rows, width)),
            whole((rows, inner // 2)),
            whole((rows, inner // 2)),
            whole((rows, width // 2)),
            whole((rows, width // 2)),
            whole((8, width)),
            pl.BlockSpec((1, part), lambda at: (0, at)),
        ],
    )


def product_kernel(counts, *refs):
    out_ref = refs[-1]
    start = 0
    at_ref = 0
    for count in counts:
        size = refs[at_ref + 1].shape[1]
        total = turned_mul(refs[at_ref][...], refs[at_ref + 1][...])
        for more in range(1, count):
            total += turned_mul(refs[at_ref + 2 * more][...], refs[at_ref + 2 * more + 1][...])
        out_ref[:, start : start + size] = total.astype(LOW)
        start += size
        at_ref += 2 * count
    if at_ref < len(refs) - 1:
        extra = refs[at_ref]
        out_ref[:, start : start + extra.shape[1]] = extra[...].astype(LOW)


def products(groups, extra=None, part=256):
    counts = [len(group) for group in groups]
    arrays = [array for group in groups for pair in group for array in pair]
    blocks = []
    for group in groups:
        for left, right in group:
            blocks += [pl.BlockSpec((left.shape[0], part), lambda at: (0, at)), whole(right.shape)]
    cols = sum(group[0][1].shape[1] for group in groups)
    if extra is not None:
        arrays.append(extra)
        blocks.append(pl.BlockSpec((part, extra.shape[1]), lambda at: (at, 0)))
        cols += extra.shape[1]
    lines = groups[0][0][0].shape[1]
    return run_kernel(
        partial(product_kernel, counts),
        [shape_of(lines, cols, LOW)],
        arrays,
        7,
        grid=(lines // part,),
        in_blocks=blocks,
        out_blocks=[pl.BlockSpec((part, cols), lambda at: (at, 0))],
    )[0]


def one_hot_rows(target, slots):
    hit = lax.broadcasted_iota(jnp.int32, (slots, target.shape[1]), 0) == target
    return jnp.where(hit, 1.0, 0.0).astype(LOW)


def one_hot_cols(target, slots):
    hit = lax.broadcasted_iota(jnp.int32, (target.shape[0], slots), 1) == target
    return jnp.where(hit, 1.0, 0.0).astype(LOW)


def dispatch_kernel(
    experts, lines_of, x_ref, vec_ref, router_ref, route_ref, target_ref, up_ref,
    mn_ref, gate_ref, pick_ref, out_ref, grad_ref, spot_ref, low_ref,
):
    gain, shift = lines_of
    slots = out_ref.shape[0]
    mn_ref[...] = norm_low(x_ref[...], vec_ref[gain : gain + 1, :], vec_ref[shift : shift + 1, :])
    logits = mul(mn_ref[...], router_ref[...])
    lane = lax.broadcasted_iota(jnp.int32, logits.shape, 1)
    logits = jnp.where(lane < experts, logits, -1e30)
    raised = jnp.exp(logits - jnp.max(logits, axis=-1, keepdims=True))
    gate = raised / jnp.sum(raised, axis=-1, keepdims=True)
    gate_ref[...] = gate
    picks = [
        jnp.sum(jnp.where(lane == route_ref[:, k : k + 1], gate, 0.0), axis=-1, keepdims=True)
        for k in range(2)
    ]
    pick_ref[...] = jnp.where(lane == 0, picks[0], jnp.where(lane == 1, picks[1], 0.0))
    spots = [one_hot_rows(target_ref[k : k + 1, :], slots) for k in range(2)]
    spot_ref[0, :, :] = spots[0]
    spot_ref[1, :, :] = spots[1]
    low_ref[0, :, :] = (picks[0] * up_ref[...].astype(FULL)).astype(LOW)
    low_ref[1, :, :] = (picks[1] * up_ref[...].astype(FULL)).astype(LOW)
    for at in range(out_ref.shape[1] // TILE):
        cols = span(at, TILE)
        out_ref[:, cols] = mul(spot_ref[0, :, :] + spot_ref[1, :, :], mn_ref[:, cols]).astype(LOW)
        grad_ref[:, cols] = (
            mul(spot_ref[0, :, :], low_ref[0, :, cols]) + mul(spot_ref[1, :, :], low_ref[1, :, cols])
        ).astype(LOW)


def dispatch(x, vec, router, routes, targets, up, experts, slots, lines_of):
    rows, width = x.shape
    return run_kernel(
        partial(dispatch_kernel, experts, lines_of),
        [
            shape_of(rows, width, LOW),
            shape_of(rows, 128, FULL),
            shape_of(rows, 128, FULL),
            shape_of(slots, width, LOW),
            shape_of(slots, width, LOW),
        ],
        [x, vec, router, routes, targets, up],
        6,
        scratch=[pltpu.VMEM((2, slots, rows), LOW), pltpu.VMEM((2, rows, width), LOW)],
    )


def restore(place_ref, source, target):
    planes, lines, _ = target.shape
    for mask in range(planes):
        target[place_ref[0] ^ mask, :, :] = source[mask * lines : (mask + 1) * lines, :]


def unfold_lines(place_ref, source, target, lines):
    width = target.shape[1]
    fold = source.shape[1] // width
    many = source.shape[0] // lines
    for mask in range(many):
        group = mask ^ (place_ref[0] % many)
        for at in range(fold):
            start = pl.multiple_of((group * fold + at) * lines, lines)
            target[pl.ds(start, lines), :] = source[
                mask * lines : (mask + 1) * lines, span(at, width)
            ]


def hidden_kernel(place_ref, x_ref, bias_ref, pack_ref, act_ref, slope_ref, w_ref):
    restore(place_ref, pack_ref, w_ref)
    for at in range(act_ref.shape[1] // TILE):
        cols = span(at, TILE)
        weight = w_ref[:, :, cols].reshape(x_ref.shape[1], TILE)
        act, slope = gelu_parts(mul(x_ref[...], weight) + bias_ref[:, cols])
        act_ref[:, cols] = act
        slope_ref[:, cols] = slope


def hidden_forward(place, x, bias, weight, planes):
    rows, width = x.shape
    inner = bias.shape[1]
    part = 768
    return run_kernel(
        hidden_kernel,
        [shape_of(rows, inner, LOW), shape_of(rows, inner, LOW)],
        [x, bias, weight],
        11,
        scalars=[place],
        scratch=[pltpu.VMEM((planes, width // planes, part), LOW)],
        grid=(inner // part,),
        in_blocks=[
            whole(x.shape),
            pl.BlockSpec((1, part), lambda at: (0, at)),
            pl.BlockSpec((width, part), lambda at: (0, at)),
        ],
        out_blocks=[pl.BlockSpec((rows, part), lambda at: (0, at))] * 2,
    )


def expert_out_kernel(lines, place_ref, act_ref, bias_ref, pack_ref, out_ref, sum_ref, w_ref):
    step = pl.program_id(0)
    unfold_lines(place_ref, pack_ref, w_ref, lines)

    @pl.when(step == 0)
    def _():
        sum_ref[...] = jnp.zeros(sum_ref.shape, FULL) + bias_ref[...]

    for at in range(w_ref.shape[1] // TILE):
        cols = span(at, TILE)
        sum_ref[:, cols] += mul(act_ref[...], w_ref[:, cols])

    @pl.when(step == pl.num_programs(0) - 1)
    def _():
        out_ref[...] = sum_ref[...].astype(LOW)


def expert_out_forward(place, act, bias, weight, lines):
    rows, width = act.shape[0], weight.shape[0]
    inner = act.shape[1]
    part = 768
    many = part * width // (inner * lines)
    return run_kernel(
        partial(expert_out_kernel, lines),
        [shape_of(rows, width, LOW)],
        [act, bias, weight],
        8,
        scalars=[place],
        scratch=[pltpu.VMEM((rows, width), FULL), pltpu.VMEM((part, width), LOW)],
        grid=(inner // part,),
        in_blocks=[
            pl.BlockSpec((rows, part), lambda at, place: (0, at ^ (place[0] // many))),
            pl.BlockSpec(bias.shape, lambda at, place: (0, 0)),
            pl.BlockSpec((many * lines, inner), lambda at, place: (at, 1)),
        ],
        out_blocks=[pl.BlockSpec((rows, width), lambda at, place: (0, 0))],
        ahead=True,
    )[0]


def expert_backward_kernel(
    lines, place_ref, dy_ref, slope_ref, pack_ref, in_ref,
    dh_ref, bias_ref, last_ref, back_ref, sum_ref, out_w_ref, in_w_ref,
):
    step = pl.program_id(0)
    unfold_lines(place_ref, pack_ref, out_w_ref, lines)
    restore(place_ref, in_ref, in_w_ref)

    @pl.when(step == 0)
    def _():
        sum_ref[...] = jnp.zeros(sum_ref.shape, FULL)
        last_ref[...] = jnp.sum(dy_ref[...].astype(FULL), axis=0, keepdims=True)

    for at in range(slope_ref.shape[1] // TILE):
        cols = span(at, TILE)
        part = (
            mul_turned(dy_ref[...], out_w_ref[cols, :]) * slope_ref[:, cols].astype(FULL)
        ).astype(LOW)
        dh_ref[:, cols] = part
        bias_ref[:, cols] = jnp.sum(part.astype(FULL), axis=0, keepdims=True)
    planes, lines, part_cols = in_w_ref.shape
    for at in range(2):
        weight = in_w_ref[span(at, planes // 2), :, :].reshape(planes * lines // 2, part_cols)
        sum_ref[:, span(at, planes * lines // 2)] += mul_turned(dh_ref[...], weight)

    @pl.when(step == pl.num_programs(0) - 1)
    def _():
        back_ref[...] = sum_ref[...].astype(LOW)


def expert_backward(place, dy, slope, weight, lines):
    rows, width = dy.shape
    inner = slope.shape[1]
    part = 768
    many = part * width // (inner * lines)

    def moved(at, place):
        return (0, at ^ (place[0] // many))

    def fixed(at, place):
        return (0, 0)

    return run_kernel(
        partial(expert_backward_kernel, lines),
        [
            shape_of(rows, inner, LOW),
            shape_of(1, inner, FULL),
            shape_of(1, width, FULL),
            shape_of(rows, width, LOW),
        ],
        [dy, slope, weight, weight],
        14,
        scalars=[place],
        scratch=[
            pltpu.VMEM((rows, width), FULL),
            pltpu.VMEM((part, width), LOW),
            pltpu.VMEM((width // lines, lines, part), LOW),
        ],
        grid=(inner // part,),
        in_blocks=[
            pl.BlockSpec(dy.shape, fixed),
            pl.BlockSpec((rows, part), moved),
            pl.BlockSpec((many * lines, inner), lambda at, place: (at, 1)),
            pl.BlockSpec((width, part), moved),
        ],
        out_blocks=[
            pl.BlockSpec((rows, part), moved),
            pl.BlockSpec((1, part), moved),
            pl.BlockSpec((1, width), fixed),
            pl.BlockSpec((rows, width), fixed),
        ],
        ahead=True,
    )


def combine_kernel(
    x_ref, home_ref, gate_ref, pick_ref, route_ref, target_ref, up_ref, live_ref, mn_ref, router_ref,
    out_ref, part_ref, router_grad_ref, spot_ref, dot_ref,
):
    rows, width = x_ref.shape
    slots = home_ref.shape[0]
    for k in range(2):
        spot_ref[k, :, :] = one_hot_cols(target_ref[:, k : k + 1], slots)
    lane = lax.broadcasted_iota(jnp.int32, (rows, 128), 1)
    dot_ref[...] = jnp.zeros((rows, 128), FULL)

    @pl.loop(0, width // TILE)
    def _(at):
        cols = span(at, TILE)
        up = up_ref[:, cols].astype(FULL)
        total = x_ref[:, cols]
        for k in range(2):
            fetched = mul(spot_ref[k, :, :], home_ref[:, cols])
            total += pick_ref[:, k : k + 1] * fetched
            dot_ref[...] += jnp.where(lane == k, jnp.sum(up * fetched, axis=-1, keepdims=True), 0.0)
        out_ref[:, cols] = (total * live_ref[...]).astype(LOW)

    gate = gate_ref[...]
    spread = jnp.zeros((rows, 128), FULL)
    for k in range(2):
        spread += jnp.where(lane == route_ref[:, k : k + 1], dot_ref[:, k : k + 1], 0.0)
    logit = gate * (spread - jnp.sum(gate * spread, axis=-1, keepdims=True))
    high, rest = split_low(pltpu.roll(logit, 15, 1))
    router_grad_ref[...] = turned_mul(mn_ref[...], high) + turned_mul(mn_ref[...], rest)
    high, rest = split_low(logit)
    part_ref[...] = mul_turned(high, router_ref[...]) + mul_turned(rest, router_ref[...])


def combine(x, home, gate, pick, routes, targets, up, live, mn, router):
    rows, width = x.shape
    slots = home.shape[0]
    return run_kernel(
        combine_kernel,
        [shape_of(rows, width, LOW), shape_of(rows, width, FULL), shape_of(width, 128, FULL)],
        [x, home, gate, pick, routes, targets, up, live, mn, router],
        8,
        scratch=[pltpu.VMEM((2, rows, slots), LOW), pltpu.VMEM((rows, 128), FULL)],
    )


def return_kernel(gain, x_ref, vec_ref, part_ref, home_ref, target_ref, up_ref, out_ref, sums_ref, spot_ref):
    width = x_ref.shape[1]
    slots = home_ref.shape[0]
    spot_ref[...] = one_hot_cols(target_ref[:, 0:1], slots) + one_hot_cols(target_ref[:, 1:2], slots)
    for at in range(width // TILE):
        cols = span(at, TILE)
        out_ref[:, cols] = part_ref[:, cols] + mul(spot_ref[...], home_ref[:, cols])

    grad, gain_sum, shift_sum = norm_back(x_ref[...], vec_ref[gain : gain + 1, :], out_ref[...])
    out_ref[...] = up_ref[...].astype(FULL) + grad
    sums_ref[0:1, :] = gain_sum
    sums_ref[1:2, :] = shift_sum
    sums_ref[2:8, :] = jnp.zeros((6, width), FULL)


def return_grad(x, vec, part, home, targets, up, gain):
    rows, width = x.shape
    slots = home.shape[0]
    return run_kernel(
        partial(return_kernel, gain),
        [shape_of(rows, width, FULL), shape_of(8, width, FULL)],
        [x, vec, part, home, targets, up],
        5,
        scratch=[pltpu.VMEM((rows, slots), LOW)],
    )


def feed_products_kernel(lines, fold, hn_ref, hn_far_ref, du_ref, du_far_ref, act_ref, act_far_ref, low_ref, low_far_ref, out_ref):
    cols = du_ref.shape[1] // fold
    tall = 2 * fold * lines
    tile = hn_ref.shape[1]
    for at in range(fold):
        part = turned_mul(hn_ref[...], du_ref[:, span(at, cols)])
        part += turned_mul(hn_far_ref[...], du_far_ref[:, span(at, cols)])
        part = part.astype(LOW)
        for spot in range(tile // lines):
            start = spot * tall + at * lines
            out_ref[start : start + lines, :] = part[spot * lines : (spot + 1) * lines, :]
    for at in range(act_ref.shape[1] // tile):
        part = turned_mul(act_ref[:, span(at, tile)], low_ref[...])
        part += turned_mul(act_far_ref[:, span(at, tile)], low_far_ref[...])
        part = part.astype(LOW)
        size = fold * lines
        for spot in range(tile // size):
            start = (at * (tile // size) + spot) * tall + size
            out_ref[start : start + size, :] = part[spot * size : (spot + 1) * size, :]


def feed_products(hn, hn_far, du, du_far, act, act_far, low, low_far, blocks, fold):
    rows, width = hn.shape
    lines = width // blocks
    tall = 2 * fold * lines
    steps = 2
    left = pl.BlockSpec((rows, width // steps), lambda at: (0, at))
    wide = pl.BlockSpec((rows, fold * width // steps), lambda at: (0, at))
    return run_kernel(
        partial(feed_products_kernel, lines, fold),
        [shape_of(blocks * tall, low.shape[1], LOW)],
        [hn, hn_far, du, du_far, act, act_far, low, low_far],
        11,
        grid=(steps,),
        in_blocks=[left, left, whole(du.shape), whole(du.shape), wide, wide, whole(low.shape), whole(low.shape)],
        out_blocks=[pl.BlockSpec((blocks * tall // steps, low.shape[1]), lambda at: (at, 0))],
    )[0]


def expert_products_kernel(lines, fold, x_ref, dh_ref, act_ref, dy_ref, out_ref):
    width = dy_ref.shape[1]
    tile = x_ref.shape[1]
    for at in range(fold):
        part = turned_mul(x_ref[...], dh_ref[:, span(at, width)]).astype(LOW)
        for spot in range(tile // lines):
            start = 2 * spot * lines
            out_ref[start : start + lines, span(at, width)] = part[spot * lines : (spot + 1) * lines, :]
    for at in range(fold):
        part = turned_mul(act_ref[:, span(at, tile)], dy_ref[...]).astype(LOW)
        for spot in range(tile // lines):
            group = at * (tile // lines) + spot
            start = (2 * (group // fold) + 1) * lines
            out_ref[start : start + lines, span(group % fold, width)] = part[
                spot * lines : (spot + 1) * lines, :
            ]


def expert_products(x, dh, act, dy, planes):
    slots, width = x.shape
    fold = dh.shape[1] // width
    steps = 2
    return run_kernel(
        partial(expert_products_kernel, width // planes, fold),
        [shape_of(2 * width, fold * width, LOW)],
        [x, dh, act, dy],
        14,
        grid=(steps,),
        in_blocks=[
            pl.BlockSpec((slots, width // steps), lambda at: (0, at)),
            whole(dh.shape),
            pl.BlockSpec((slots, fold * width // steps), lambda at: (0, at)),
            whole(dy.shape),
        ],
        out_blocks=[pl.BlockSpec((2 * width // steps, fold * width), lambda at: (at, 0))],
    )[0]


tie = lax.optimization_barrier


def trade(value, axis_name, mask):
    count = lax.axis_size(axis_name)
    return lax.ppermute(value, axis_name, [(place, place ^ mask) for place in range(count)])


def in_order(pieces, place):
    level = 0
    while len(pieces) > 1:
        flip = ((place >> level) & 1) == 1
        pieces = [
            jnp.where(
                flip,
                jnp.concatenate([pieces[at + 1], pieces[at]], axis=0),
                jnp.concatenate([pieces[at], pieces[at + 1]], axis=0),
            )
            for at in range(0, len(pieces), 2)
        ]
        level += 1
    return pieces[0]


def core_side():
    return lax.axis_index("expert") % 2


def core_half(shard):
    side = core_side()
    half = shard.shape[1] // 2
    mine = lax.dynamic_slice_in_dim(shard, side * half, half, 1)
    away = lax.dynamic_slice_in_dim(shard, (1 - side) * half, half, 1)
    return in_order([mine, trade(away, "expert", 1)], side)


def layer_gather(shard):
    layers = lax.axis_size("expert") // 2
    stacked = [shard] + [trade(shard, "expert", 2 * mask) for mask in range(1, layers)]
    return in_order(stacked, lax.axis_index("expert") // 2)


def plane_near(piece):
    count = lax.axis_size("fsdp")
    masks = (1, 2) if count == 4 else range(1, count)
    return [trade(piece, "fsdp", mask) for mask in masks]


def plane_far(near):
    if lax.axis_size("fsdp") != 4:
        return []
    half = near[0].shape[0] // 2
    return [trade(near[1][:half], "fsdp", 1), trade(near[0][half:], "fsdp", 2)]


def both_cores(own, near, far):
    held = jnp.concatenate([own] + near + far, axis=0)
    return held, trade(held, "expert", 1)


def sum_first(blocks):
    count = lax.axis_size("fsdp")
    place = lax.axis_index("fsdp")
    parts = [
        lax.dynamic_index_in_dim(blocks, place ^ mask, 0, keepdims=False) for mask in range(count)
    ]
    if count != 4:
        return parts, []
    half = blocks.shape[1] // 2
    return parts[:3], [
        trade(parts[3][:half], "fsdp", 1),
        trade(parts[3][half:], "fsdp", 2),
    ]


def added(left, right):
    return (left.astype(FULL) + right.astype(FULL)).astype(LOW)


def sum_second(parts, got):
    if not got:
        return [trade(part, "fsdp", mask) for mask, part in enumerate(parts) if mask > 0]
    half = parts[1].shape[0] // 2
    send_x = jnp.concatenate([parts[1][:half], added(parts[1][half:], got[1])], axis=0)
    send_y = jnp.concatenate([added(parts[2][:half], got[0]), parts[2][half:]], axis=0)
    return [trade(send_x, "fsdp", 1), trade(send_y, "fsdp", 2)]


def sum_total(own, arrived):
    total = own.astype(FULL)
    for term in arrived:
        total = total + term.astype(FULL)
    return total


def layer_first(held):
    layer = lax.axis_index("expert") // 2
    layers = lax.axis_size("expert") // 2
    parts = [
        lax.dynamic_index_in_dim(held, layer ^ mask, 0, keepdims=False) for mask in range(layers)
    ]
    return parts[0], [trade(parts[mask], "expert", 2 * mask) for mask in range(1, layers)]


def core_last(total):
    side = core_side()
    rows = total.shape[0] // 2
    mine = lax.dynamic_slice_in_dim(total, side * rows, rows, 0)
    away = lax.dynamic_slice_in_dim(total, (1 - side) * rows, rows, 0).astype(LOW)
    came = trade(away, "expert", 1).astype(FULL)
    return jnp.where(side == 0, mine, came), jnp.where(side == 0, came, mine)


def feed_half(fc_in, fc_out):
    side = core_side()
    lines, inner = fc_in.shape
    fold = inner // fc_out.shape[1]
    blocks = [fc_out[at * lines : (at + 1) * lines] for at in range(fold)]
    folded = jnp.concatenate(blocks, axis=1)
    came = trade(jnp.where(side == 0, folded, fc_in), "expert", 1)
    width = fc_out.shape[1]
    rows_came = [came[:, at * width : (at + 1) * width] for at in range(fold)]
    stacked = [
        jnp.concatenate([group[at], group[at + 1]], axis=0)
        for group in (rows_came, blocks)
        for at in range(0, fold, 2)
    ]
    return jnp.where(
        side == 0, jnp.concatenate([fc_in, came], axis=0), jnp.concatenate(stacked, axis=1)
    )


def feed_last(total, fold):
    side = core_side()
    cols = total.shape[1]
    size = total.shape[0] // 2
    inside = total[:size].reshape(fold, 2, -1, cols)
    outside = total[size:].reshape(2, -1, cols)

    def part(core):
        return jnp.concatenate(
            [
                lax.dynamic_index_in_dim(inside, core, 1, keepdims=False).reshape(-1, cols),
                lax.dynamic_index_in_dim(outside, core, 0, keepdims=False),
            ],
            axis=0,
        )

    mine = part(side)
    came = trade(part(1 - side).astype(LOW), "expert", 1).astype(FULL)
    return jnp.where(side == 0, mine, came), jnp.where(side == 0, came, mine)


def in_blocks(half_grad):
    planes = lax.axis_size("fsdp")
    layers = lax.axis_size("expert") // 2
    return half_grad.reshape(planes, layers, -1, half_grad.shape[-1])


def per_device(
    patches,
    dense_gains,
    dense_shifts,
    dense_qkv,
    dense_proj,
    dense_fc_in,
    dense_fc_bias,
    dense_fc_out,
    moe_gains,
    moe_shifts,
    moe_qkv,
    moe_proj,
    router,
    expert_in,
    expert_in_bias,
    expert_out,
    expert_out_bias,
    routes,
    slot_pos,
    image_counts,
    cotangent,
):
    images, length, width = patches.shape
    shard_rows = dense_qkv.shape[0]
    inner = dense_fc_in.shape[1]
    local_experts = expert_in.shape[0]
    experts = local_experts * lax.axis_size("expert")
    planes = lax.axis_size("fsdp")
    plane = lax.axis_index("fsdp")
    place = jnp.stack([plane, core_side()]).astype(jnp.int32)
    block = fit(length, 16)
    rows = images * block
    lowest = (images + 1) // 2
    capacity = fit(5 * (images + lowest) * length // (4 * experts) + 2, 16)
    slots = experts * capacity

    def padded(array, fill=0):
        return jnp.pad(
            array, ((0, 0), (0, block - length), (0, 0)), constant_values=fill
        ).reshape(rows, array.shape[-1])

    def trimmed(array):
        return array.reshape(images, block, array.shape[-1])[:, :length]

    def far(array):
        return trade(array, "expert", 1)

    layers = lax.axis_size("expert") // 2
    fold = inner // width
    small_rows = jnp.concatenate(
        [
            dense_gains.T,
            dense_shifts.T,
            moe_gains.T,
            moe_shifts.T,
            router,
            dense_fc_bias.reshape(shard_rows, -1),
        ],
        axis=1,
    )
    small_cols = small_rows.shape[1]
    small_rows = jnp.pad(small_rows, ((0, 0), (0, 256 - small_cols)))
    first_half = core_half(jnp.concatenate([dense_qkv, dense_proj, small_rows], axis=1))
    moe_rows = jnp.concatenate([moe_qkv, moe_proj], axis=1)
    if (2 * shard_rows) % 16 == 0:
        later = jnp.concatenate([feed_half(dense_fc_in, dense_fc_out), core_half(moe_rows)], axis=1)
        pack = lax.all_gather(later, ("fsdp", "expert"), axis=0, tiled=True)
        pack = pack.reshape(planes * layers, 2, 2 * shard_rows, later.shape[1])
    else:
        groups = width // 48
        whole_in = lax.all_gather(dense_fc_in, ("fsdp", "expert"), axis=0, tiled=True)
        whole_out = lax.all_gather(dense_fc_out, ("fsdp", "expert"), axis=0, tiled=True)
        whole_moe = lax.all_gather(moe_rows, ("fsdp", "expert"), axis=0, tiled=True)
        folded = whole_out.reshape(groups, fold, 48, width).swapaxes(1, 2).reshape(groups, 48, inner)
        pack = jnp.concatenate(
            [
                jnp.stack([whole_in.reshape(groups, 48, inner), folded], axis=1),
                whole_moe.reshape(groups, 48, 2, 2 * width).swapaxes(1, 2),
            ],
            axis=3,
        )
    dense_own = layer_gather(first_half)
    dense_near = plane_near(dense_own)
    expert_rows = width // planes
    expert_own = jnp.concatenate(
        [expert_in[0]]
        + [expert_out[0, at * expert_rows : (at + 1) * expert_rows] for at in range(fold)],
        axis=1,
    )
    dense_pieces = both_cores(dense_own, dense_near, plane_far(dense_near))

    live_images = jnp.arange(images) < image_counts[0]
    live_rows = jnp.repeat(live_images, block).astype(FULL)[:, None]
    up = padded(jnp.where(live_images[:, None, None], cotangent, jnp.zeros_like(cotangent)))
    route_cols = padded(routes)
    target_cols = padded(jnp.where(slot_pos >= 0, routes * capacity + slot_pos, -1), -1)
    target_rows = target_cols.T

    x0 = padded(patches).astype(FULL)
    an, qkv, mixed, x1, vec, fc_bias, router_full = attend_forward(
        place, x0, None, dense_pieces, planes, (0, 2, 4, 5, 6), length, images, experts, inner
    )
    x1, expert_own = tie((x1, expert_own))
    expert_near = plane_near(expert_own)
    expert_bias = jnp.concatenate([expert_in_bias[0], expert_out_bias[0]])
    other_bias = tie([trade(expert_bias, "fsdp", mask) for mask in range(1, planes)])
    expert_bias = in_order([part[None] for part in [expert_bias] + other_bias], plane).astype(FULL)
    hidden_part = expert_in_bias.shape[1]
    in_bias = expert_bias[:, :hidden_part].reshape(1, -1)
    out_bias = expert_bias[:, hidden_part:].reshape(1, -1)

    hn, act, slope, x2 = feed_forward(x1, vec, fc_bias, pack, (1, 3, 7))
    an2, qkv2, mixed2, x3 = attend_forward(
        place, x2, vec, [pack], planes, (8, 10, 12, 13, 14), length, images, experts, inner
    )
    x3, expert_near = tie((x3, expert_near))
    expert_far = plane_far(expert_near)
    mn, gate, pick, outgoing, grad_out = dispatch(
        x3, vec, router_full, route_cols, target_rows, up, experts, slots, (9, 11)
    )

    def exchange(array):
        return lax.all_to_all(
            array.reshape(experts, capacity, width), "expert", split_axis=0, concat_axis=0, tiled=True
        ).reshape(slots, width)

    arrived = exchange(outgoing)
    dy = exchange(grad_out)
    expert_w = jnp.concatenate([expert_own] + expert_near + expert_far, axis=0)
    e_act, e_slope = hidden_forward(place, arrived, in_bias, expert_w, planes)
    home = exchange(expert_out_forward(place, e_act, out_bias, expert_w, expert_rows))
    dh, in_bias_grad, out_bias_grad, back = expert_backward(place, dy, e_slope, expert_w, expert_rows)
    back = exchange(back)
    expert_grad = expert_products(arrived, dh, e_act, dy, planes)
    expert_grad, home = tie((expert_grad, home))
    expert_sum = lax.psum_scatter(expert_grad, "fsdp", scatter_dimension=0, tiled=True)
    bias_grads = jnp.concatenate(
        [in_bias_grad.reshape(planes, -1), out_bias_grad.reshape(planes, -1)], axis=1
    )
    bias_parts = [
        lax.dynamic_index_in_dim(bias_grads, plane ^ mask, 0) for mask in range(planes)
    ]
    bias_came = tie([trade(bias_parts[mask], "fsdp", mask) for mask in range(1, planes)])
    bias_sum = sum_total(bias_parts[0], bias_came)

    output, part, router_grad = combine(
        x3, home, gate, pick, route_cols, target_cols, up, live_rows, mn, router_full
    )
    dx3, gate_sums = return_grad(x3, vec, part, back, target_cols, up, 9)
    dx2, mine2, away2, low_mine2, low_away2, moe_sums = attend_backward(
        place, dx3, x2, vec, qkv2, [pack], planes, 8, length, images
    )
    moe_grad = products(
        [
            [(an2, mine2), (far(an2), far(away2))],
            [(mixed2, low_mine2), (far(mixed2), far(low_away2))],
        ]
    )
    moe_grad, dx2 = tie((moe_grad, dx2))
    moe_parts, moe_got = sum_first(in_blocks(moe_grad))
    dx1, mine1, away1, low_mine1, low_away1, feed_sums, fc_bias_grad = feed_backward(
        place, dx2, x1, vec, slope, pack, 1
    )
    moe_got, dx1 = tie((moe_got, dx1))
    moe_came = sum_second(moe_parts, moe_got)
    if (2 * shard_rows) % 16 == 0:
        feed_grad = feed_products(
            hn, far(hn), mine1, far(away1), act, far(act), low_mine1, far(low_away1),
            planes * layers, fold,
        )
    else:
        in_part = products([[(hn, mine1), (far(hn), far(away1))]])
        out_part = products([[(act, low_mine1), (far(act), far(low_away1))]], part=768)
        in_part = in_blocks(in_part)
        in_part = in_part.reshape(in_part.shape[:3] + (fold, -1)).swapaxes(2, 3)
        in_part = in_part.reshape(planes, layers, -1, in_part.shape[-1])
        feed_grad = jnp.concatenate([in_part, in_blocks(out_part)], axis=2)
        feed_grad = feed_grad.reshape(-1, feed_grad.shape[-1])
    feed_grad, dx1 = tie((feed_grad, dx1))
    feed_parts, feed_got = sum_first(in_blocks(feed_grad))
    dx0, mine0, away0, low_mine0, low_away0, vectors = attend_backward(
        place, dx1, x0, vec, qkv, dense_pieces, planes, 0, length, images, experts,
        [feed_sums, moe_sums, gate_sums, fc_bias_grad, router_grad],
    )
    moe_came, feed_got, mine0, expert_sum = tie((moe_came, feed_got, mine0, expert_sum))
    feed_came = sum_second(feed_parts, feed_got)
    moe_mine, moe_layers = layer_first(sum_total(moe_parts[0], moe_came).astype(LOW))
    dense_grad = products(
        [
            [(an, mine0), (far(an), far(away0))],
            [(mixed, low_mine0), (far(mixed), far(low_away0))],
        ],
        vectors,
    )
    dense_parts, dense_got = sum_first(in_blocks(dense_grad))
    dense_got, feed_came, moe_layers = tie((dense_got, feed_came, moe_layers))
    feed_mine, feed_layers = layer_first(sum_total(feed_parts[0], feed_came).astype(LOW))
    moe_left, moe_right = core_last(sum_total(moe_mine, moe_layers))
    dense_came = sum_second(dense_parts, dense_got)
    feed_left, feed_right = feed_last(sum_total(feed_mine, feed_layers), fold)
    dense_mine, dense_layers = layer_first(sum_total(dense_parts[0], dense_came).astype(LOW))
    dense_left, dense_right = core_last(sum_total(dense_mine, dense_layers))
    third = 3 * width // 2

    def split(left, right):
        return (
            jnp.concatenate([left[:, :third], right[:, :third]], axis=1),
            jnp.concatenate([left[:, third : 2 * width], right[:, third : 2 * width]], axis=1),
        )

    dense_qkv_sum, dense_proj_sum = split(dense_left, dense_right)
    moe_qkv_sum, moe_proj_sum = split(moe_left, moe_right)
    small_sum = dense_left[:, 2 * width :] + dense_right[:, 2 * width :]
    feed_in_sum = jnp.concatenate(
        [
            half[at * shard_rows : (at + 1) * shard_rows]
            for half in (feed_left, feed_right)
            for at in range(fold)
        ],
        axis=1,
    )
    feed_out_sum = jnp.concatenate(
        [feed_left[fold * shard_rows :], feed_right[fold * shard_rows :]], axis=1
    )
    expert_in_sum = expert_sum[:expert_rows].astype(FULL)[None]
    expert_out_sum = jnp.concatenate(
        [expert_sum[expert_rows:, at * width : (at + 1) * width] for at in range(fold)], axis=0
    ).astype(FULL)[None]
    small_turn = small_sum[:, :15].T
    return (
        trimmed(output),
        trimmed(dx0),
        small_turn[0:2],
        small_turn[2:8],
        dense_qkv_sum,
        dense_proj_sum,
        feed_in_sum,
        small_sum[:, 15 + experts : small_cols].reshape(-1),
        feed_out_sum,
        small_turn[8:10],
        small_turn[10:15],
        moe_qkv_sum,
        moe_proj_sum,
        small_sum[:, 15 : 15 + experts],
        expert_in_sum,
        bias_sum[:, :hidden_part],
        expert_out_sum,
        bias_sum[:, hidden_part:],
    )


def solution(mesh):
    return jax.shard_map(
        per_device,
        mesh=mesh,
        in_specs=(
            P(("fsdp", "expert"), None, None),
            P(None, ("fsdp", "expert")),
            P(None, ("fsdp", "expert")),
            P(("fsdp", "expert"), None),
            P(("fsdp", "expert"), None),
            P(("fsdp", "expert"), None),
            P(("fsdp", "expert")),
            P(("fsdp", "expert"), None),
            P(None, ("fsdp", "expert")),
            P(None, ("fsdp", "expert")),
            P(("fsdp", "expert"), None),
            P(("fsdp", "expert"), None),
            P(("fsdp", "expert"), None),
            P("expert", "fsdp", None),
            P("expert", "fsdp"),
            P("expert", "fsdp", None),
            P("expert", "fsdp"),
            P(("fsdp", "expert"), None, None),
            P(("fsdp", "expert"), None, None),
            P(("fsdp", "expert")),
            P(("fsdp", "expert"), None, None),
        ),
        out_specs=(
            P(("fsdp", "expert"), None, None),
            P(("fsdp", "expert"), None, None),
            P(None, ("fsdp", "expert")),
            P(None, ("fsdp", "expert")),
            P(("fsdp", "expert"), None),
            P(("fsdp", "expert"), None),
            P(("fsdp", "expert"), None),
            P(("fsdp", "expert")),
            P(("fsdp", "expert"), None),
            P(None, ("fsdp", "expert")),
            P(None, ("fsdp", "expert")),
            P(("fsdp", "expert"), None),
            P(("fsdp", "expert"), None),
            P(("fsdp", "expert"), None),
            P("expert", "fsdp", None),
            P("expert", "fsdp"),
            P("expert", "fsdp", None),
            P("expert", "fsdp"),
        ),
        check_vma=False,
    )
```

```python
from functools import partial

import jax
import jax.numpy as jnp
from jax import lax
from jax.experimental import pallas as pl
from jax.experimental.pallas import tpu as pltpu
from jax.sharding import PartitionSpec as P

TILE = 256
LOW = jnp.bfloat16
FULL = jnp.float32
eps_norm = 1e-06


def fit(count, step):
    return -(-count // step) * step


def whole(shape):
    return pl.BlockSpec(shape, lambda *at: (0,) * len(shape))


def shape_of(rows, cols, kind):
    return jax.ShapeDtypeStruct((rows, cols), kind)


def run_kernel(kernel, outs, arrays, micros, scalars=(), scratch=(), far=(), grid=None, in_blocks=None, out_blocks=None, ahead=False):
    nbytes = sum(a.size * a.dtype.itemsize for a in list(arrays) + list(far))
    nbytes += sum(o.size * o.dtype.itemsize for o in outs)
    if grid is None:
        in_blocks = [pl.BlockSpec(memory_space=pltpu.VMEM)] * len(arrays)
        out_blocks = [pl.BlockSpec(memory_space=pltpu.VMEM)] * len(outs)
    in_specs = [pl.BlockSpec(memory_space=pltpu.SMEM)] * len(scalars)
    in_specs += list(in_blocks) + [pl.BlockSpec(memory_space=pl.ANY)] * len(far)
    if ahead:
        more = {
            "grid_spec": pltpu.PrefetchScalarGridSpec(
                num_scalar_prefetch=len(scalars),
                grid=grid,
                in_specs=in_specs[len(scalars) :],
                out_specs=list(out_blocks),
                scratch_shapes=list(scratch),
            )
        }
    else:
        more = {
            "in_specs": in_specs,
            "out_specs": list(out_blocks),
            "scratch_shapes": list(scratch),
        }
        if grid is not None:
            more["grid"] = grid
    return pl.pallas_call(
        kernel,
        out_shape=list(outs),
        compiler_params=pltpu.CompilerParams(vmem_limit_bytes=56 * 1024 * 1024),
        cost_estimate=pl.CostEstimate(
            flops=int(micros * 0.4e9), bytes_accessed=nbytes, transcendentals=0
        ),
        **more,
    )(*scalars, *arrays, *far)


def mul(left, right):
    return jnp.dot(left, right, preferred_element_type=FULL)


def mul_turned(left, right):
    return lax.dot_general(left, right, (((1,), (1,)), ((), ())), preferred_element_type=FULL)


def turned_mul(left, right):
    return lax.dot_general(left, right, (((0,), (0,)), ((), ())), preferred_element_type=FULL)


def span(at, size):
    if isinstance(at, int):
        return slice(at * size, (at + 1) * size)
    return pl.ds(pl.multiple_of(at * size, size), size)


def norm_parts(values):
    center = values - jnp.mean(values, axis=-1, keepdims=True)
    spread = jnp.mean(center * center, axis=-1, keepdims=True)
    return center, lax.rsqrt(spread + eps_norm)


def norm_low(values, gain, shift):
    center, scale = norm_parts(values)
    return (center * scale * gain + shift).astype(LOW)


def norm_back(values, gain, upstream):
    center, scale = norm_parts(values)
    unit = center * scale
    inner = upstream * gain
    grad = scale * (
        inner
        - jnp.mean(inner, axis=-1, keepdims=True)
        - unit * jnp.mean(inner * unit, axis=-1, keepdims=True)
    )
    return (
        grad,
        jnp.sum(upstream * unit, axis=0, keepdims=True),
        jnp.sum(upstream, axis=0, keepdims=True),
    )


def gelu_parts(values):
    rate = 0.7978845608028654
    square = values * values
    bend = jnp.tanh(values * (rate + (rate * 0.044715) * square))
    half = 0.5 + 0.5 * bend
    slope = half + (values * (1.0 - bend * bend)) * (0.5 * rate + (1.5 * rate * 0.044715) * square)
    return (values * half).astype(LOW), slope.astype(LOW)


def split_low(values):
    high = values.astype(LOW)
    return high, (values - high.astype(FULL)).astype(LOW)


def head_masks():
    lane = lax.broadcasted_iota(jnp.int32, (1, 128), 1)
    first = (lane < 64).astype(FULL)
    return first, 1.0 - first


def near_copies(place_ref, own_ref, other_ref, target, sems):
    plane, side = place_ref[0], place_ref[1]
    count = sems.shape[0] // 2
    half_cols = own_ref.shape[1]
    lines = own_ref.shape[0] // count
    copies = []
    for core, source in enumerate((own_ref, other_ref)):
        cols = pl.ds(pl.multiple_of((side if core == 0 else 1 - side) * half_cols, 128), half_cols)
        for mask in range(count):
            start = pl.multiple_of((plane ^ mask) * lines, lines)
            copies.append(
                pltpu.make_async_copy(
                    source.at[pl.ds(mask * lines, lines), :],
                    target.at[pl.ds(start, lines), cols],
                    sems.at[core * count + mask],
                )
            )
    return copies


def score_parts(query, key, mask, keep):
    scores = mul_turned(query * (0.125 * mask).astype(LOW), key)
    scores = jnp.where(keep, scores, -1e30)
    raised = jnp.exp(scores - jnp.max(scores, axis=-1, keepdims=True))
    return raised * (1.0 / jnp.sum(raised, axis=-1, keepdims=True))


def attend_forward_kernel(length, images, lines_of, own, experts, *refs):
    if own:
        (
            place_ref, x_ref, near_ref, other_ref,
            an_ref, qkv_ref, o_ref, out_ref, vec_ref, wide_ref, router_ref, w_ref, sems,
        ) = refs
    else:
        (
            place_ref, x_ref, vec_ref, near_ref, other_ref,
            an_ref, qkv_ref, o_ref, out_ref, w_ref, sems,
        ) = refs
    copies = near_copies(place_ref, near_ref, other_ref, w_ref, sems)
    gain, shift, q_line, v_line, o_line = lines_of
    for copy in copies:
        copy.start()
    rows, width = x_ref.shape
    block = rows // images
    pairs = width // 128
    for copy in copies:
        copy.wait()
    if own:
        small = w_ref[:, 4 * width : 4 * width + 128]
        turned = small.astype(FULL).T
        vec_ref[...] = turned[0:32, :]
        spot = lax.broadcasted_iota(jnp.int32, (128, 128), 0) - lax.broadcasted_iota(
            jnp.int32, (128, 128), 1
        )
        lane = lax.broadcasted_iota(jnp.int32, (128, 128), 1)
        pick = jnp.where((spot == 15) & (lane < experts), 1.0, 0.0).astype(LOW)
        router_ref[...] = mul(small, pick).astype(LOW)
        depth = wide_ref.shape[1] // width
        near = lax.broadcasted_iota(jnp.int32, (128, 128 * depth), 0)
        place = lax.broadcasted_iota(jnp.int32, (128, 128 * depth), 1)
        spread = jnp.where(place // depth == near, 1.0, 0.0).astype(LOW)
        line = lax.broadcasted_iota(jnp.int32, (128, 128 * depth), 0)
        for at in range(width // 128):
            many = mul(turned[:, span(at, 128)].astype(LOW), spread)
            keep_line = line == place % depth + 15 + experts
            wide_ref[:, span(at, 128 * depth)] = jnp.sum(
                jnp.where(keep_line, many, 0.0), axis=0, keepdims=True
            )
    an_ref[...] = norm_low(x_ref[...], vec_ref[gain : gain + 1, :], vec_ref[shift : shift + 1, :])
    for at in range(3 * width // TILE):
        part = mul(an_ref[...], w_ref[:, span(at, TILE)])
        here = (at * TILE) % width
        if at * TILE < width:
            part = part + vec_ref[q_line : q_line + 1, here : here + TILE]
        elif at * TILE >= 2 * width:
            part = part + vec_ref[v_line : v_line + 1, here : here + TILE]
        qkv_ref[:, span(at, TILE)] = part.astype(LOW)

    first, second = head_masks()
    keep = lax.broadcasted_iota(jnp.int32, (1, block), 1) < length
    for image in range(images):
        for pair in range(pairs):
            lines = span(image, block)
            query = qkv_ref[lines, span(pair, 128)]
            key = qkv_ref[lines, span(pair + pairs, 128)]
            value = qkv_ref[lines, span(pair + 2 * pairs, 128)]
            mixed = [
                mul(score_parts(query, key, mask, keep).astype(LOW), value)
                for mask in (first, second)
            ]
            o_ref[lines, span(pair, 128)] = (mixed[0] * first + mixed[1] * second).astype(LOW)

    for at in range(width // TILE):
        cols = span(at, TILE)
        weight = w_ref[:, 3 * width + at * TILE : 3 * width + (at + 1) * TILE]
        out_ref[:, cols] = x_ref[:, cols] + (
            mul(o_ref[...], weight) + vec_ref[o_line : o_line + 1, cols]
        )


def weight_scratch(width, pieces, planes):
    cols = 2 * pieces[0].shape[1]
    return [pltpu.VMEM((width, cols), LOW), pltpu.SemaphoreType.DMA((2 * planes,))]


def attend_forward(place, x, vec, pieces, planes, lines_of, length, images, experts, inner):
    rows, width = x.shape
    outs = [
        shape_of(rows, width, LOW),
        shape_of(rows, 3 * width, LOW),
        shape_of(rows, width, LOW),
        shape_of(rows, width, FULL),
    ]
    own = vec is None
    if own:
        outs += [shape_of(32, width, FULL), shape_of(1, inner, FULL), shape_of(width, 128, LOW)]
    return run_kernel(
        partial(attend_forward_kernel, length, images, lines_of, own, experts),
        outs,
        [x] if own else [x, vec],
        11,
        scalars=[place],
        far=pieces,
        scratch=weight_scratch(width, pieces, planes),
    )


def attend_backward_kernel(length, images, lines_of, own, experts, place_ref, up_ref, x_ref, vec_ref, qkv_ref, *refs):
    gain = lines_of[0]
    if own:
        (
            feed_ref, moe_ref, gate_ref, wide_ref, router_ref, near_ref, other_ref,
            din_ref, mine_ref, away_ref, low_mine_ref, low_away_ref, small_ref,
            dol_ref, mix_ref, grad_ref, sums_ref, w_ref, sems,
        ) = refs
    else:
        (
            near_ref, other_ref, din_ref, mine_ref, away_ref, low_mine_ref, low_away_ref, sums_ref,
            dol_ref, mix_ref, grad_ref, w_ref, sems,
        ) = refs
    copies = near_copies(place_ref, near_ref, other_ref, w_ref, sems)
    for copy in copies:
        copy.start()
    rows, width = x_ref.shape
    block = rows // images
    pairs = width // 128
    side = place_ref[1]
    dol_ref[...] = up_ref[...].astype(LOW)
    for copy in copies:
        copy.wait()
    for at in range(width // TILE):
        cols = span(at, TILE)
        mix_ref[:, cols] = mul_turned(dol_ref[...], w_ref[cols, 3 * width : 4 * width]).astype(LOW)

    first, second = head_masks()
    keep = lax.broadcasted_iota(jnp.int32, (block, 1), 0) < length
    for image in range(images):
        for pair in range(pairs):
            lines = span(image, block)
            query = qkv_ref[lines, span(pair, 128)]
            key = qkv_ref[lines, span(pair + pairs, 128)]
            value = qkv_ref[lines, span(pair + 2 * pairs, 128)]
            mix = mix_ref[lines, span(pair, 128)]
            grads = []
            for mask in (first, second):
                scores = mul_turned(key * (0.125 * mask).astype(LOW), query)
                scores = jnp.where(keep, scores, -1e30)
                raised = jnp.exp(scores - jnp.max(scores, axis=0, keepdims=True))
                prob = raised * (1.0 / jnp.sum(raised, axis=0, keepdims=True))
                slope = mul_turned(value * mask.astype(LOW), mix)
                inner = jnp.sum(slope * prob, axis=0, keepdims=True)
                change = (prob * (slope - inner)).astype(LOW)
                grads.append(
                    (turned_mul(change, key), mul(change, query), mul(prob.astype(LOW), mix))
                )
            for part, rate in ((0, 0.125), (1, 0.125), (2, 1.0)):
                both = grads[0][part] * (rate * first) + grads[1][part] * (rate * second)
                grad_ref[lines, span(pair + part * pairs, 128)] = both.astype(LOW)

    for at in range(width // TILE):
        cols = span(at, TILE)
        din_ref[:, cols] = mul_turned(grad_ref[...], w_ref[cols, 0 : 3 * width])

    grad, gain_sum, shift_sum = norm_back(x_ref[...], vec_ref[gain : gain + 1, :], din_ref[...])
    din_ref[...] = up_ref[...] + grad
    sums_ref[0:1, :] = gain_sum
    sums_ref[1:2, :] = shift_sum
    sums_ref[2:3, :] = jnp.sum(grad_ref[:, 0:width].astype(FULL), axis=0, keepdims=True)
    sums_ref[3:4, :] = jnp.sum(
        grad_ref[:, 2 * width : 3 * width].astype(FULL), axis=0, keepdims=True
    )
    sums_ref[4:5, :] = jnp.sum(dol_ref[...].astype(FULL), axis=0, keepdims=True)
    sums_ref[5:8, :] = jnp.zeros((3, width), FULL)
    mine_ref[...] = grad_ref[:, span(side, 3 * width // 2)]
    away_ref[...] = grad_ref[:, span(1 - side, 3 * width // 2)]
    low_mine_ref[...] = dol_ref[:, span(side, width // 2)]
    low_away_ref[...] = dol_ref[:, span(1 - side, width // 2)]
    if not own:
        return
    depth = wide_ref.shape[1] // width
    line = lax.broadcasted_iota(jnp.int32, (8, 128 * depth), 0)
    place = lax.broadcasted_iota(jnp.int32, (8, 128 * depth), 1)
    near = lax.broadcasted_iota(jnp.int32, (128 * depth, 128), 1)
    spot = lax.broadcasted_iota(jnp.int32, (128 * depth, 128), 0)
    collect = jnp.where(spot // depth == near, 1.0, 0.0).astype(LOW)
    pieces = []
    for at in range(width // 128):
        many = jnp.where(place % depth == line, wide_ref[:, span(at, 128 * depth)], 0.0)
        high, rest = split_low(many)
        pieces.append(mul(high, collect) + mul(rest, collect))
    wide_rows = jnp.concatenate(pieces, axis=1)
    order = (
        (sums_ref, 0), (feed_ref, 0), (sums_ref, 1), (feed_ref, 1), (sums_ref, 2), (sums_ref, 3),
        (sums_ref, 4), (feed_ref, 2), (moe_ref, 0), (gate_ref, 0), (moe_ref, 1), (gate_ref, 1),
        (moe_ref, 2), (moe_ref, 3), (moe_ref, 4),
    )
    row = lax.broadcasted_iota(jnp.int32, (128, 1), 0)
    total = jnp.zeros((128, width), FULL)
    for at, (source, spot_line) in enumerate(order):
        total = jnp.where(row == at, source[spot_line : spot_line + 1, :], total)
    for at in range(depth):
        total = jnp.where(row == 15 + experts + at, wide_rows[at : at + 1, :], total)
    small_ref[...] = total.T + router_ref[...]


def attend_backward(place, up, x, vec, qkv, pieces, planes, gain, length, images, experts=0, more=()):
    rows, width = x.shape
    own = len(more) > 0
    return run_kernel(
        partial(attend_backward_kernel, length, images, (gain,), own, experts),
        [
            shape_of(rows, width, FULL),
            shape_of(rows, 3 * width // 2, LOW),
            shape_of(rows, 3 * width // 2, LOW),
            shape_of(rows, width // 2, LOW),
            shape_of(rows, width // 2, LOW),
            shape_of(width, 128, FULL) if own else shape_of(8, width, FULL),
        ],
        [up, x, vec, qkv] + list(more),
        19,
        scalars=[place],
        far=pieces,
        scratch=[
            pltpu.VMEM((rows, width), LOW),
            pltpu.VMEM((rows, width), LOW),
            pltpu.VMEM((rows, 3 * width), LOW),
        ]
        + ([pltpu.VMEM((8, width), FULL)] if own else [])
        + weight_scratch(width, pieces, planes),
    )


def unfold(source, target):
    groups, _, lines, wide = source.shape
    width = target.shape[1]
    fold = wide // width
    for group in range(groups):
        for at in range(fold):
            start = (group * fold + at) * lines
            target[start : start + lines, :] = source[group, 0, :, span(at, width)]


def feed_forward_kernel(
    lines_of, x_ref, vec_ref, bias_ref, in_ref, pack_ref, hn_ref, act_ref, slope_ref, out_ref, out_w_ref
):
    gain, shift, last = lines_of
    step = pl.program_id(0)

    @pl.when(step == 0)
    def _():
        hn_ref[...] = norm_low(
            x_ref[...], vec_ref[gain : gain + 1, :], vec_ref[shift : shift + 1, :]
        )
        out_ref[...] = x_ref[...] + vec_ref[last : last + 1, :]

    unfold(pack_ref, out_w_ref)
    for at in range(act_ref.shape[1] // TILE):
        cols = span(at, TILE)
        weight = in_ref[:, 0, :, cols].reshape(x_ref.shape[1], TILE)
        act, slope = gelu_parts(mul(hn_ref[...], weight) + bias_ref[:, cols])
        act_ref[:, cols] = act
        slope_ref[:, cols] = slope
    for at in range(out_ref.shape[1] // TILE):
        cols = span(at, TILE)
        out_ref[:, cols] += mul(act_ref[...], out_w_ref[:, cols])


def pack_blocks(pack, part, inner):
    groups, _, lines, _ = pack.shape
    return [
        pl.BlockSpec((groups, 1, lines, part), lambda at: (0, 0, 0, at)),
        pl.BlockSpec((part * groups // inner, 1, lines, inner), lambda at: (at, 1, 0, 0)),
    ]


def feed_forward(x, vec, bias, pack, lines_of):
    rows, width = x.shape
    inner = bias.shape[1]
    part = 768
    return run_kernel(
        partial(feed_forward_kernel, lines_of),
        [
            shape_of(rows, width, LOW),
            shape_of(rows, inner, LOW),
            shape_of(rows, inner, LOW),
            shape_of(rows, width, FULL),
        ],
        [x, vec, bias, pack, pack],
        11,
        scratch=[pltpu.VMEM((part, width), LOW)],
        grid=(inner // part,),
        in_blocks=[
            whole((rows, width)),
            whole(vec.shape),
            pl.BlockSpec((1, part), lambda at: (0, at)),
        ]
        + pack_blocks(pack, part, inner),
        out_blocks=[
            whole((rows, width)),
            pl.BlockSpec((rows, part), lambda at: (0, at)),
            pl.BlockSpec((rows, part), lambda at: (0, at)),
            whole((rows, width)),
        ],
    )


def feed_backward_kernel(
    gain, place_ref, up_ref, x_ref, vec_ref, slope_ref, in_ref, pack_ref,
    down_ref, mine_ref, away_ref, low_mine_ref, low_away_ref, sums_ref, bias_ref,
    dml_ref, du_ref, out_w_ref,
):
    step = pl.program_id(0)
    last = pl.num_programs(0) - 1
    width = x_ref.shape[1]
    part_cols = slope_ref.shape[1]

    @pl.when(step == 0)
    def _():
        dml_ref[...] = up_ref[...].astype(LOW)
        down_ref[...] = jnp.zeros(down_ref.shape, FULL)

    unfold(pack_ref, out_w_ref)
    for at in range(part_cols // TILE):
        cols = span(at, TILE)
        part = (
            mul_turned(dml_ref[...], out_w_ref[cols, :]) * slope_ref[:, cols].astype(FULL)
        ).astype(LOW)
        du_ref[step, :, cols] = part
        bias_ref[:, cols] = jnp.sum(part.astype(FULL), axis=0, keepdims=True)
    groups = in_ref.shape[0] // 2
    for at in range(2):
        weight = in_ref[span(at, groups), 0, :, :].reshape(width // 2, part_cols)
        down_ref[:, span(at, width // 2)] += mul_turned(du_ref[step, :, :], weight)

    @pl.when(step == last)
    def _():
        side = place_ref[1]
        grad, gain_sum, shift_sum = norm_back(x_ref[...], vec_ref[gain : gain + 1, :], down_ref[...])
        down_ref[...] = up_ref[...] + grad
        sums_ref[0:1, :] = gain_sum
        sums_ref[1:2, :] = shift_sum
        sums_ref[2:3, :] = jnp.sum(dml_ref[...].astype(FULL), axis=0, keepdims=True)
        sums_ref[3:8, :] = jnp.zeros((5, width), FULL)
        half = du_ref.shape[0] // 2
        for at in range(half):
            mine_ref[:, span(at, part_cols)] = du_ref[side * half + at, :, :]
            away_ref[:, span(at, part_cols)] = du_ref[(1 - side) * half + at, :, :]
        low_mine_ref[...] = dml_ref[:, span(side, width // 2)]
        low_away_ref[...] = dml_ref[:, span(1 - side, width // 2)]


def feed_backward(place, up, x, vec, slope, pack, gain):
    rows, width = x.shape
    inner = slope.shape[1]
    part = 768
    return run_kernel(
        partial(feed_backward_kernel, gain),
        [
            shape_of(rows, width, FULL),
            shape_of(rows, inner // 2, LOW),
            shape_of(rows, inner // 2, LOW),
            shape_of(rows, width // 2, LOW),
            shape_of(rows, width // 2, LOW),
            shape_of(8, width, FULL),
            shape_of(1, inner, FULL),
        ],
        [up, x, vec, slope, pack, pack],
        13,
        scalars=[place],
        scratch=[
            pltpu.VMEM((rows, width), LOW),
            pltpu.VMEM((inner // part, rows, part), LOW),
            pltpu.VMEM((part, width), LOW),
        ],
        grid=(inner // part,),
        in_blocks=[
            whole((rows, width)),
            whole((rows, width)),
            whole(vec.shape),
            pl.BlockSpec((rows, part), lambda at: (0, at)),
        ]
        + pack_blocks(pack, part, inner),
        out_blocks=[
            whole((rows, width)),
            whole((rows, inner // 2)),
            whole((rows, inner // 2)),
            whole((rows, width // 2)),
            whole((rows, width // 2)),
            whole((8, width)),
            pl.BlockSpec((1, part), lambda at: (0, at)),
        ],
    )


def product_kernel(counts, *refs):
    out_ref = refs[-1]
    start = 0
    at_ref = 0
    for count in counts:
        size = refs[at_ref + 1].shape[1]
        total = turned_mul(refs[at_ref][...], refs[at_ref + 1][...])
        for more in range(1, count):
            total += turned_mul(refs[at_ref + 2 * more][...], refs[at_ref + 2 * more + 1][...])
        out_ref[:, start : start + size] = total.astype(LOW)
        start += size
        at_ref += 2 * count
    if at_ref < len(refs) - 1:
        extra = refs[at_ref]
        out_ref[:, start : start + extra.shape[1]] = extra[...].astype(LOW)


def products(groups, extra=None, part=256):
    counts = [len(group) for group in groups]
    arrays = [array for group in groups for pair in group for array in pair]
    blocks = []
    for group in groups:
        for left, right in group:
            blocks += [pl.BlockSpec((left.shape[0], part), lambda at: (0, at)), whole(right.shape)]
    cols = sum(group[0][1].shape[1] for group in groups)
    if extra is not None:
        arrays.append(extra)
        blocks.append(pl.BlockSpec((part, extra.shape[1]), lambda at: (at, 0)))
        cols += extra.shape[1]
    lines = groups[0][0][0].shape[1]
    return run_kernel(
        partial(product_kernel, counts),
        [shape_of(lines, cols, LOW)],
        arrays,
        7,
        grid=(lines // part,),
        in_blocks=blocks,
        out_blocks=[pl.BlockSpec((part, cols), lambda at: (at, 0))],
    )[0]


def one_hot_rows(target, slots):
    hit = lax.broadcasted_iota(jnp.int32, (slots, target.shape[1]), 0) == target
    return jnp.where(hit, 1.0, 0.0).astype(LOW)


def one_hot_cols(target, slots):
    hit = lax.broadcasted_iota(jnp.int32, (target.shape[0], slots), 1) == target
    return jnp.where(hit, 1.0, 0.0).astype(LOW)


def slot_lanes(expert, slots, capacity):
    line = lax.broadcasted_iota(jnp.int32, (slots, 128), 0)
    lane = lax.broadcasted_iota(jnp.int32, (slots, 128), 1)
    return jnp.where((line == lane + expert * capacity) & (lane < capacity), 1.0, 0.0).astype(LOW)


def dispatch_kernel(
    experts, lines_of, x_ref, vec_ref, router_ref, route_ref, target_ref,
    mn_ref, gate_ref, pick_ref, out_ref, spot_ref,
):
    gain, shift = lines_of
    slots = out_ref.shape[0]
    capacity = slots // experts
    mn_ref[...] = norm_low(x_ref[...], vec_ref[gain : gain + 1, :], vec_ref[shift : shift + 1, :])
    logits = mul(mn_ref[...], router_ref[...])
    lane = lax.broadcasted_iota(jnp.int32, logits.shape, 1)
    logits = jnp.where(lane < experts, logits, -1e30)
    raised = jnp.exp(logits - jnp.max(logits, axis=-1, keepdims=True))
    gate = raised / jnp.sum(raised, axis=-1, keepdims=True)
    gate_ref[...] = gate
    picks = [
        jnp.sum(jnp.where(lane == route_ref[:, k : k + 1], gate, 0.0), axis=-1, keepdims=True)
        for k in range(2)
    ]
    pick = jnp.where(lane == 0, picks[0], jnp.where(lane == 1, picks[1], 0.0))
    pick_ref[...] = pick
    turned = pick.T
    for k in range(2):
        spot_ref[k, :, :] = one_hot_rows(target_ref[k : k + 1, :], slots)
    for at in range(out_ref.shape[1] // TILE):
        cols = span(at, TILE)
        out_ref[:, cols] = mul(spot_ref[0, :, :] + spot_ref[1, :, :], mn_ref[:, cols]).astype(LOW)
    row = lax.broadcasted_iota(jnp.int32, (16, 1), 0)
    weights = jnp.zeros((16, slots), FULL)
    for k in range(2):
        high, rest = split_low(turned[k : k + 1, :])
        both = jnp.where(row == 14, high.astype(FULL), jnp.where(row == 15, rest.astype(FULL), 0.0))
        weights += mul_turned(both.astype(LOW), spot_ref[k, :, :])
    weights = weights.astype(LOW)
    for expert in range(experts):
        lines = slice((expert + 1) * capacity - 16, (expert + 1) * capacity)
        chosen = mul(weights, slot_lanes(expert, slots, capacity))
        out_ref[lines, 0:128] = jnp.where(
            row >= 14, chosen, out_ref[lines, 0:128].astype(FULL)
        ).astype(LOW)


def dispatch(x, vec, router, routes, targets, experts, slots, lines_of):
    rows, width = x.shape
    return run_kernel(
        partial(dispatch_kernel, experts, lines_of),
        [
            shape_of(rows, width, LOW),
            shape_of(rows, 128, FULL),
            shape_of(rows, 128, FULL),
            shape_of(slots, width, LOW),
        ],
        [x, vec, router, routes, targets],
        6,
        scratch=[pltpu.VMEM((2, slots, rows), LOW)],
    )


def restore(place_ref, source, target):
    planes, lines, _ = target.shape
    for mask in range(planes):
        target[place_ref[0] ^ mask, :, :] = source[mask * lines : (mask + 1) * lines, :]


def unfold_lines(place_ref, source, target, lines):
    width = target.shape[1]
    fold = source.shape[1] // width
    many = source.shape[0] // lines
    for mask in range(many):
        group = mask ^ (place_ref[0] % many)
        for at in range(fold):
            start = pl.multiple_of((group * fold + at) * lines, lines)
            target[pl.ds(start, lines), :] = source[
                mask * lines : (mask + 1) * lines, span(at, width)
            ]


def hidden_kernel(
    experts, place_ref, x_ref, bias_ref, pack_ref, up_ref, act_ref, slope_ref, dy_ref, last_ref, w_ref
):
    restore(place_ref, pack_ref, w_ref)

    @pl.when(pl.program_id(0) == 0)
    def _():
        capacity = x_ref.shape[0] // experts
        row = lax.broadcasted_iota(jnp.int32, (128, 1), 0)
        table = jnp.zeros((128, 128), FULL)
        for group in range(experts):
            mark = x_ref[(group + 1) * capacity - 16 : (group + 1) * capacity, 0:128].astype(FULL)
            table = jnp.where(row == group, mark[14:15, :] + mark[15:16, :], table)
        table = table.T
        total = jnp.zeros(last_ref.shape, FULL)
        for group in range(experts):
            spots = slice(group * capacity, (group + 1) * capacity)
            part = (table[0:capacity, group : group + 1] * up_ref[spots, :].astype(FULL)).astype(LOW)
            dy_ref[spots, :] = part
            total += jnp.sum(part.astype(FULL), axis=0, keepdims=True)
        last_ref[...] = total

    for at in range(act_ref.shape[1] // TILE):
        cols = span(at, TILE)
        weight = w_ref[:, :, cols].reshape(x_ref.shape[1], TILE)
        act, slope = gelu_parts(mul(x_ref[...], weight) + bias_ref[:, cols])
        act_ref[:, cols] = act
        slope_ref[:, cols] = slope


def hidden_forward(place, x, bias, weight, up, planes, experts):
    rows, width = x.shape
    inner = bias.shape[1]
    part = 768
    return run_kernel(
        partial(hidden_kernel, experts),
        [
            shape_of(rows, inner, LOW),
            shape_of(rows, inner, LOW),
            shape_of(rows, width, LOW),
            shape_of(1, width, FULL),
        ],
        [x, bias, weight, up],
        11,
        scalars=[place],
        scratch=[pltpu.VMEM((planes, width // planes, part), LOW)],
        grid=(inner // part,),
        in_blocks=[
            whole(x.shape),
            pl.BlockSpec((1, part), lambda at: (0, at)),
            pl.BlockSpec((width, part), lambda at: (0, at)),
            whole(up.shape),
        ],
        out_blocks=[pl.BlockSpec((rows, part), lambda at: (0, at))] * 2
        + [whole((rows, width)), whole((1, width))],
    )


def expert_out_kernel(
    lines, experts, place_ref, act_ref, bias_ref, pack_ref, up_ref, out_ref, dot_ref, sum_ref, w_ref
):
    step = pl.program_id(0)
    unfold_lines(place_ref, pack_ref, w_ref, lines)

    @pl.when(step == 0)
    def _():
        sum_ref[...] = jnp.zeros(sum_ref.shape, FULL) + bias_ref[...]

    for at in range(w_ref.shape[1] // TILE):
        cols = span(at, TILE)
        sum_ref[:, cols] += mul(act_ref[...], w_ref[:, cols])

    @pl.when(step == pl.num_programs(0) - 1)
    def _():
        result = sum_ref[...].astype(LOW)
        out_ref[...] = result
        dots = jnp.sum(result.astype(FULL) * up_ref[...].astype(FULL), axis=-1, keepdims=True)
        capacity = result.shape[0] // experts
        lane = lax.broadcasted_iota(jnp.int32, (capacity, 128), 1)
        table = jnp.zeros((capacity, 128), FULL)
        for group in range(experts):
            table = jnp.where(lane == group, dots[group * capacity : (group + 1) * capacity], table)
        if capacity < 128:
            table = jnp.concatenate([table, jnp.zeros((128 - capacity, 128), FULL)], axis=0)
        table = table.T
        row = lax.broadcasted_iota(jnp.int32, (16, 1), 0)
        for group in range(experts):
            high, rest = split_low(table[group : group + 1, :])
            both = jnp.where(
                row == 14, high.astype(FULL), jnp.where(row == 15, rest.astype(FULL), 0.0)
            )
            dot_ref[group * 16 : (group + 1) * 16, :] = both.astype(LOW)


def expert_out_forward(place, act, bias, weight, up, lines, experts):
    rows, width = act.shape[0], weight.shape[1]
    inner = act.shape[1]
    part = 768
    many = part // lines
    return run_kernel(
        partial(expert_out_kernel, lines, experts),
        [shape_of(rows, width, LOW), shape_of(experts * 16, 128, LOW)],
        [act, bias, weight, up],
        9,
        scalars=[place],
        scratch=[pltpu.VMEM((rows, width), FULL), pltpu.VMEM((part, width), LOW)],
        grid=(inner // part,),
        in_blocks=[
            pl.BlockSpec((rows, part), lambda at, place: (0, at ^ (place[0] // many))),
            pl.BlockSpec(bias.shape, lambda at, place: (0, 0)),
            pl.BlockSpec((part, width), lambda at, place: (at, 0)),
            pl.BlockSpec(up.shape, lambda at, place: (0, 0)),
        ],
        out_blocks=[
            pl.BlockSpec((rows, width), lambda at, place: (0, 0)),
            pl.BlockSpec((experts * 16, 128), lambda at, place: (0, 0)),
        ],
        ahead=True,
    )


def expert_backward_kernel(
    lines, experts, place_ref, dy_ref, slope_ref, pack_ref, in_ref, dot_ref,
    dh_ref, bias_ref, back_ref, sum_ref, out_w_ref, in_w_ref,
):
    step = pl.program_id(0)
    rows = dy_ref.shape[0]
    capacity = rows // experts
    unfold_lines(place_ref, pack_ref, out_w_ref, lines)
    restore(place_ref, in_ref, in_w_ref)

    @pl.when(step == 0)
    def _():
        sum_ref[...] = jnp.zeros(sum_ref.shape, FULL)

    for at in range(slope_ref.shape[1] // TILE):
        cols = span(at, TILE)
        part = (
            mul_turned(dy_ref[...], out_w_ref[cols, :]) * slope_ref[:, cols].astype(FULL)
        ).astype(LOW)
        dh_ref[:, cols] = part
        bias_ref[:, cols] = jnp.sum(part.astype(FULL), axis=0, keepdims=True)
    planes, tall, part_cols = in_w_ref.shape
    for at in range(2):
        weight = in_w_ref[span(at, planes // 2), :, :].reshape(planes * tall // 2, part_cols)
        sum_ref[:, span(at, planes * tall // 2)] += mul_turned(dh_ref[...], weight)

    @pl.when(step == pl.num_programs(0) - 1)
    def _():
        back_ref[...] = sum_ref[...].astype(LOW)
        row = lax.broadcasted_iota(jnp.int32, (16, 1), 0)
        for group in range(experts):
            spots = slice((group + 1) * capacity - 16, (group + 1) * capacity)
            back_ref[spots, 0:128] = jnp.where(
                row >= 14,
                dot_ref[group * 16 : (group + 1) * 16, :].astype(FULL),
                sum_ref[spots, 0:128],
            ).astype(LOW)


def expert_backward(place, dy, slope, w_out, w_in, dots, lines, experts):
    rows, width = dy.shape
    inner = slope.shape[1]
    planes = inner // lines
    part = 768
    many = part // lines

    def moved(at, place):
        return (0, at ^ (place[0] // many))

    def fixed(at, place):
        return (0, 0)

    return run_kernel(
        partial(expert_backward_kernel, lines, experts),
        [
            shape_of(rows, inner, LOW),
            shape_of(1, inner, FULL),
            shape_of(rows, width, LOW),
        ],
        [dy, slope, w_out, w_in, dots],
        15,
        scalars=[place],
        scratch=[
            pltpu.VMEM((rows, width), FULL),
            pltpu.VMEM((part, width), LOW),
            pltpu.VMEM((planes, width // planes, part), LOW),
        ],
        grid=(inner // part,),
        in_blocks=[
            pl.BlockSpec((rows, width), fixed),
            pl.BlockSpec((rows, part), moved),
            pl.BlockSpec((part, width), lambda at, place: (at, 0)),
            pl.BlockSpec((width, part), moved),
            pl.BlockSpec(dots.shape, fixed),
        ],
        out_blocks=[
            pl.BlockSpec((rows, part), moved),
            pl.BlockSpec((1, part), moved),
            pl.BlockSpec((rows, width), fixed),
        ],
        ahead=True,
    )


def output_kernel(x_ref, home_ref, pick_ref, target_ref, live_ref, out_ref, spot_ref):
    slots = home_ref.shape[0]
    for k in range(2):
        spot_ref[k, :, :] = one_hot_cols(target_ref[:, k : k + 1], slots)
    for at in range(x_ref.shape[1] // TILE):
        cols = span(at, TILE)
        total = x_ref[:, cols]
        for k in range(2):
            total += pick_ref[:, k : k + 1] * mul(spot_ref[k, :, :], home_ref[:, cols])
        out_ref[:, cols] = (total * live_ref[...]).astype(LOW)


def output_rows(x, home, pick, targets, live):
    rows, width = x.shape
    return run_kernel(
        output_kernel,
        [shape_of(rows, width, LOW)],
        [x, home, pick, targets, live],
        7,
        scratch=[pltpu.VMEM((2, rows, home.shape[0]), LOW)],
    )[0]


def return_kernel(
    gain, experts, x_ref, vec_ref, home_ref, gate_ref, route_ref, target_ref, up_ref, mn_ref,
    router_ref, out_ref, sums_ref, router_grad_ref, spot_ref,
):
    rows, width = x_ref.shape
    slots = home_ref.shape[0]
    capacity = slots // experts
    for k in range(2):
        spot_ref[k, :, :] = one_hot_cols(target_ref[:, k : k + 1], slots)
    line = jnp.zeros((16, slots), FULL)
    for expert in range(experts):
        marks = home_ref[(expert + 1) * capacity - 16 : (expert + 1) * capacity, 0:128]
        line += mul_turned(marks, slot_lanes(expert, slots, capacity))
    line = line.astype(LOW)
    lane = lax.broadcasted_iota(jnp.int32, (rows, 128), 1)
    gate = gate_ref[...]
    spread = jnp.zeros((rows, 128), FULL)
    for k in range(2):
        dots = mul_turned(spot_ref[k, :, :], line)
        spread += jnp.where(lane == route_ref[:, k : k + 1], dots[:, 14:15] + dots[:, 15:16], 0.0)
    logit = gate * (spread - jnp.sum(gate * spread, axis=-1, keepdims=True))
    high, rest = split_low(pltpu.roll(logit, 15, 1))
    router_grad_ref[...] = turned_mul(mn_ref[...], high) + turned_mul(mn_ref[...], rest)
    high, rest = split_low(logit)
    for at in range(width // TILE):
        cols = span(at, TILE)
        out_ref[:, cols] = (
            mul_turned(high, router_ref[cols, :])
            + mul_turned(rest, router_ref[cols, :])
            + mul(spot_ref[0, :, :] + spot_ref[1, :, :], home_ref[:, cols])
        )

    grad, gain_sum, shift_sum = norm_back(x_ref[...], vec_ref[gain : gain + 1, :], out_ref[...])
    out_ref[...] = up_ref[...].astype(FULL) + grad
    sums_ref[0:1, :] = gain_sum
    sums_ref[1:2, :] = shift_sum
    sums_ref[2:8, :] = jnp.zeros((6, width), FULL)


def return_grad(x, vec, home, gate, routes, targets, up, mn, router, gain, experts, after):
    rows, width = x.shape
    slots = home.shape[0]
    return run_kernel(
        partial(return_kernel, gain, experts),
        [shape_of(rows, width, FULL), shape_of(8, width, FULL), shape_of(width, 128, FULL)],
        [x, vec, home, gate, routes, targets, up, mn, router],
        7,
        far=after,
        scratch=[pltpu.VMEM((2, rows, slots), LOW)],
    )


def feed_products_kernel(lines, fold, hn_ref, hn_far_ref, du_ref, du_far_ref, act_ref, act_far_ref, low_ref, low_far_ref, out_ref):
    cols = du_ref.shape[1] // fold
    tall = 2 * fold * lines
    tile = hn_ref.shape[1]
    for at in range(fold):
        part = turned_mul(hn_ref[...], du_ref[:, span(at, cols)])
        part += turned_mul(hn_far_ref[...], du_far_ref[:, span(at, cols)])
        part = part.astype(LOW)
        for spot in range(tile // lines):
            start = spot * tall + at * lines
            out_ref[start : start + lines, :] = part[spot * lines : (spot + 1) * lines, :]
    for at in range(act_ref.shape[1] // tile):
        part = turned_mul(act_ref[:, span(at, tile)], low_ref[...])
        part += turned_mul(act_far_ref[:, span(at, tile)], low_far_ref[...])
        part = part.astype(LOW)
        size = fold * lines
        for spot in range(tile // size):
            start = (at * (tile // size) + spot) * tall + size
            out_ref[start : start + size, :] = part[spot * size : (spot + 1) * size, :]


def feed_products(hn, hn_far, du, du_far, act, act_far, low, low_far, blocks, fold):
    rows, width = hn.shape
    lines = width // blocks
    tall = 2 * fold * lines
    steps = 2
    left = pl.BlockSpec((rows, width // steps), lambda at: (0, at))
    wide = pl.BlockSpec((rows, fold * width // steps), lambda at: (0, at))
    return run_kernel(
        partial(feed_products_kernel, lines, fold),
        [shape_of(blocks * tall, low.shape[1], LOW)],
        [hn, hn_far, du, du_far, act, act_far, low, low_far],
        11,
        grid=(steps,),
        in_blocks=[left, left, whole(du.shape), whole(du.shape), wide, wide, whole(low.shape), whole(low.shape)],
        out_blocks=[pl.BlockSpec((blocks * tall // steps, low.shape[1]), lambda at: (at, 0))],
    )[0]


def expert_products_kernel(lines, x_ref, dh_ref, in_bias_ref, out_bias_ref, out_ref):
    width = out_bias_ref.shape[1]
    planes = width // lines
    tall = lines + 16
    step = pl.program_id(0)
    row = lax.broadcasted_iota(jnp.int32, (16, 1), 0)
    last = jnp.where(step == 0, 1.0, 0.0) * out_bias_ref[...]
    both = jnp.where(row == 0, in_bias_ref[...], jnp.where(row == 1, last, 0.0)).astype(LOW)
    many = max(1, 384 // lines)
    for at in range(planes // many):
        part = turned_mul(x_ref[:, span(at, many * lines)], dh_ref[...]).astype(LOW)
        for spot in range(many):
            start = (at * many + spot) * tall
            out_ref[start : start + lines, :] = part[spot * lines : (spot + 1) * lines, :]
            out_ref[start + lines : start + tall, :] = both


def expert_products(x, dh, in_bias, out_bias, planes):
    slots, width = x.shape
    inner = dh.shape[1]
    lines = width + 16 * planes
    return run_kernel(
        partial(expert_products_kernel, width // planes),
        [shape_of(lines, inner, LOW)],
        [x, dh, in_bias, out_bias],
        8,
        grid=(inner // width,),
        in_blocks=[
            whole(x.shape),
            pl.BlockSpec((slots, width), lambda at: (0, at)),
            pl.BlockSpec((1, width), lambda at: (0, at)),
            whole(out_bias.shape),
        ],
        out_blocks=[pl.BlockSpec((lines, width), lambda at: (0, at))],
    )[0]


def spread_kernel(target_ref, up_ref, out_ref, spot_ref):
    slots = out_ref.shape[0]
    spot_ref[...] = one_hot_rows(target_ref[0:1, :], slots) + one_hot_rows(target_ref[1:2, :], slots)
    for at in range(out_ref.shape[1] // TILE):
        cols = span(at, TILE)
        out_ref[:, cols] = mul(spot_ref[...], up_ref[:, cols]).astype(LOW)


def spread_up(targets, up, slots):
    rows, width = up.shape
    return run_kernel(
        spread_kernel,
        [shape_of(slots, width, LOW)],
        [targets, up],
        4,
        scratch=[pltpu.VMEM((slots, rows), LOW)],
    )[0]


tie = lax.optimization_barrier


def trade(value, axis_name, mask):
    count = lax.axis_size(axis_name)
    return lax.ppermute(value, axis_name, [(place, place ^ mask) for place in range(count)])


def in_order(pieces, place):
    level = 0
    while len(pieces) > 1:
        flip = ((place >> level) & 1) == 1
        pieces = [
            jnp.where(
                flip,
                jnp.concatenate([pieces[at + 1], pieces[at]], axis=0),
                jnp.concatenate([pieces[at], pieces[at + 1]], axis=0),
            )
            for at in range(0, len(pieces), 2)
        ]
        level += 1
    return pieces[0]


def core_side():
    return lax.axis_index("expert") % 2


def core_half(shard):
    side = core_side()
    half = shard.shape[1] // 2
    mine = lax.dynamic_slice_in_dim(shard, side * half, half, 1)
    away = lax.dynamic_slice_in_dim(shard, (1 - side) * half, half, 1)
    return in_order([mine, trade(away, "expert", 1)], side)


def layer_gather(shard):
    layers = lax.axis_size("expert") // 2
    stacked = [shard] + [trade(shard, "expert", 2 * mask) for mask in range(1, layers)]
    return in_order(stacked, lax.axis_index("expert") // 2)


def plane_near(piece):
    count = lax.axis_size("fsdp")
    masks = (1, 2) if count == 4 else range(1, count)
    return [trade(piece, "fsdp", mask) for mask in masks]


def plane_far(near):
    if lax.axis_size("fsdp") != 4:
        return []
    half = near[0].shape[0] // 2
    return [trade(near[1][:half], "fsdp", 1), trade(near[0][half:], "fsdp", 2)]


def both_cores(own, near, far):
    held = jnp.concatenate([own] + near + far, axis=0)
    return held, trade(held, "expert", 1)


def sum_first(blocks):
    count = lax.axis_size("fsdp")
    place = lax.axis_index("fsdp")
    parts = [
        lax.dynamic_index_in_dim(blocks, place ^ mask, 0, keepdims=False) for mask in range(count)
    ]
    if count != 4:
        return parts, []
    half = blocks.shape[1] // 2
    return parts[:3], [
        trade(parts[3][:half], "fsdp", 1),
        trade(parts[3][half:], "fsdp", 2),
    ]


def added(left, right):
    return (left.astype(FULL) + right.astype(FULL)).astype(LOW)


def sum_second(parts, got):
    if not got:
        return [trade(part, "fsdp", mask) for mask, part in enumerate(parts) if mask > 0]
    half = parts[1].shape[0] // 2
    send_x = jnp.concatenate([parts[1][:half], added(parts[1][half:], got[1])], axis=0)
    send_y = jnp.concatenate([added(parts[2][:half], got[0]), parts[2][half:]], axis=0)
    return [trade(send_x, "fsdp", 1), trade(send_y, "fsdp", 2)]


def sum_total(own, arrived):
    total = own.astype(FULL)
    for term in arrived:
        total = total + term.astype(FULL)
    return total


def layer_first(held):
    layer = lax.axis_index("expert") // 2
    layers = lax.axis_size("expert") // 2
    parts = [
        lax.dynamic_index_in_dim(held, layer ^ mask, 0, keepdims=False) for mask in range(layers)
    ]
    return parts[0], [trade(parts[mask], "expert", 2 * mask) for mask in range(1, layers)]


def core_last(total):
    side = core_side()
    rows = total.shape[0] // 2
    mine = lax.dynamic_slice_in_dim(total, side * rows, rows, 0)
    away = lax.dynamic_slice_in_dim(total, (1 - side) * rows, rows, 0).astype(LOW)
    came = trade(away, "expert", 1).astype(FULL)
    return jnp.where(side == 0, mine, came), jnp.where(side == 0, came, mine)


def feed_half(fc_in, fc_out):
    side = core_side()
    lines, inner = fc_in.shape
    fold = inner // fc_out.shape[1]
    blocks = [fc_out[at * lines : (at + 1) * lines] for at in range(fold)]
    folded = jnp.concatenate(blocks, axis=1)
    came = trade(jnp.where(side == 0, folded, fc_in), "expert", 1)
    width = fc_out.shape[1]
    rows_came = [came[:, at * width : (at + 1) * width] for at in range(fold)]
    stacked = [
        jnp.concatenate([group[at], group[at + 1]], axis=0)
        for group in (rows_came, blocks)
        for at in range(0, fold, 2)
    ]
    return jnp.where(
        side == 0, jnp.concatenate([fc_in, came], axis=0), jnp.concatenate(stacked, axis=1)
    )


def feed_last(total, fold):
    side = core_side()
    cols = total.shape[1]
    size = total.shape[0] // 2
    inside = total[:size].reshape(fold, 2, -1, cols)
    outside = total[size:].reshape(2, -1, cols)

    def part(core):
        return jnp.concatenate(
            [
                lax.dynamic_index_in_dim(inside, core, 1, keepdims=False).reshape(-1, cols),
                lax.dynamic_index_in_dim(outside, core, 0, keepdims=False),
            ],
            axis=0,
        )

    mine = part(side)
    came = trade(part(1 - side).astype(LOW), "expert", 1).astype(FULL)
    return jnp.where(side == 0, mine, came), jnp.where(side == 0, came, mine)


def in_blocks(half_grad):
    planes = lax.axis_size("fsdp")
    layers = lax.axis_size("expert") // 2
    return half_grad.reshape(planes, layers, -1, half_grad.shape[-1])


def per_device(
    patches,
    dense_gains,
    dense_shifts,
    dense_qkv,
    dense_proj,
    dense_fc_in,
    dense_fc_bias,
    dense_fc_out,
    moe_gains,
    moe_shifts,
    moe_qkv,
    moe_proj,
    router,
    expert_in,
    expert_in_bias,
    expert_out,
    expert_out_bias,
    routes,
    slot_pos,
    image_counts,
    cotangent,
):
    images, length, width = patches.shape
    shard_rows = dense_qkv.shape[0]
    inner = dense_fc_in.shape[1]
    local_experts = expert_in.shape[0]
    experts = local_experts * lax.axis_size("expert")
    planes = lax.axis_size("fsdp")
    plane = lax.axis_index("fsdp")
    place = jnp.stack([plane, core_side()]).astype(jnp.int32)
    block = fit(length, 16)
    rows = images * block
    lowest = (images + 1) // 2
    capacity = fit(5 * (images + lowest) * length // (4 * experts) + 4, 16)
    slots = experts * capacity

    def padded(array, fill=0):
        return jnp.pad(
            array, ((0, 0), (0, block - length), (0, 0)), constant_values=fill
        ).reshape(rows, array.shape[-1])

    def trimmed(array):
        return array.reshape(images, block, array.shape[-1])[:, :length]

    def far(array):
        return trade(array, "expert", 1)

    layers = lax.axis_size("expert") // 2
    fold = inner // width
    small_rows = jnp.concatenate(
        [
            dense_gains.T,
            dense_shifts.T,
            moe_gains.T,
            moe_shifts.T,
            router,
            dense_fc_bias.reshape(shard_rows, -1),
        ],
        axis=1,
    )
    small_cols = small_rows.shape[1]
    small_rows = jnp.pad(small_rows, ((0, 0), (0, 256 - small_cols)))
    first_half = core_half(jnp.concatenate([dense_qkv, dense_proj, small_rows], axis=1))
    moe_half = core_half(jnp.concatenate([moe_qkv, moe_proj], axis=1))
    if (2 * shard_rows) % 16 == 0:
        later = feed_half(dense_fc_in, dense_fc_out)
        pack = lax.all_gather(later, ("fsdp", "expert"), axis=0, tiled=True)
        pack = pack.reshape(planes * layers, 2, 2 * shard_rows, later.shape[1])
    else:
        groups = width // 48
        whole_in = lax.all_gather(dense_fc_in, ("fsdp", "expert"), axis=0, tiled=True)
        whole_out = lax.all_gather(dense_fc_out, ("fsdp", "expert"), axis=0, tiled=True)
        folded = whole_out.reshape(groups, fold, 48, width).swapaxes(1, 2).reshape(groups, 48, inner)
        pack = jnp.stack([whole_in.reshape(groups, 48, inner), folded], axis=1)
    dense_own = layer_gather(first_half)
    dense_own, moe_half = tie((dense_own, moe_half))
    dense_near = plane_near(dense_own)
    moe_own = layer_gather(moe_half)
    dense_near, moe_own = tie((dense_near, moe_own))
    dense_far = plane_far(dense_near)
    moe_near = plane_near(moe_own)
    dense_pieces = both_cores(dense_own, dense_near, dense_far)

    live_images = jnp.arange(images) < image_counts[0]
    live_rows = jnp.repeat(live_images, block).astype(FULL)[:, None]
    up = padded(jnp.where(live_images[:, None, None], cotangent, jnp.zeros_like(cotangent)))
    route_cols = padded(routes)
    target_cols = padded(jnp.where(slot_pos >= 0, routes * capacity + slot_pos, -1), -1)
    target_rows = target_cols.T

    def exchange(array):
        return lax.all_to_all(
            array.reshape(experts, capacity, width), "expert", split_axis=0, concat_axis=0, tiled=True
        ).reshape(slots, width)

    x0, up_spread = tie((padded(patches).astype(FULL), spread_up(target_rows, up, slots)))
    up_slots = exchange(up_spread)
    an, qkv, mixed, x1, vec, fc_bias, router_full = attend_forward(
        place, x0, None, dense_pieces, planes, (0, 2, 4, 5, 6), length, images, experts, inner
    )
    x1, moe_near, in_own, out_own = tie((x1, moe_near, expert_in[0], expert_out[0]))
    moe_pieces = both_cores(moe_own, moe_near, plane_far(moe_near))
    in_near = plane_near(in_own)
    out_near = plane_near(out_own)
    expert_bias = jnp.concatenate([expert_in_bias[0], expert_out_bias[0]])
    other_bias = tie([trade(expert_bias, "fsdp", mask) for mask in range(1, planes)])
    expert_bias = in_order([part[None] for part in [expert_bias] + other_bias], plane).astype(FULL)
    hidden_part = expert_in_bias.shape[1]
    in_bias = expert_bias[:, :hidden_part].reshape(1, -1)
    out_bias = expert_bias[:, hidden_part:].reshape(1, -1)

    hn, act, slope, x2 = feed_forward(x1, vec, fc_bias, pack, (1, 3, 7))
    an2, qkv2, mixed2, x3 = attend_forward(
        place, x2, vec, moe_pieces, planes, (8, 10, 12, 13, 14), length, images, experts, inner
    )
    x3, up_slots = tie((x3, up_slots))
    in_far = plane_far(in_near)
    out_far = plane_far(out_near)
    w_in = jnp.concatenate([in_own] + in_near + in_far, axis=0)
    w_out = jnp.concatenate([out_own] + out_near + out_far, axis=0)
    mn, gate, pick, outgoing = dispatch(
        x3, vec, router_full, route_cols, target_rows, experts, slots, (9, 11)
    )
    arrived = exchange(outgoing)
    arrived, an2_far, mixed2_far, w_out = tie((arrived, far(an2), far(mixed2), w_out))
    e_act, e_slope, dy, out_bias_grad = hidden_forward(
        place, arrived, in_bias, w_in, up_slots, planes, experts
    )
    out_grad = products([[(e_act, dy)]], part=768)
    out_grad, e_act = tie((out_grad, e_act))
    expert_out_sum = lax.psum_scatter(out_grad, "fsdp", scatter_dimension=0, tiled=True)
    hidden_rows = inner // planes
    result, dots = expert_out_forward(
        place, e_act, out_bias, w_out, up_slots, hidden_rows, experts
    )
    dh, in_bias_grad, back = expert_backward(
        place, dy, e_slope, w_out, w_in, dots, hidden_rows, experts
    )
    back = exchange(back)
    expert_grad = expert_products(arrived, dh, in_bias_grad, out_bias_grad, planes)
    lefts = [far(array) for array in (hn, act, an, mixed)]
    expert_grad, back, result, expert_out_sum, lefts = tie(
        (expert_grad, back, result, expert_out_sum, lefts)
    )
    hn_far, act_far, an_far, mixed_far = lefts
    expert_sum = lax.psum_scatter(expert_grad, "fsdp", scatter_dimension=0, tiled=True)
    home = exchange(result)
    dx3, gate_sums, router_grad = return_grad(
        x3, vec, back, gate, route_cols, target_cols, up, mn, router_full, 9, experts, []
    )
    dx2, mine2, away2, low_mine2, low_away2, moe_sums = attend_backward(
        place, dx3, x2, vec, qkv2, moe_pieces, planes, 8, length, images
    )
    dx1, mine1, away1, low_mine1, low_away1, feed_sums, fc_bias_grad = feed_backward(
        place, dx2, x1, vec, slope, pack, 1
    )
    away2, low_away2, away1, low_away1, dx1 = tie(
        (far(away2), far(low_away2), far(away1), far(low_away1), dx1)
    )
    moe_grad = products(
        [
            [(an2, mine2), (an2_far, away2)],
            [(mixed2, low_mine2), (mixed2_far, low_away2)],
        ]
    )
    moe_parts, moe_got = sum_first(in_blocks(moe_grad))
    if (2 * shard_rows) % 16 == 0:
        feed_grad = feed_products(
            hn, hn_far, mine1, away1, act, act_far, low_mine1, low_away1,
            planes * layers, fold,
        )
    else:
        in_part = products([[(hn, mine1), (hn_far, away1)]])
        out_part = products([[(act, low_mine1), (act_far, low_away1)]], part=768)
        in_part = in_blocks(in_part)
        in_part = in_part.reshape(in_part.shape[:3] + (fold, -1)).swapaxes(2, 3)
        in_part = in_part.reshape(planes, layers, -1, in_part.shape[-1])
        feed_grad = jnp.concatenate([in_part, in_blocks(out_part)], axis=2)
        feed_grad = feed_grad.reshape(-1, feed_grad.shape[-1])
    feed_grad, dx1, home, moe_got = tie((feed_grad, dx1, home, moe_got))
    feed_parts, feed_got = sum_first(in_blocks(feed_grad))
    moe_came = sum_second(moe_parts, moe_got)
    dx0, mine0, away0, low_mine0, low_away0, vectors = attend_backward(
        place, dx1, x0, vec, qkv, dense_pieces, planes, 0, length, images, experts,
        [feed_sums, moe_sums, gate_sums, fc_bias_grad, router_grad],
    )
    feed_got, moe_came, mine0, expert_sum = tie((feed_got, moe_came, mine0, expert_sum))
    feed_came = sum_second(feed_parts, feed_got)
    moe_mine, moe_layers = layer_first(sum_total(moe_parts[0], moe_came).astype(LOW))
    dense_grad = products(
        [
            [(an, mine0), (an_far, far(away0))],
            [(mixed, low_mine0), (mixed_far, far(low_away0))],
        ],
        vectors,
    )
    dense_grad, moe_layers = tie((dense_grad, moe_layers))
    dense_parts, dense_got = sum_first(in_blocks(dense_grad))
    output = output_rows(x3, home, pick, target_cols, live_rows)
    dense_got, feed_came = tie((dense_got, feed_came))
    dense_came = sum_second(dense_parts, dense_got)
    feed_mine, feed_layers = layer_first(sum_total(feed_parts[0], feed_came).astype(LOW))
    moe_left, moe_right = core_last(sum_total(moe_mine, moe_layers))
    dense_came, feed_layers, output = tie((dense_came, feed_layers, output))
    dense_mine, dense_layers = layer_first(sum_total(dense_parts[0], dense_came).astype(LOW))
    feed_left, feed_right = feed_last(sum_total(feed_mine, feed_layers), fold)
    dense_left, dense_right = core_last(sum_total(dense_mine, dense_layers))
    third = 3 * width // 2

    def split(left, right):
        return (
            jnp.concatenate([left[:, :third], right[:, :third]], axis=1),
            jnp.concatenate([left[:, third : 2 * width], right[:, third : 2 * width]], axis=1),
        )

    dense_qkv_sum, dense_proj_sum = split(dense_left, dense_right)
    moe_qkv_sum, moe_proj_sum = split(moe_left, moe_right)
    small_sum = dense_left[:, 2 * width :] + dense_right[:, 2 * width :]
    feed_in_sum = jnp.concatenate(
        [
            half[at * shard_rows : (at + 1) * shard_rows]
            for half in (feed_left, feed_right)
            for at in range(fold)
        ],
        axis=1,
    )
    feed_out_sum = jnp.concatenate(
        [feed_left[fold * shard_rows :], feed_right[fold * shard_rows :]], axis=1
    )
    expert_rows = width // planes
    expert_in_sum = expert_sum[:expert_rows].astype(FULL)[None]
    expert_out_sum = expert_out_sum.astype(FULL)[None]
    bias_rows = expert_sum[expert_rows:].astype(FULL)
    in_bias_sum = lax.dynamic_slice(bias_rows, (0, plane * hidden_part), (1, hidden_part))
    out_bias_sum = lax.dynamic_slice(bias_rows, (1, plane * expert_rows), (1, expert_rows))
    small_turn = small_sum[:, :15].T
    return (
        trimmed(output),
        trimmed(dx0),
        small_turn[0:2],
        small_turn[2:8],
        dense_qkv_sum,
        dense_proj_sum,
        feed_in_sum,
        small_sum[:, 15 + experts : small_cols].reshape(-1),
        feed_out_sum,
        small_turn[8:10],
        small_turn[10:15],
        moe_qkv_sum,
        moe_proj_sum,
        small_sum[:, 15 : 15 + experts],
        expert_in_sum,
        in_bias_sum,
        expert_out_sum,
        out_bias_sum,
    )


def solution(mesh):
    return jax.shard_map(
        per_device,
        mesh=mesh,
        in_specs=(
            P(("fsdp", "expert"), None, None),
            P(None, ("fsdp", "expert")),
            P(None, ("fsdp", "expert")),
            P(("fsdp", "expert"), None),
            P(("fsdp", "expert"), None),
            P(("fsdp", "expert"), None),
            P(("fsdp", "expert")),
            P(("fsdp", "expert"), None),
            P(None, ("fsdp", "expert")),
            P(None, ("fsdp", "expert")),
            P(("fsdp", "expert"), None),
            P(("fsdp", "expert"), None),
            P(("fsdp", "expert"), None),
            P("expert", "fsdp", None),
            P("expert", "fsdp"),
            P("expert", "fsdp", None),
            P("expert", "fsdp"),
            P(("fsdp", "expert"), None, None),
            P(("fsdp", "expert"), None, None),
            P(("fsdp", "expert")),
            P(("fsdp", "expert"), None, None),
        ),
        out_specs=(
            P(("fsdp", "expert"), None, None),
            P(("fsdp", "expert"), None, None),
            P(None, ("fsdp", "expert")),
            P(None, ("fsdp", "expert")),
            P(("fsdp", "expert"), None),
            P(("fsdp", "expert"), None),
            P(("fsdp", "expert"), None),
            P(("fsdp", "expert")),
            P(("fsdp", "expert"), None),
            P(None, ("fsdp", "expert")),
            P(None, ("fsdp", "expert")),
            P(("fsdp", "expert"), None),
            P(("fsdp", "expert"), None),
            P(("fsdp", "expert"), None),
            P("expert", "fsdp", None),
            P("expert", "fsdp"),
            P("expert", "fsdp", None),
            P("expert", "fsdp"),
        ),
        check_vma=False,
    )
```

```python
from functools import partial

import jax
import jax.numpy as jnp
from jax import lax
from jax.experimental import pallas as pl
from jax.experimental.pallas import tpu as pltpu
from jax.sharding import PartitionSpec as P

TILE = 256
LOW = jnp.bfloat16
FULL = jnp.float32
eps_norm = 1e-06


def fit(count, step):
    return -(-count // step) * step


def whole(shape):
    return pl.BlockSpec(shape, lambda *at: (0,) * len(shape))


def shape_of(rows, cols, kind):
    return jax.ShapeDtypeStruct((rows, cols), kind)


def run_kernel(kernel, outs, arrays, micros, scalars=(), scratch=(), far=(), grid=None, in_blocks=None, out_blocks=None, ahead=False):
    nbytes = sum(a.size * a.dtype.itemsize for a in list(arrays) + list(far))
    nbytes += sum(o.size * o.dtype.itemsize for o in outs)
    if grid is None:
        in_blocks = [pl.BlockSpec(memory_space=pltpu.VMEM)] * len(arrays)
        out_blocks = [pl.BlockSpec(memory_space=pltpu.VMEM)] * len(outs)
    in_specs = [pl.BlockSpec(memory_space=pltpu.SMEM)] * len(scalars)
    in_specs += list(in_blocks) + [pl.BlockSpec(memory_space=pl.ANY)] * len(far)
    if ahead:
        more = {
            "grid_spec": pltpu.PrefetchScalarGridSpec(
                num_scalar_prefetch=len(scalars),
                grid=grid,
                in_specs=in_specs[len(scalars) :],
                out_specs=list(out_blocks),
                scratch_shapes=list(scratch),
            )
        }
    else:
        more = {
            "in_specs": in_specs,
            "out_specs": list(out_blocks),
            "scratch_shapes": list(scratch),
        }
        if grid is not None:
            more["grid"] = grid
    return pl.pallas_call(
        kernel,
        out_shape=list(outs),
        compiler_params=pltpu.CompilerParams(vmem_limit_bytes=56 * 1024 * 1024),
        cost_estimate=pl.CostEstimate(
            flops=int(micros * 0.4e9), bytes_accessed=nbytes, transcendentals=0
        ),
        **more,
    )(*scalars, *arrays, *far)


def mul(left, right):
    return jnp.dot(left, right, preferred_element_type=FULL)


def mul_turned(left, right):
    return lax.dot_general(left, right, (((1,), (1,)), ((), ())), preferred_element_type=FULL)


def turned_mul(left, right):
    return lax.dot_general(left, right, (((0,), (0,)), ((), ())), preferred_element_type=FULL)


def span(at, size):
    if isinstance(at, int):
        return slice(at * size, (at + 1) * size)
    return pl.ds(pl.multiple_of(at * size, size), size)


def norm_parts(values):
    center = values - jnp.mean(values, axis=-1, keepdims=True)
    spread = jnp.mean(center * center, axis=-1, keepdims=True)
    return center, lax.rsqrt(spread + eps_norm)


def norm_low(values, gain, shift):
    center, scale = norm_parts(values)
    return (center * scale * gain + shift).astype(LOW)


def norm_back(values, gain, upstream):
    center, scale = norm_parts(values)
    unit = center * scale
    inner = upstream * gain
    grad = scale * (
        inner
        - jnp.mean(inner, axis=-1, keepdims=True)
        - unit * jnp.mean(inner * unit, axis=-1, keepdims=True)
    )
    return (
        grad,
        jnp.sum(upstream * unit, axis=0, keepdims=True),
        jnp.sum(upstream, axis=0, keepdims=True),
    )


def gelu_parts(values):
    rate = 0.7978845608028654
    square = values * values
    bend = jnp.tanh(values * (rate + (rate * 0.044715) * square))
    half = 0.5 + 0.5 * bend
    slope = half + (values * (1.0 - bend * bend)) * (0.5 * rate + (1.5 * rate * 0.044715) * square)
    return (values * half).astype(LOW), slope.astype(LOW)


def split_low(values):
    high = values.astype(LOW)
    return high, (values - high.astype(FULL)).astype(LOW)


def head_masks():
    lane = lax.broadcasted_iota(jnp.int32, (1, 128), 1)
    first = (lane < 64).astype(FULL)
    return first, 1.0 - first


def near_copies(place_ref, own_ref, other_ref, target, sems):
    plane, side = place_ref[0], place_ref[1]
    count = sems.shape[0] // 2
    half_cols = own_ref.shape[1]
    lines = own_ref.shape[0] // count
    copies = []
    for core, source in enumerate((own_ref, other_ref)):
        cols = pl.ds(pl.multiple_of((side if core == 0 else 1 - side) * half_cols, 128), half_cols)
        for mask in range(count):
            start = pl.multiple_of((plane ^ mask) * lines, lines)
            copies.append(
                pltpu.make_async_copy(
                    source.at[pl.ds(mask * lines, lines), :],
                    target.at[pl.ds(start, lines), cols],
                    sems.at[core * count + mask],
                )
            )
    return copies


def score_parts(query, key, mask, keep):
    scores = mul_turned(query * (0.125 * mask).astype(LOW), key)
    scores = jnp.where(keep, scores, -1e30)
    raised = jnp.exp(scores - jnp.max(scores, axis=-1, keepdims=True))
    return raised * (1.0 / jnp.sum(raised, axis=-1, keepdims=True))


def attend_forward_kernel(length, images, lines_of, own, experts, *refs):
    if own:
        (
            place_ref, x_ref, near_ref, other_ref,
            an_ref, qkv_ref, o_ref, out_ref, vec_ref, wide_ref, router_ref, w_ref, sems,
        ) = refs
    else:
        (
            place_ref, x_ref, vec_ref, near_ref, other_ref,
            an_ref, qkv_ref, o_ref, out_ref, w_ref, sems,
        ) = refs
    copies = near_copies(place_ref, near_ref, other_ref, w_ref, sems)
    gain, shift, q_line, v_line, o_line = lines_of
    for copy in copies:
        copy.start()
    rows, width = x_ref.shape
    block = rows // images
    pairs = width // 128
    for copy in copies:
        copy.wait()
    if own:
        small = w_ref[:, 4 * width : 4 * width + 128]
        turned = small.astype(FULL).T
        vec_ref[...] = turned[0:32, :]
        spot = lax.broadcasted_iota(jnp.int32, (128, 128), 0) - lax.broadcasted_iota(
            jnp.int32, (128, 128), 1
        )
        lane = lax.broadcasted_iota(jnp.int32, (128, 128), 1)
        pick = jnp.where((spot == 15) & (lane < experts), 1.0, 0.0).astype(LOW)
        router_ref[...] = mul(small, pick).astype(LOW)
        depth = wide_ref.shape[1] // width
        near = lax.broadcasted_iota(jnp.int32, (128, 128 * depth), 0)
        place = lax.broadcasted_iota(jnp.int32, (128, 128 * depth), 1)
        spread = jnp.where(place // depth == near, 1.0, 0.0).astype(LOW)
        line = lax.broadcasted_iota(jnp.int32, (128, 128 * depth), 0)
        for at in range(width // 128):
            many = mul(turned[:, span(at, 128)].astype(LOW), spread)
            keep_line = line == place % depth + 15 + experts
            wide_ref[:, span(at, 128 * depth)] = jnp.sum(
                jnp.where(keep_line, many, 0.0), axis=0, keepdims=True
            )
    an_ref[...] = norm_low(x_ref[...], vec_ref[gain : gain + 1, :], vec_ref[shift : shift + 1, :])
    for at in range(3 * width // TILE):
        part = mul(an_ref[...], w_ref[:, span(at, TILE)])
        here = (at * TILE) % width
        if at * TILE < width:
            part = part + vec_ref[q_line : q_line + 1, here : here + TILE]
        elif at * TILE >= 2 * width:
            part = part + vec_ref[v_line : v_line + 1, here : here + TILE]
        qkv_ref[:, span(at, TILE)] = part.astype(LOW)

    first, second = head_masks()
    keep = lax.broadcasted_iota(jnp.int32, (1, block), 1) < length
    for image in range(images):
        for pair in range(pairs):
            lines = span(image, block)
            query = qkv_ref[lines, span(pair, 128)]
            key = qkv_ref[lines, span(pair + pairs, 128)]
            value = qkv_ref[lines, span(pair + 2 * pairs, 128)]
            mixed = [
                mul(score_parts(query, key, mask, keep).astype(LOW), value)
                for mask in (first, second)
            ]
            o_ref[lines, span(pair, 128)] = (mixed[0] * first + mixed[1] * second).astype(LOW)

    for at in range(width // TILE):
        cols = span(at, TILE)
        weight = w_ref[:, 3 * width + at * TILE : 3 * width + (at + 1) * TILE]
        out_ref[:, cols] = x_ref[:, cols] + (
            mul(o_ref[...], weight) + vec_ref[o_line : o_line + 1, cols]
        )


def weight_scratch(width, pieces, planes):
    cols = 2 * pieces[0].shape[1]
    return [pltpu.VMEM((width, cols), LOW), pltpu.SemaphoreType.DMA((2 * planes,))]


def attend_forward(place, x, vec, pieces, planes, lines_of, length, images, experts, inner):
    rows, width = x.shape
    outs = [
        shape_of(rows, width, LOW),
        shape_of(rows, 3 * width, LOW),
        shape_of(rows, width, LOW),
        shape_of(rows, width, FULL),
    ]
    own = vec is None
    if own:
        outs += [shape_of(32, width, FULL), shape_of(1, inner, FULL), shape_of(width, 128, LOW)]
    return run_kernel(
        partial(attend_forward_kernel, length, images, lines_of, own, experts),
        outs,
        [x] if own else [x, vec],
        11,
        scalars=[place],
        far=pieces,
        scratch=weight_scratch(width, pieces, planes),
    )


def attend_backward_kernel(length, images, lines_of, own, experts, place_ref, up_ref, x_ref, vec_ref, qkv_ref, *refs):
    gain = lines_of[0]
    if own:
        (
            feed_ref, moe_ref, gate_ref, wide_ref, router_ref, near_ref, other_ref,
            din_ref, mine_ref, away_ref, low_mine_ref, low_away_ref, small_ref,
            dol_ref, mix_ref, grad_ref, sums_ref, w_ref, sems,
        ) = refs
    else:
        (
            near_ref, other_ref, din_ref, mine_ref, away_ref, low_mine_ref, low_away_ref, sums_ref,
            dol_ref, mix_ref, grad_ref, w_ref, sems,
        ) = refs
    copies = near_copies(place_ref, near_ref, other_ref, w_ref, sems)
    for copy in copies:
        copy.start()
    rows, width = x_ref.shape
    block = rows // images
    pairs = width // 128
    side = place_ref[1]
    dol_ref[...] = up_ref[...].astype(LOW)
    for copy in copies:
        copy.wait()
    for at in range(width // TILE):
        cols = span(at, TILE)
        mix_ref[:, cols] = mul_turned(dol_ref[...], w_ref[cols, 3 * width : 4 * width]).astype(LOW)

    first, second = head_masks()
    keep = lax.broadcasted_iota(jnp.int32, (block, 1), 0) < length
    for image in range(images):
        for pair in range(pairs):
            lines = span(image, block)
            query = qkv_ref[lines, span(pair, 128)]
            key = qkv_ref[lines, span(pair + pairs, 128)]
            value = qkv_ref[lines, span(pair + 2 * pairs, 128)]
            mix = mix_ref[lines, span(pair, 128)]
            grads = []
            for mask in (first, second):
                scores = mul_turned(key * (0.125 * mask).astype(LOW), query)
                scores = jnp.where(keep, scores, -1e30)
                raised = jnp.exp(scores - jnp.max(scores, axis=0, keepdims=True))
                prob = raised * (1.0 / jnp.sum(raised, axis=0, keepdims=True))
                slope = mul_turned(value * mask.astype(LOW), mix)
                inner = jnp.sum(slope * prob, axis=0, keepdims=True)
                change = (prob * (slope - inner)).astype(LOW)
                grads.append(
                    (turned_mul(change, key), mul(change, query), mul(prob.astype(LOW), mix))
                )
            for part, rate in ((0, 0.125), (1, 0.125), (2, 1.0)):
                both = grads[0][part] * (rate * first) + grads[1][part] * (rate * second)
                grad_ref[lines, span(pair + part * pairs, 128)] = both.astype(LOW)

    for at in range(width // TILE):
        cols = span(at, TILE)
        din_ref[:, cols] = mul_turned(grad_ref[...], w_ref[cols, 0 : 3 * width])

    grad, gain_sum, shift_sum = norm_back(x_ref[...], vec_ref[gain : gain + 1, :], din_ref[...])
    din_ref[...] = up_ref[...] + grad
    sums_ref[0:1, :] = gain_sum
    sums_ref[1:2, :] = shift_sum
    sums_ref[2:3, :] = jnp.sum(grad_ref[:, 0:width].astype(FULL), axis=0, keepdims=True)
    sums_ref[3:4, :] = jnp.sum(
        grad_ref[:, 2 * width : 3 * width].astype(FULL), axis=0, keepdims=True
    )
    sums_ref[4:5, :] = jnp.sum(dol_ref[...].astype(FULL), axis=0, keepdims=True)
    sums_ref[5:8, :] = jnp.zeros((3, width), FULL)
    mine_ref[...] = grad_ref[:, span(side, 3 * width // 2)]
    away_ref[...] = grad_ref[:, span(1 - side, 3 * width // 2)]
    low_mine_ref[...] = dol_ref[:, span(side, width // 2)]
    low_away_ref[...] = dol_ref[:, span(1 - side, width // 2)]
    if not own:
        return
    depth = wide_ref.shape[1] // width
    line = lax.broadcasted_iota(jnp.int32, (8, 128 * depth), 0)
    place = lax.broadcasted_iota(jnp.int32, (8, 128 * depth), 1)
    near = lax.broadcasted_iota(jnp.int32, (128 * depth, 128), 1)
    spot = lax.broadcasted_iota(jnp.int32, (128 * depth, 128), 0)
    collect = jnp.where(spot // depth == near, 1.0, 0.0).astype(LOW)
    pieces = []
    for at in range(width // 128):
        many = jnp.where(place % depth == line, wide_ref[:, span(at, 128 * depth)], 0.0)
        high, rest = split_low(many)
        pieces.append(mul(high, collect) + mul(rest, collect))
    wide_rows = jnp.concatenate(pieces, axis=1)
    order = (
        (sums_ref, 0), (feed_ref, 0), (sums_ref, 1), (feed_ref, 1), (sums_ref, 2), (sums_ref, 3),
        (sums_ref, 4), (feed_ref, 2), (moe_ref, 0), (gate_ref, 0), (moe_ref, 1), (gate_ref, 1),
        (moe_ref, 2), (moe_ref, 3), (moe_ref, 4),
    )
    row = lax.broadcasted_iota(jnp.int32, (128, 1), 0)
    total = jnp.zeros((128, width), FULL)
    for at, (source, spot_line) in enumerate(order):
        total = jnp.where(row == at, source[spot_line : spot_line + 1, :], total)
    for at in range(depth):
        total = jnp.where(row == 15 + experts + at, wide_rows[at : at + 1, :], total)
    small_ref[...] = total.T + router_ref[...]


def attend_backward(place, up, x, vec, qkv, pieces, planes, gain, length, images, experts=0, more=()):
    rows, width = x.shape
    own = len(more) > 0
    return run_kernel(
        partial(attend_backward_kernel, length, images, (gain,), own, experts),
        [
            shape_of(rows, width, FULL),
            shape_of(rows, 3 * width // 2, LOW),
            shape_of(rows, 3 * width // 2, LOW),
            shape_of(rows, width // 2, LOW),
            shape_of(rows, width // 2, LOW),
            shape_of(width, 128, FULL) if own else shape_of(8, width, FULL),
        ],
        [up, x, vec, qkv] + list(more),
        19,
        scalars=[place],
        far=pieces,
        scratch=[
            pltpu.VMEM((rows, width), LOW),
            pltpu.VMEM((rows, width), LOW),
            pltpu.VMEM((rows, 3 * width), LOW),
        ]
        + ([pltpu.VMEM((8, width), FULL)] if own else [])
        + weight_scratch(width, pieces, planes),
    )


def unfold(source, target):
    groups, _, lines, wide = source.shape
    width = target.shape[1]
    fold = wide // width
    for group in range(groups):
        for at in range(fold):
            start = (group * fold + at) * lines
            target[start : start + lines, :] = source[group, 0, :, span(at, width)]


def feed_forward_kernel(
    lines_of, x_ref, vec_ref, bias_ref, in_ref, pack_ref, hn_ref, act_ref, slope_ref, out_ref, out_w_ref
):
    gain, shift, last = lines_of
    step = pl.program_id(0)

    @pl.when(step == 0)
    def _():
        hn_ref[...] = norm_low(
            x_ref[...], vec_ref[gain : gain + 1, :], vec_ref[shift : shift + 1, :]
        )
        out_ref[...] = x_ref[...] + vec_ref[last : last + 1, :]

    unfold(pack_ref, out_w_ref)
    for at in range(act_ref.shape[1] // TILE):
        cols = span(at, TILE)
        weight = in_ref[:, 0, :, cols].reshape(x_ref.shape[1], TILE)
        act, slope = gelu_parts(mul(hn_ref[...], weight) + bias_ref[:, cols])
        act_ref[:, cols] = act
        slope_ref[:, cols] = slope
    for at in range(out_ref.shape[1] // TILE):
        cols = span(at, TILE)
        out_ref[:, cols] += mul(act_ref[...], out_w_ref[:, cols])


def pack_blocks(pack, part, inner):
    groups, _, lines, _ = pack.shape
    return [
        pl.BlockSpec((groups, 1, lines, part), lambda at: (0, 0, 0, at)),
        pl.BlockSpec((part * groups // inner, 1, lines, inner), lambda at: (at, 1, 0, 0)),
    ]


def feed_forward(x, vec, bias, pack, lines_of):
    rows, width = x.shape
    inner = bias.shape[1]
    part = 768
    return run_kernel(
        partial(feed_forward_kernel, lines_of),
        [
            shape_of(rows, width, LOW),
            shape_of(rows, inner, LOW),
            shape_of(rows, inner, LOW),
            shape_of(rows, width, FULL),
        ],
        [x, vec, bias, pack, pack],
        11,
        scratch=[pltpu.VMEM((part, width), LOW)],
        grid=(inner // part,),
        in_blocks=[
            whole((rows, width)),
            whole(vec.shape),
            pl.BlockSpec((1, part), lambda at: (0, at)),
        ]
        + pack_blocks(pack, part, inner),
        out_blocks=[
            whole((rows, width)),
            pl.BlockSpec((rows, part), lambda at: (0, at)),
            pl.BlockSpec((rows, part), lambda at: (0, at)),
            whole((rows, width)),
        ],
    )


def feed_backward_kernel(
    gain, place_ref, up_ref, x_ref, vec_ref, slope_ref, in_ref, pack_ref,
    down_ref, mine_ref, away_ref, low_mine_ref, low_away_ref, sums_ref, bias_ref,
    dml_ref, du_ref, out_w_ref,
):
    step = pl.program_id(0)
    last = pl.num_programs(0) - 1
    width = x_ref.shape[1]
    part_cols = slope_ref.shape[1]

    @pl.when(step == 0)
    def _():
        dml_ref[...] = up_ref[...].astype(LOW)
        down_ref[...] = jnp.zeros(down_ref.shape, FULL)

    unfold(pack_ref, out_w_ref)
    for at in range(part_cols // TILE):
        cols = span(at, TILE)
        part = (
            mul_turned(dml_ref[...], out_w_ref[cols, :]) * slope_ref[:, cols].astype(FULL)
        ).astype(LOW)
        du_ref[step, :, cols] = part
        bias_ref[:, cols] = jnp.sum(part.astype(FULL), axis=0, keepdims=True)
    groups = in_ref.shape[0] // 2
    for at in range(2):
        weight = in_ref[span(at, groups), 0, :, :].reshape(width // 2, part_cols)
        down_ref[:, span(at, width // 2)] += mul_turned(du_ref[step, :, :], weight)

    @pl.when(step == last)
    def _():
        side = place_ref[1]
        grad, gain_sum, shift_sum = norm_back(x_ref[...], vec_ref[gain : gain + 1, :], down_ref[...])
        down_ref[...] = up_ref[...] + grad
        sums_ref[0:1, :] = gain_sum
        sums_ref[1:2, :] = shift_sum
        sums_ref[2:3, :] = jnp.sum(dml_ref[...].astype(FULL), axis=0, keepdims=True)
        sums_ref[3:8, :] = jnp.zeros((5, width), FULL)
        half = du_ref.shape[0] // 2
        for at in range(half):
            mine_ref[:, span(at, part_cols)] = du_ref[side * half + at, :, :]
            away_ref[:, span(at, part_cols)] = du_ref[(1 - side) * half + at, :, :]
        low_mine_ref[...] = dml_ref[:, span(side, width // 2)]
        low_away_ref[...] = dml_ref[:, span(1 - side, width // 2)]


def feed_backward(place, up, x, vec, slope, pack, gain):
    rows, width = x.shape
    inner = slope.shape[1]
    part = 768
    return run_kernel(
        partial(feed_backward_kernel, gain),
        [
            shape_of(rows, width, FULL),
            shape_of(rows, inner // 2, LOW),
            shape_of(rows, inner // 2, LOW),
            shape_of(rows, width // 2, LOW),
            shape_of(rows, width // 2, LOW),
            shape_of(8, width, FULL),
            shape_of(1, inner, FULL),
        ],
        [up, x, vec, slope, pack, pack],
        13,
        scalars=[place],
        scratch=[
            pltpu.VMEM((rows, width), LOW),
            pltpu.VMEM((inner // part, rows, part), LOW),
            pltpu.VMEM((part, width), LOW),
        ],
        grid=(inner // part,),
        in_blocks=[
            whole((rows, width)),
            whole((rows, width)),
            whole(vec.shape),
            pl.BlockSpec((rows, part), lambda at: (0, at)),
        ]
        + pack_blocks(pack, part, inner),
        out_blocks=[
            whole((rows, width)),
            whole((rows, inner // 2)),
            whole((rows, inner // 2)),
            whole((rows, width // 2)),
            whole((rows, width // 2)),
            whole((8, width)),
            pl.BlockSpec((1, part), lambda at: (0, at)),
        ],
    )


def product_kernel(counts, *refs):
    out_ref = refs[-1]
    start = 0
    at_ref = 0
    for count in counts:
        size = refs[at_ref + 1].shape[1]
        total = turned_mul(refs[at_ref][...], refs[at_ref + 1][...])
        for more in range(1, count):
            total += turned_mul(refs[at_ref + 2 * more][...], refs[at_ref + 2 * more + 1][...])
        out_ref[:, start : start + size] = total.astype(LOW)
        start += size
        at_ref += 2 * count
    if at_ref < len(refs) - 1:
        extra = refs[at_ref]
        out_ref[:, start : start + extra.shape[1]] = extra[...].astype(LOW)


def products(groups, extra=None, part=256):
    counts = [len(group) for group in groups]
    arrays = [array for group in groups for pair in group for array in pair]
    blocks = []
    for group in groups:
        for left, right in group:
            blocks += [pl.BlockSpec((left.shape[0], part), lambda at: (0, at)), whole(right.shape)]
    cols = sum(group[0][1].shape[1] for group in groups)
    if extra is not None:
        arrays.append(extra)
        blocks.append(pl.BlockSpec((part, extra.shape[1]), lambda at: (at, 0)))
        cols += extra.shape[1]
    lines = groups[0][0][0].shape[1]
    return run_kernel(
        partial(product_kernel, counts),
        [shape_of(lines, cols, LOW)],
        arrays,
        7,
        grid=(lines // part,),
        in_blocks=blocks,
        out_blocks=[pl.BlockSpec((part, cols), lambda at: (at, 0))],
    )[0]


def one_hot_rows(target, slots):
    hit = lax.broadcasted_iota(jnp.int32, (slots, target.shape[1]), 0) == target
    return jnp.where(hit, 1.0, 0.0).astype(LOW)


def one_hot_cols(target, slots):
    hit = lax.broadcasted_iota(jnp.int32, (target.shape[0], slots), 1) == target
    return jnp.where(hit, 1.0, 0.0).astype(LOW)


def slot_lanes(expert, slots, capacity):
    line = lax.broadcasted_iota(jnp.int32, (slots, 128), 0)
    lane = lax.broadcasted_iota(jnp.int32, (slots, 128), 1)
    return jnp.where((line == lane + expert * capacity) & (lane < capacity), 1.0, 0.0).astype(LOW)


def dispatch_kernel(
    experts, lines_of, x_ref, vec_ref, router_ref, route_ref, target_ref,
    mn_ref, gate_ref, pick_ref, out_ref, spot_ref,
):
    gain, shift = lines_of
    slots = out_ref.shape[0]
    capacity = slots // experts
    mn_ref[...] = norm_low(x_ref[...], vec_ref[gain : gain + 1, :], vec_ref[shift : shift + 1, :])
    logits = mul(mn_ref[...], router_ref[...])
    lane = lax.broadcasted_iota(jnp.int32, logits.shape, 1)
    logits = jnp.where(lane < experts, logits, -1e30)
    raised = jnp.exp(logits - jnp.max(logits, axis=-1, keepdims=True))
    gate = raised / jnp.sum(raised, axis=-1, keepdims=True)
    gate_ref[...] = gate
    picks = [
        jnp.sum(jnp.where(lane == route_ref[:, k : k + 1], gate, 0.0), axis=-1, keepdims=True)
        for k in range(2)
    ]
    pick = jnp.where(lane == 0, picks[0], jnp.where(lane == 1, picks[1], 0.0))
    pick_ref[...] = pick
    turned = pick.T
    for k in range(2):
        spot_ref[k, :, :] = one_hot_rows(target_ref[k : k + 1, :], slots)
    for at in range(out_ref.shape[1] // TILE):
        cols = span(at, TILE)
        out_ref[:, cols] = mul(spot_ref[0, :, :] + spot_ref[1, :, :], mn_ref[:, cols]).astype(LOW)
    row = lax.broadcasted_iota(jnp.int32, (16, 1), 0)
    weights = jnp.zeros((16, slots), FULL)
    for k in range(2):
        high, rest = split_low(turned[k : k + 1, :])
        both = jnp.where(row == 14, high.astype(FULL), jnp.where(row == 15, rest.astype(FULL), 0.0))
        weights += mul_turned(both.astype(LOW), spot_ref[k, :, :])
    weights = weights.astype(LOW)
    for expert in range(experts):
        lines = slice((expert + 1) * capacity - 16, (expert + 1) * capacity)
        chosen = mul(weights, slot_lanes(expert, slots, capacity))
        out_ref[lines, 0:128] = jnp.where(
            row >= 14, chosen, out_ref[lines, 0:128].astype(FULL)
        ).astype(LOW)


def dispatch(x, vec, router, routes, targets, experts, slots, lines_of):
    rows, width = x.shape
    return run_kernel(
        partial(dispatch_kernel, experts, lines_of),
        [
            shape_of(rows, width, LOW),
            shape_of(rows, 128, FULL),
            shape_of(rows, 128, FULL),
            shape_of(slots, width, LOW),
        ],
        [x, vec, router, routes, targets],
        6,
        scratch=[pltpu.VMEM((2, slots, rows), LOW)],
    )


def restore(place_ref, source, target):
    planes, lines, _ = target.shape
    for mask in range(planes):
        target[place_ref[0] ^ mask, :, :] = source[mask * lines : (mask + 1) * lines, :]


def unfold_lines(place_ref, source, target, lines):
    width = target.shape[1]
    fold = source.shape[1] // width
    many = source.shape[0] // lines
    for mask in range(many):
        group = mask ^ (place_ref[0] % many)
        for at in range(fold):
            start = pl.multiple_of((group * fold + at) * lines, lines)
            target[pl.ds(start, lines), :] = source[
                mask * lines : (mask + 1) * lines, span(at, width)
            ]


def hidden_kernel(
    experts, place_ref, x_ref, bias_ref, pack_ref, up_ref, act_ref, slope_ref, dy_ref, last_ref, w_ref
):
    restore(place_ref, pack_ref, w_ref)

    @pl.when(pl.program_id(0) == 0)
    def _():
        capacity = x_ref.shape[0] // experts
        row = lax.broadcasted_iota(jnp.int32, (128, 1), 0)
        table = jnp.zeros((128, 128), FULL)
        for group in range(experts):
            mark = x_ref[(group + 1) * capacity - 16 : (group + 1) * capacity, 0:128].astype(FULL)
            table = jnp.where(row == group, mark[14:15, :] + mark[15:16, :], table)
        table = table.T
        total = jnp.zeros(last_ref.shape, FULL)
        for group in range(experts):
            spots = slice(group * capacity, (group + 1) * capacity)
            part = (table[0:capacity, group : group + 1] * up_ref[spots, :].astype(FULL)).astype(LOW)
            dy_ref[spots, :] = part
            total += jnp.sum(part.astype(FULL), axis=0, keepdims=True)
        last_ref[...] = total

    for at in range(act_ref.shape[1] // TILE):
        cols = span(at, TILE)
        weight = w_ref[:, :, cols].reshape(x_ref.shape[1], TILE)
        act, slope = gelu_parts(mul(x_ref[...], weight) + bias_ref[:, cols])
        act_ref[:, cols] = act
        slope_ref[:, cols] = slope


def hidden_forward(place, x, bias, weight, up, planes, experts):
    rows, width = x.shape
    inner = bias.shape[1]
    part = 768
    return run_kernel(
        partial(hidden_kernel, experts),
        [
            shape_of(rows, inner, LOW),
            shape_of(rows, inner, LOW),
            shape_of(rows, width, LOW),
            shape_of(1, width, FULL),
        ],
        [x, bias, weight, up],
        11,
        scalars=[place],
        scratch=[pltpu.VMEM((planes, width // planes, part), LOW)],
        grid=(inner // part,),
        in_blocks=[
            whole(x.shape),
            pl.BlockSpec((1, part), lambda at: (0, at)),
            pl.BlockSpec((width, part), lambda at: (0, at)),
            whole(up.shape),
        ],
        out_blocks=[pl.BlockSpec((rows, part), lambda at: (0, at))] * 2
        + [whole((rows, width)), whole((1, width))],
    )


def expert_out_kernel(
    lines, experts, place_ref, act_ref, bias_ref, pack_ref, up_ref, out_ref, dot_ref, sum_ref, w_ref
):
    step = pl.program_id(0)
    unfold_lines(place_ref, pack_ref, w_ref, lines)

    @pl.when(step == 0)
    def _():
        sum_ref[...] = jnp.zeros(sum_ref.shape, FULL) + bias_ref[...]

    for at in range(w_ref.shape[1] // TILE):
        cols = span(at, TILE)
        sum_ref[:, cols] += mul(act_ref[...], w_ref[:, cols])

    @pl.when(step == pl.num_programs(0) - 1)
    def _():
        result = sum_ref[...].astype(LOW)
        out_ref[...] = result
        dots = jnp.sum(result.astype(FULL) * up_ref[...].astype(FULL), axis=-1, keepdims=True)
        capacity = result.shape[0] // experts
        lane = lax.broadcasted_iota(jnp.int32, (capacity, 128), 1)
        table = jnp.zeros((capacity, 128), FULL)
        for group in range(experts):
            table = jnp.where(lane == group, dots[group * capacity : (group + 1) * capacity], table)
        if capacity < 128:
            table = jnp.concatenate([table, jnp.zeros((128 - capacity, 128), FULL)], axis=0)
        table = table.T
        row = lax.broadcasted_iota(jnp.int32, (16, 1), 0)
        for group in range(experts):
            high, rest = split_low(table[group : group + 1, :])
            both = jnp.where(
                row == 14, high.astype(FULL), jnp.where(row == 15, rest.astype(FULL), 0.0)
            )
            dot_ref[group * 16 : (group + 1) * 16, :] = both.astype(LOW)


def expert_out_forward(place, act, bias, weight, up, lines, experts):
    rows, width = act.shape[0], weight.shape[1]
    inner = act.shape[1]
    part = 768
    many = part // lines
    return run_kernel(
        partial(expert_out_kernel, lines, experts),
        [shape_of(rows, width, LOW), shape_of(experts * 16, 128, LOW)],
        [act, bias, weight, up],
        9,
        scalars=[place],
        scratch=[pltpu.VMEM((rows, width), FULL), pltpu.VMEM((part, width), LOW)],
        grid=(inner // part,),
        in_blocks=[
            pl.BlockSpec((rows, part), lambda at, place: (0, at ^ (place[0] // many))),
            pl.BlockSpec(bias.shape, lambda at, place: (0, 0)),
            pl.BlockSpec((part, width), lambda at, place: (at, 0)),
            pl.BlockSpec(up.shape, lambda at, place: (0, 0)),
        ],
        out_blocks=[
            pl.BlockSpec((rows, width), lambda at, place: (0, 0)),
            pl.BlockSpec((experts * 16, 128), lambda at, place: (0, 0)),
        ],
        ahead=True,
    )


def expert_backward_kernel(
    lines, experts, place_ref, dy_ref, slope_ref, pack_ref, in_ref, dot_ref,
    dh_ref, bias_ref, back_ref, sum_ref, out_w_ref, in_w_ref,
):
    step = pl.program_id(0)
    rows = dy_ref.shape[0]
    capacity = rows // experts
    unfold_lines(place_ref, pack_ref, out_w_ref, lines)
    restore(place_ref, in_ref, in_w_ref)

    @pl.when(step == 0)
    def _():
        sum_ref[...] = jnp.zeros(sum_ref.shape, FULL)

    for at in range(slope_ref.shape[1] // TILE):
        cols = span(at, TILE)
        part = (
            mul_turned(dy_ref[...], out_w_ref[cols, :]) * slope_ref[:, cols].astype(FULL)
        ).astype(LOW)
        dh_ref[:, cols] = part
        bias_ref[:, cols] = jnp.sum(part.astype(FULL), axis=0, keepdims=True)
    planes, tall, part_cols = in_w_ref.shape
    for at in range(2):
        weight = in_w_ref[span(at, planes // 2), :, :].reshape(planes * tall // 2, part_cols)
        sum_ref[:, span(at, planes * tall // 2)] += mul_turned(dh_ref[...], weight)

    @pl.when(step == pl.num_programs(0) - 1)
    def _():
        back_ref[...] = sum_ref[...].astype(LOW)
        row = lax.broadcasted_iota(jnp.int32, (16, 1), 0)
        for group in range(experts):
            spots = slice((group + 1) * capacity - 16, (group + 1) * capacity)
            back_ref[spots, 0:128] = jnp.where(
                row >= 14,
                dot_ref[group * 16 : (group + 1) * 16, :].astype(FULL),
                sum_ref[spots, 0:128],
            ).astype(LOW)


def expert_backward(place, dy, slope, w_out, w_in, dots, lines, experts):
    rows, width = dy.shape
    inner = slope.shape[1]
    planes = inner // lines
    part = 768
    many = part // lines

    def moved(at, place):
        return (0, at ^ (place[0] // many))

    def fixed(at, place):
        return (0, 0)

    return run_kernel(
        partial(expert_backward_kernel, lines, experts),
        [
            shape_of(rows, inner, LOW),
            shape_of(1, inner, FULL),
            shape_of(rows, width, LOW),
        ],
        [dy, slope, w_out, w_in, dots],
        15,
        scalars=[place],
        scratch=[
            pltpu.VMEM((rows, width), FULL),
            pltpu.VMEM((part, width), LOW),
            pltpu.VMEM((planes, width // planes, part), LOW),
        ],
        grid=(inner // part,),
        in_blocks=[
            pl.BlockSpec((rows, width), fixed),
            pl.BlockSpec((rows, part), moved),
            pl.BlockSpec((part, width), lambda at, place: (at, 0)),
            pl.BlockSpec((width, part), moved),
            pl.BlockSpec(dots.shape, fixed),
        ],
        out_blocks=[
            pl.BlockSpec((rows, part), moved),
            pl.BlockSpec((1, part), moved),
            pl.BlockSpec((rows, width), fixed),
        ],
        ahead=True,
    )


def output_kernel(x_ref, home_ref, pick_ref, target_ref, live_ref, out_ref, spot_ref):
    slots = home_ref.shape[0]
    for k in range(2):
        spot_ref[k, :, :] = one_hot_cols(target_ref[:, k : k + 1], slots)
    for at in range(x_ref.shape[1] // TILE):
        cols = span(at, TILE)
        total = x_ref[:, cols]
        for k in range(2):
            total += pick_ref[:, k : k + 1] * mul(spot_ref[k, :, :], home_ref[:, cols])
        out_ref[:, cols] = (total * live_ref[...]).astype(LOW)


def output_rows(x, home, pick, targets, live):
    rows, width = x.shape
    return run_kernel(
        output_kernel,
        [shape_of(rows, width, LOW)],
        [x, home, pick, targets, live],
        7,
        scratch=[pltpu.VMEM((2, rows, home.shape[0]), LOW)],
    )[0]


def return_kernel(
    gain, experts, x_ref, vec_ref, home_ref, gate_ref, route_ref, target_ref, up_ref, mn_ref,
    router_ref, out_ref, sums_ref, router_grad_ref, spot_ref,
):
    rows, width = x_ref.shape
    slots = home_ref.shape[0]
    capacity = slots // experts
    for k in range(2):
        spot_ref[k, :, :] = one_hot_cols(target_ref[:, k : k + 1], slots)
    line = jnp.zeros((16, slots), FULL)
    for expert in range(experts):
        marks = home_ref[(expert + 1) * capacity - 16 : (expert + 1) * capacity, 0:128]
        line += mul_turned(marks, slot_lanes(expert, slots, capacity))
    line = line.astype(LOW)
    lane = lax.broadcasted_iota(jnp.int32, (rows, 128), 1)
    gate = gate_ref[...]
    spread = jnp.zeros((rows, 128), FULL)
    for k in range(2):
        dots = mul_turned(spot_ref[k, :, :], line)
        spread += jnp.where(lane == route_ref[:, k : k + 1], dots[:, 14:15] + dots[:, 15:16], 0.0)
    logit = gate * (spread - jnp.sum(gate * spread, axis=-1, keepdims=True))
    high, rest = split_low(pltpu.roll(logit, 15, 1))
    router_grad_ref[...] = turned_mul(mn_ref[...], high) + turned_mul(mn_ref[...], rest)
    high, rest = split_low(logit)
    for at in range(width // TILE):
        cols = span(at, TILE)
        out_ref[:, cols] = (
            mul_turned(high, router_ref[cols, :])
            + mul_turned(rest, router_ref[cols, :])
            + mul(spot_ref[0, :, :] + spot_ref[1, :, :], home_ref[:, cols])
        )

    grad, gain_sum, shift_sum = norm_back(x_ref[...], vec_ref[gain : gain + 1, :], out_ref[...])
    out_ref[...] = up_ref[...].astype(FULL) + grad
    sums_ref[0:1, :] = gain_sum
    sums_ref[1:2, :] = shift_sum
    sums_ref[2:8, :] = jnp.zeros((6, width), FULL)


def return_grad(x, vec, home, gate, routes, targets, up, mn, router, gain, experts, after):
    rows, width = x.shape
    slots = home.shape[0]
    return run_kernel(
        partial(return_kernel, gain, experts),
        [shape_of(rows, width, FULL), shape_of(8, width, FULL), shape_of(width, 128, FULL)],
        [x, vec, home, gate, routes, targets, up, mn, router],
        7,
        far=after,
        scratch=[pltpu.VMEM((2, rows, slots), LOW)],
    )


def feed_products_kernel(lines, fold, hn_ref, hn_far_ref, du_ref, du_far_ref, act_ref, act_far_ref, low_ref, low_far_ref, out_ref):
    cols = du_ref.shape[1] // fold
    tall = 2 * fold * lines
    tile = hn_ref.shape[1]
    for at in range(fold):
        part = turned_mul(hn_ref[...], du_ref[:, span(at, cols)])
        part += turned_mul(hn_far_ref[...], du_far_ref[:, span(at, cols)])
        part = part.astype(LOW)
        for spot in range(tile // lines):
            start = spot * tall + at * lines
            out_ref[start : start + lines, :] = part[spot * lines : (spot + 1) * lines, :]
    for at in range(act_ref.shape[1] // tile):
        part = turned_mul(act_ref[:, span(at, tile)], low_ref[...])
        part += turned_mul(act_far_ref[:, span(at, tile)], low_far_ref[...])
        part = part.astype(LOW)
        size = fold * lines
        for spot in range(tile // size):
            start = (at * (tile // size) + spot) * tall + size
            out_ref[start : start + size, :] = part[spot * size : (spot + 1) * size, :]


def feed_products(hn, hn_far, du, du_far, act, act_far, low, low_far, blocks, fold):
    rows, width = hn.shape
    lines = width // blocks
    tall = 2 * fold * lines
    steps = 2
    left = pl.BlockSpec((rows, width // steps), lambda at: (0, at))
    wide = pl.BlockSpec((rows, fold * width // steps), lambda at: (0, at))
    return run_kernel(
        partial(feed_products_kernel, lines, fold),
        [shape_of(blocks * tall, low.shape[1], LOW)],
        [hn, hn_far, du, du_far, act, act_far, low, low_far],
        11,
        grid=(steps,),
        in_blocks=[left, left, whole(du.shape), whole(du.shape), wide, wide, whole(low.shape), whole(low.shape)],
        out_blocks=[pl.BlockSpec((blocks * tall // steps, low.shape[1]), lambda at: (at, 0))],
    )[0]


def expert_products_kernel(lines, x_ref, dh_ref, in_bias_ref, out_bias_ref, out_ref):
    width = out_bias_ref.shape[1]
    planes = width // lines
    tall = lines + 16
    step = pl.program_id(0)
    row = lax.broadcasted_iota(jnp.int32, (16, 1), 0)
    last = jnp.where(step == 0, 1.0, 0.0) * out_bias_ref[...]
    both = jnp.where(row == 0, in_bias_ref[...], jnp.where(row == 1, last, 0.0)).astype(LOW)
    many = max(1, 384 // lines)
    for at in range(planes // many):
        part = turned_mul(x_ref[:, span(at, many * lines)], dh_ref[...]).astype(LOW)
        for spot in range(many):
            start = (at * many + spot) * tall
            out_ref[start : start + lines, :] = part[spot * lines : (spot + 1) * lines, :]
            out_ref[start + lines : start + tall, :] = both


def expert_products(x, dh, in_bias, out_bias, planes):
    slots, width = x.shape
    inner = dh.shape[1]
    lines = width + 16 * planes
    return run_kernel(
        partial(expert_products_kernel, width // planes),
        [shape_of(lines, inner, LOW)],
        [x, dh, in_bias, out_bias],
        8,
        grid=(inner // width,),
        in_blocks=[
            whole(x.shape),
            pl.BlockSpec((slots, width), lambda at: (0, at)),
            pl.BlockSpec((1, width), lambda at: (0, at)),
            whole(out_bias.shape),
        ],
        out_blocks=[pl.BlockSpec((lines, width), lambda at: (0, at))],
    )[0]


def spread_kernel(target_ref, up_ref, out_ref, spot_ref):
    slots = out_ref.shape[0]
    spot_ref[...] = one_hot_rows(target_ref[0:1, :], slots) + one_hot_rows(target_ref[1:2, :], slots)
    for at in range(out_ref.shape[1] // TILE):
        cols = span(at, TILE)
        out_ref[:, cols] = mul(spot_ref[...], up_ref[:, cols]).astype(LOW)


def spread_up(targets, up, slots):
    rows, width = up.shape
    return run_kernel(
        spread_kernel,
        [shape_of(slots, width, LOW)],
        [targets, up],
        4,
        scratch=[pltpu.VMEM((slots, rows), LOW)],
    )[0]


tie = lax.optimization_barrier


def trade(value, axis_name, mask):
    count = lax.axis_size(axis_name)
    return lax.ppermute(value, axis_name, [(place, place ^ mask) for place in range(count)])


def in_order(pieces, place):
    level = 0
    while len(pieces) > 1:
        flip = ((place >> level) & 1) == 1
        pieces = [
            jnp.where(
                flip,
                jnp.concatenate([pieces[at + 1], pieces[at]], axis=0),
                jnp.concatenate([pieces[at], pieces[at + 1]], axis=0),
            )
            for at in range(0, len(pieces), 2)
        ]
        level += 1
    return pieces[0]


def core_side():
    return lax.axis_index("expert") % 2


def core_half(shard):
    side = core_side()
    half = shard.shape[1] // 2
    mine = lax.dynamic_slice_in_dim(shard, side * half, half, 1)
    away = lax.dynamic_slice_in_dim(shard, (1 - side) * half, half, 1)
    return in_order([mine, trade(away, "expert", 1)], side)


def layer_gather(shard):
    layers = lax.axis_size("expert") // 2
    stacked = [shard] + [trade(shard, "expert", 2 * mask) for mask in range(1, layers)]
    return in_order(stacked, lax.axis_index("expert") // 2)


def plane_near(piece):
    count = lax.axis_size("fsdp")
    masks = (1, 2) if count == 4 else range(1, count)
    return [trade(piece, "fsdp", mask) for mask in masks]


def plane_far(near):
    if lax.axis_size("fsdp") != 4:
        return []
    half = near[0].shape[0] // 2
    return [trade(near[1][:half], "fsdp", 1), trade(near[0][half:], "fsdp", 2)]


def both_cores(own, near, far):
    held = jnp.concatenate([own] + near + far, axis=0)
    return held, trade(held, "expert", 1)


def sum_first(blocks):
    count = lax.axis_size("fsdp")
    place = lax.axis_index("fsdp")
    parts = [
        lax.dynamic_index_in_dim(blocks, place ^ mask, 0, keepdims=False) for mask in range(count)
    ]
    if count != 4:
        return parts, []
    half = blocks.shape[1] // 2
    return parts[:3], [
        trade(parts[3][:half], "fsdp", 1),
        trade(parts[3][half:], "fsdp", 2),
    ]


def added(left, right):
    return (left.astype(FULL) + right.astype(FULL)).astype(LOW)


def sum_second(parts, got):
    if not got:
        return [trade(part, "fsdp", mask) for mask, part in enumerate(parts) if mask > 0]
    half = parts[1].shape[0] // 2
    send_x = jnp.concatenate([parts[1][:half], added(parts[1][half:], got[1])], axis=0)
    send_y = jnp.concatenate([added(parts[2][:half], got[0]), parts[2][half:]], axis=0)
    return [trade(send_x, "fsdp", 1), trade(send_y, "fsdp", 2)]


def sum_total(own, arrived):
    total = own.astype(FULL)
    for term in arrived:
        total = total + term.astype(FULL)
    return total


def layer_first(held):
    layer = lax.axis_index("expert") // 2
    layers = lax.axis_size("expert") // 2
    parts = [
        lax.dynamic_index_in_dim(held, layer ^ mask, 0, keepdims=False) for mask in range(layers)
    ]
    return parts[0], [trade(parts[mask], "expert", 2 * mask) for mask in range(1, layers)]


def core_last(total):
    side = core_side()
    rows = total.shape[0] // 2
    mine = lax.dynamic_slice_in_dim(total, side * rows, rows, 0)
    away = lax.dynamic_slice_in_dim(total, (1 - side) * rows, rows, 0).astype(LOW)
    came = trade(away, "expert", 1).astype(FULL)
    return jnp.where(side == 0, mine, came), jnp.where(side == 0, came, mine)


def feed_half(fc_in, fc_out):
    side = core_side()
    lines, inner = fc_in.shape
    fold = inner // fc_out.shape[1]
    blocks = [fc_out[at * lines : (at + 1) * lines] for at in range(fold)]
    folded = jnp.concatenate(blocks, axis=1)
    came = trade(jnp.where(side == 0, folded, fc_in), "expert", 1)
    width = fc_out.shape[1]
    rows_came = [came[:, at * width : (at + 1) * width] for at in range(fold)]
    stacked = [
        jnp.concatenate([group[at], group[at + 1]], axis=0)
        for group in (rows_came, blocks)
        for at in range(0, fold, 2)
    ]
    return jnp.where(
        side == 0, jnp.concatenate([fc_in, came], axis=0), jnp.concatenate(stacked, axis=1)
    )


def feed_last(total, fold):
    side = core_side()
    cols = total.shape[1]
    size = total.shape[0] // 2
    inside = total[:size].reshape(fold, 2, -1, cols)
    outside = total[size:].reshape(2, -1, cols)

    def part(core):
        return jnp.concatenate(
            [
                lax.dynamic_index_in_dim(inside, core, 1, keepdims=False).reshape(-1, cols),
                lax.dynamic_index_in_dim(outside, core, 0, keepdims=False),
            ],
            axis=0,
        )

    mine = part(side)
    came = trade(part(1 - side).astype(LOW), "expert", 1).astype(FULL)
    return jnp.where(side == 0, mine, came), jnp.where(side == 0, came, mine)


def in_blocks(half_grad):
    planes = lax.axis_size("fsdp")
    layers = lax.axis_size("expert") // 2
    return half_grad.reshape(planes, layers, -1, half_grad.shape[-1])


def per_device(
    patches,
    dense_gains,
    dense_shifts,
    dense_qkv,
    dense_proj,
    dense_fc_in,
    dense_fc_bias,
    dense_fc_out,
    moe_gains,
    moe_shifts,
    moe_qkv,
    moe_proj,
    router,
    expert_in,
    expert_in_bias,
    expert_out,
    expert_out_bias,
    routes,
    slot_pos,
    image_counts,
    cotangent,
):
    images, length, width = patches.shape
    shard_rows = dense_qkv.shape[0]
    inner = dense_fc_in.shape[1]
    local_experts = expert_in.shape[0]
    experts = local_experts * lax.axis_size("expert")
    planes = lax.axis_size("fsdp")
    plane = lax.axis_index("fsdp")
    place = jnp.stack([plane, core_side()]).astype(jnp.int32)
    block = fit(length, 16)
    rows = images * block
    lowest = (images + 1) // 2
    capacity = fit(5 * (images + lowest) * length // (4 * experts) + 4, 16)
    slots = experts * capacity

    def padded(array, fill=0):
        return jnp.pad(
            array, ((0, 0), (0, block - length), (0, 0)), constant_values=fill
        ).reshape(rows, array.shape[-1])

    def trimmed(array):
        return array.reshape(images, block, array.shape[-1])[:, :length]

    def far(array):
        return trade(array, "expert", 1)

    layers = lax.axis_size("expert") // 2
    fold = inner // width
    small_rows = jnp.concatenate(
        [
            dense_gains.T,
            dense_shifts.T,
            moe_gains.T,
            moe_shifts.T,
            router,
            dense_fc_bias.reshape(shard_rows, -1),
        ],
        axis=1,
    )
    small_cols = small_rows.shape[1]
    small_rows = jnp.pad(small_rows, ((0, 0), (0, 256 - small_cols)))
    first_half = core_half(jnp.concatenate([dense_qkv, dense_proj, small_rows], axis=1))
    moe_half = core_half(jnp.concatenate([moe_qkv, moe_proj], axis=1))
    if (2 * shard_rows) % 16 == 0:
        later = feed_half(dense_fc_in, dense_fc_out)
        pack = lax.all_gather(later, ("fsdp", "expert"), axis=0, tiled=True)
        pack = pack.reshape(planes * layers, 2, 2 * shard_rows, later.shape[1])
    else:
        groups = width // 48
        whole_in = lax.all_gather(dense_fc_in, ("fsdp", "expert"), axis=0, tiled=True)
        whole_out = lax.all_gather(dense_fc_out, ("fsdp", "expert"), axis=0, tiled=True)
        folded = whole_out.reshape(groups, fold, 48, width).swapaxes(1, 2).reshape(groups, 48, inner)
        pack = jnp.stack([whole_in.reshape(groups, 48, inner), folded], axis=1)
    dense_own = layer_gather(first_half)
    expert_bias = jnp.concatenate([expert_in_bias[0], expert_out_bias[0]])
    other_bias = [trade(expert_bias, "fsdp", mask) for mask in range(1, planes)]
    dense_own, other_bias = tie((dense_own, other_bias))
    expert_bias = in_order([part[None] for part in [expert_bias] + other_bias], plane).astype(FULL)
    dense_own, moe_half = tie((dense_own, moe_half))
    dense_near = plane_near(dense_own)
    moe_own = layer_gather(moe_half)
    dense_near, moe_own = tie((dense_near, moe_own))
    dense_far = plane_far(dense_near)
    moe_near = plane_near(moe_own)
    dense_pieces = both_cores(dense_own, dense_near, dense_far)

    live_images = jnp.arange(images) < image_counts[0]
    live_rows = jnp.repeat(live_images, block).astype(FULL)[:, None]
    up = padded(jnp.where(live_images[:, None, None], cotangent, jnp.zeros_like(cotangent)))
    route_cols = padded(routes)
    target_cols = padded(jnp.where(slot_pos >= 0, routes * capacity + slot_pos, -1), -1)
    target_rows = target_cols.T

    def exchange(array):
        return lax.all_to_all(
            array.reshape(experts, capacity, width), "expert", split_axis=0, concat_axis=0, tiled=True
        ).reshape(slots, width)

    x0, up_spread = tie((padded(patches).astype(FULL), spread_up(target_rows, up, slots)))
    up_slots = exchange(up_spread)
    an, qkv, mixed, x1, vec, fc_bias, router_full = attend_forward(
        place, x0, None, dense_pieces, planes, (0, 2, 4, 5, 6), length, images, experts, inner
    )
    x1, moe_near, in_own, out_own = tie((x1, moe_near, expert_in[0], expert_out[0]))
    moe_pieces = both_cores(moe_own, moe_near, plane_far(moe_near))
    in_near = plane_near(in_own)
    out_near = plane_near(out_own)
    hidden_part = expert_in_bias.shape[1]
    in_bias = expert_bias[:, :hidden_part].reshape(1, -1)
    out_bias = expert_bias[:, hidden_part:].reshape(1, -1)

    hn, act, slope, x2 = feed_forward(x1, vec, fc_bias, pack, (1, 3, 7))
    an2, qkv2, mixed2, x3 = attend_forward(
        place, x2, vec, moe_pieces, planes, (8, 10, 12, 13, 14), length, images, experts, inner
    )
    x3, up_slots = tie((x3, up_slots))
    in_far = plane_far(in_near)
    out_far = plane_far(out_near)
    w_in = jnp.concatenate([in_own] + in_near + in_far, axis=0)
    w_out = jnp.concatenate([out_own] + out_near + out_far, axis=0)
    mn, gate, pick, outgoing = dispatch(
        x3, vec, router_full, route_cols, target_rows, experts, slots, (9, 11)
    )
    arrived = exchange(outgoing)
    e_act, e_slope, dy, out_bias_grad = hidden_forward(
        place, arrived, in_bias, w_in, up_slots, planes, experts
    )
    e_act, w_out = tie((e_act, w_out))
    out_grad = products([[(e_act, dy)]], part=768)
    out_grad, e_act = tie((out_grad, e_act))
    expert_out_sum = lax.psum_scatter(out_grad, "fsdp", scatter_dimension=0, tiled=True)
    hidden_rows = inner // planes
    result, dots = expert_out_forward(
        place, e_act, out_bias, w_out, up_slots, hidden_rows, experts
    )
    dh, in_bias_grad, back = expert_backward(
        place, dy, e_slope, w_out, w_in, dots, hidden_rows, experts
    )
    back = exchange(back)
    expert_grad = expert_products(arrived, dh, in_bias_grad, out_bias_grad, planes)
    lefts = [far(array) for array in (hn, act, an, mixed, an2, mixed2)]
    expert_grad, back, result, expert_out_sum, lefts = tie(
        (expert_grad, back, result, expert_out_sum, lefts)
    )
    hn_far, act_far, an_far, mixed_far, an2_far, mixed2_far = lefts
    expert_sum = lax.psum_scatter(expert_grad, "fsdp", scatter_dimension=0, tiled=True)
    home = exchange(result)
    dx3, gate_sums, router_grad = return_grad(
        x3, vec, back, gate, route_cols, target_cols, up, mn, router_full, 9, experts, []
    )
    dx2, mine2, away2, low_mine2, low_away2, moe_sums = attend_backward(
        place, dx3, x2, vec, qkv2, moe_pieces, planes, 8, length, images
    )
    dx1, mine1, away1, low_mine1, low_away1, feed_sums, fc_bias_grad = feed_backward(
        place, dx2, x1, vec, slope, pack, 1
    )
    away2, low_away2, away1, low_away1, dx1 = tie(
        (far(away2), far(low_away2), far(away1), far(low_away1), dx1)
    )
    moe_grad = products(
        [
            [(an2, mine2), (an2_far, away2)],
            [(mixed2, low_mine2), (mixed2_far, low_away2)],
        ]
    )
    moe_parts, moe_got = sum_first(in_blocks(moe_grad))
    if (2 * shard_rows) % 16 == 0:
        feed_grad = feed_products(
            hn, hn_far, mine1, away1, act, act_far, low_mine1, low_away1,
            planes * layers, fold,
        )
    else:
        in_part = products([[(hn, mine1), (hn_far, away1)]])
        out_part = products([[(act, low_mine1), (act_far, low_away1)]], part=768)
        in_part = in_blocks(in_part)
        in_part = in_part.reshape(in_part.shape[:3] + (fold, -1)).swapaxes(2, 3)
        in_part = in_part.reshape(planes, layers, -1, in_part.shape[-1])
        feed_grad = jnp.concatenate([in_part, in_blocks(out_part)], axis=2)
        feed_grad = feed_grad.reshape(-1, feed_grad.shape[-1])
    feed_grad, dx1, moe_got = tie((feed_grad, dx1, moe_got))
    feed_parts, feed_got = sum_first(in_blocks(feed_grad))
    moe_came = sum_second(moe_parts, moe_got)
    dx0, mine0, away0, low_mine0, low_away0, vectors = attend_backward(
        place, dx1, x0, vec, qkv, dense_pieces, planes, 0, length, images, experts,
        [feed_sums, moe_sums, gate_sums, fc_bias_grad, router_grad],
    )
    feed_got, mine0, expert_sum, moe_came = tie((feed_got, mine0, expert_sum, moe_came))
    feed_came = sum_second(feed_parts, feed_got)
    moe_mine, moe_layers = layer_first(sum_total(moe_parts[0], moe_came).astype(LOW))
    dense_grad = products(
        [
            [(an, mine0), (an_far, far(away0))],
            [(mixed, low_mine0), (mixed_far, far(low_away0))],
        ],
        vectors,
    )
    dense_parts, dense_got = sum_first(in_blocks(dense_grad))
    dense_got, home, dx0, feed_came, moe_layers, expert_sum, expert_out_sum = tie(
        (dense_got, home, dx0, feed_came, moe_layers, expert_sum, expert_out_sum)
    )
    dense_came = sum_second(dense_parts, dense_got)
    feed_mine, feed_layers = layer_first(sum_total(feed_parts[0], feed_came).astype(LOW))
    output = output_rows(x3, home, pick, target_cols, live_rows)
    moe_left, moe_right = core_last(sum_total(moe_mine, moe_layers))
    dense_came, feed_layers, output = tie((dense_came, feed_layers, output))
    dense_mine, dense_layers = layer_first(sum_total(dense_parts[0], dense_came).astype(LOW))
    feed_left, feed_right = feed_last(sum_total(feed_mine, feed_layers), fold)
    dense_left, dense_right = core_last(sum_total(dense_mine, dense_layers))
    third = 3 * width // 2

    def split(left, right):
        return (
            jnp.concatenate([left[:, :third], right[:, :third]], axis=1),
            jnp.concatenate([left[:, third : 2 * width], right[:, third : 2 * width]], axis=1),
        )

    dense_qkv_sum, dense_proj_sum = split(dense_left, dense_right)
    moe_qkv_sum, moe_proj_sum = split(moe_left, moe_right)
    small_sum = dense_left[:, 2 * width :] + dense_right[:, 2 * width :]
    feed_in_sum = jnp.concatenate(
        [
            half[at * shard_rows : (at + 1) * shard_rows]
            for half in (feed_left, feed_right)
            for at in range(fold)
        ],
        axis=1,
    )
    feed_out_sum = jnp.concatenate(
        [feed_left[fold * shard_rows :], feed_right[fold * shard_rows :]], axis=1
    )
    expert_rows = width // planes
    expert_in_sum = expert_sum[:expert_rows].astype(FULL)[None]
    expert_out_sum = expert_out_sum.astype(FULL)[None]
    bias_rows = expert_sum[expert_rows:].astype(FULL)
    in_bias_sum = lax.dynamic_slice(bias_rows, (0, plane * hidden_part), (1, hidden_part))
    out_bias_sum = lax.dynamic_slice(bias_rows, (1, plane * expert_rows), (1, expert_rows))
    small_turn = small_sum[:, :15].T
    return (
        trimmed(output),
        trimmed(dx0),
        small_turn[0:2],
        small_turn[2:8],
        dense_qkv_sum,
        dense_proj_sum,
        feed_in_sum,
        small_sum[:, 15 + experts : small_cols].reshape(-1),
        feed_out_sum,
        small_turn[8:10],
        small_turn[10:15],
        moe_qkv_sum,
        moe_proj_sum,
        small_sum[:, 15 : 15 + experts],
        expert_in_sum,
        in_bias_sum,
        expert_out_sum,
        out_bias_sum,
    )


def solution(mesh):
    return jax.shard_map(
        per_device,
        mesh=mesh,
        in_specs=(
            P(("fsdp", "expert"), None, None),
            P(None, ("fsdp", "expert")),
            P(None, ("fsdp", "expert")),
            P(("fsdp", "expert"), None),
            P(("fsdp", "expert"), None),
            P(("fsdp", "expert"), None),
            P(("fsdp", "expert")),
            P(("fsdp", "expert"), None),
            P(None, ("fsdp", "expert")),
            P(None, ("fsdp", "expert")),
            P(("fsdp", "expert"), None),
            P(("fsdp", "expert"), None),
            P(("fsdp", "expert"), None),
            P("expert", "fsdp", None),
            P("expert", "fsdp"),
            P("expert", "fsdp", None),
            P("expert", "fsdp"),
            P(("fsdp", "expert"), None, None),
            P(("fsdp", "expert"), None, None),
            P(("fsdp", "expert")),
            P(("fsdp", "expert"), None, None),
        ),
        out_specs=(
            P(("fsdp", "expert"), None, None),
            P(("fsdp", "expert"), None, None),
            P(None, ("fsdp", "expert")),
            P(None, ("fsdp", "expert")),
            P(("fsdp", "expert"), None),
            P(("fsdp", "expert"), None),
            P(("fsdp", "expert"), None),
            P(("fsdp", "expert")),
            P(("fsdp", "expert"), None),
            P(None, ("fsdp", "expert")),
            P(None, ("fsdp", "expert")),
            P(("fsdp", "expert"), None),
            P(("fsdp", "expert"), None),
            P(("fsdp", "expert"), None),
            P("expert", "fsdp", None),
            P("expert", "fsdp"),
            P("expert", "fsdp", None),
            P("expert", "fsdp"),
        ),
        check_vma=False,
    )
```

```python
from functools import partial

import jax
import jax.numpy as jnp
from jax import lax
from jax.experimental import pallas as pl
from jax.experimental.pallas import tpu as pltpu
from jax.sharding import PartitionSpec as P

TILE = 256
LOW = jnp.bfloat16
FULL = jnp.float32
eps_norm = 1e-06


def fit(count, step):
    return -(-count // step) * step


def whole(shape):
    return pl.BlockSpec(shape, lambda *at: (0,) * len(shape))


def shape_of(rows, cols, kind):
    return jax.ShapeDtypeStruct((rows, cols), kind)


def run_kernel(kernel, outs, arrays, micros, scalars=(), scratch=(), far=(), grid=None, in_blocks=None, out_blocks=None, ahead=False):
    nbytes = sum(a.size * a.dtype.itemsize for a in list(arrays) + list(far))
    nbytes += sum(o.size * o.dtype.itemsize for o in outs)
    if grid is None:
        in_blocks = [pl.BlockSpec(memory_space=pltpu.VMEM)] * len(arrays)
        out_blocks = [pl.BlockSpec(memory_space=pltpu.VMEM)] * len(outs)
    in_specs = [pl.BlockSpec(memory_space=pltpu.SMEM)] * len(scalars)
    in_specs += list(in_blocks) + [pl.BlockSpec(memory_space=pl.ANY)] * len(far)
    if ahead:
        more = {
            "grid_spec": pltpu.PrefetchScalarGridSpec(
                num_scalar_prefetch=len(scalars),
                grid=grid,
                in_specs=in_specs[len(scalars) :],
                out_specs=list(out_blocks),
                scratch_shapes=list(scratch),
            )
        }
    else:
        more = {
            "in_specs": in_specs,
            "out_specs": list(out_blocks),
            "scratch_shapes": list(scratch),
        }
        if grid is not None:
            more["grid"] = grid
    return pl.pallas_call(
        kernel,
        out_shape=list(outs),
        compiler_params=pltpu.CompilerParams(vmem_limit_bytes=56 * 1024 * 1024),
        cost_estimate=pl.CostEstimate(
            flops=int(micros * 0.4e9), bytes_accessed=nbytes, transcendentals=0
        ),
        **more,
    )(*scalars, *arrays, *far)


def mul(left, right):
    return jnp.dot(left, right, preferred_element_type=FULL)


def mul_turned(left, right):
    return lax.dot_general(left, right, (((1,), (1,)), ((), ())), preferred_element_type=FULL)


def turned_mul(left, right):
    return lax.dot_general(left, right, (((0,), (0,)), ((), ())), preferred_element_type=FULL)


def span(at, size):
    if isinstance(at, int):
        return slice(at * size, (at + 1) * size)
    return pl.ds(pl.multiple_of(at * size, size), size)


def norm_parts(values):
    center = values - jnp.mean(values, axis=-1, keepdims=True)
    spread = jnp.mean(center * center, axis=-1, keepdims=True)
    return center, lax.rsqrt(spread + eps_norm)


def norm_low(values, gain, shift):
    center, scale = norm_parts(values)
    return (center * scale * gain + shift).astype(LOW)


def norm_back(values, gain, upstream):
    center, scale = norm_parts(values)
    unit = center * scale
    inner = upstream * gain
    grad = scale * (
        inner
        - jnp.mean(inner, axis=-1, keepdims=True)
        - unit * jnp.mean(inner * unit, axis=-1, keepdims=True)
    )
    return (
        grad,
        jnp.sum(upstream * unit, axis=0, keepdims=True),
        jnp.sum(upstream, axis=0, keepdims=True),
    )


def gelu_parts(values):
    rate = 0.7978845608028654
    square = values * values
    bend = jnp.tanh(values * (rate + (rate * 0.044715) * square))
    half = 0.5 + 0.5 * bend
    slope = half + (values * (1.0 - bend * bend)) * (0.5 * rate + (1.5 * rate * 0.044715) * square)
    return (values * half).astype(LOW), slope.astype(LOW)


def split_low(values):
    high = values.astype(LOW)
    return high, (values - high.astype(FULL)).astype(LOW)


def head_masks():
    lane = lax.broadcasted_iota(jnp.int32, (1, 128), 1)
    first = (lane < 64).astype(FULL)
    return first, 1.0 - first


def near_copies(place_ref, own_ref, other_ref, target, sems):
    plane, side = place_ref[0], place_ref[1]
    count = sems.shape[0] // 2
    half_cols = own_ref.shape[1]
    lines = own_ref.shape[0] // count
    copies = []
    for core, source in enumerate((own_ref, other_ref)):
        cols = pl.ds(pl.multiple_of((side if core == 0 else 1 - side) * half_cols, 128), half_cols)
        for mask in range(count):
            start = pl.multiple_of((plane ^ mask) * lines, lines)
            copies.append(
                pltpu.make_async_copy(
                    source.at[pl.ds(mask * lines, lines), :],
                    target.at[pl.ds(start, lines), cols],
                    sems.at[core * count + mask],
                )
            )
    return copies


def score_parts(query, key, mask, keep):
    scores = mul_turned(query * (0.125 * mask).astype(LOW), key)
    scores = jnp.where(keep, scores, -1e30)
    raised = jnp.exp(scores - jnp.max(scores, axis=-1, keepdims=True))
    return raised * (1.0 / jnp.sum(raised, axis=-1, keepdims=True))


def attend_forward_kernel(length, images, lines_of, own, experts, *refs):
    if own:
        (
            place_ref, x_ref, near_ref, other_ref,
            an_ref, qkv_ref, o_ref, out_ref, vec_ref, wide_ref, router_ref, w_ref, sems,
        ) = refs
    else:
        (
            place_ref, x_ref, vec_ref, near_ref, other_ref,
            an_ref, qkv_ref, o_ref, out_ref, w_ref, sems,
        ) = refs
    copies = near_copies(place_ref, near_ref, other_ref, w_ref, sems)
    gain, shift, q_line, v_line, o_line = lines_of
    for copy in copies:
        copy.start()
    rows, width = x_ref.shape
    block = rows // images
    pairs = width // 128
    for copy in copies:
        copy.wait()
    if own:
        small = w_ref[:, 4 * width : 4 * width + 128]
        turned = small.astype(FULL).T
        vec_ref[...] = turned[0:32, :]
        spot = lax.broadcasted_iota(jnp.int32, (128, 128), 0) - lax.broadcasted_iota(
            jnp.int32, (128, 128), 1
        )
        lane = lax.broadcasted_iota(jnp.int32, (128, 128), 1)
        pick = jnp.where((spot == 15) & (lane < experts), 1.0, 0.0).astype(LOW)
        router_ref[...] = mul(small, pick).astype(LOW)
        depth = wide_ref.shape[1] // width
        near = lax.broadcasted_iota(jnp.int32, (128, 128 * depth), 0)
        place = lax.broadcasted_iota(jnp.int32, (128, 128 * depth), 1)
        spread = jnp.where(place // depth == near, 1.0, 0.0).astype(LOW)
        line = lax.broadcasted_iota(jnp.int32, (128, 128 * depth), 0)
        for at in range(width // 128):
            many = mul(turned[:, span(at, 128)].astype(LOW), spread)
            keep_line = line == place % depth + 15 + experts
            wide_ref[:, span(at, 128 * depth)] = jnp.sum(
                jnp.where(keep_line, many, 0.0), axis=0, keepdims=True
            )
    an_ref[...] = norm_low(x_ref[...], vec_ref[gain : gain + 1, :], vec_ref[shift : shift + 1, :])
    for at in range(3 * width // TILE):
        part = mul(an_ref[...], w_ref[:, span(at, TILE)])
        here = (at * TILE) % width
        if at * TILE < width:
            part = part + vec_ref[q_line : q_line + 1, here : here + TILE]
        elif at * TILE >= 2 * width:
            part = part + vec_ref[v_line : v_line + 1, here : here + TILE]
        qkv_ref[:, span(at, TILE)] = part.astype(LOW)

    first, second = head_masks()
    keep = lax.broadcasted_iota(jnp.int32, (1, block), 1) < length
    for image in range(images):
        for pair in range(pairs):
            lines = span(image, block)
            query = qkv_ref[lines, span(pair, 128)]
            key = qkv_ref[lines, span(pair + pairs, 128)]
            value = qkv_ref[lines, span(pair + 2 * pairs, 128)]
            mixed = [
                mul(score_parts(query, key, mask, keep).astype(LOW), value)
                for mask in (first, second)
            ]
            o_ref[lines, span(pair, 128)] = (mixed[0] * first + mixed[1] * second).astype(LOW)

    for at in range(width // TILE):
        cols = span(at, TILE)
        weight = w_ref[:, 3 * width + at * TILE : 3 * width + (at + 1) * TILE]
        out_ref[:, cols] = x_ref[:, cols] + (
            mul(o_ref[...], weight) + vec_ref[o_line : o_line + 1, cols]
        )


def weight_scratch(width, pieces, planes):
    cols = 2 * pieces[0].shape[1]
    return [pltpu.VMEM((width, cols), LOW), pltpu.SemaphoreType.DMA((2 * planes,))]


def attend_forward(place, x, vec, pieces, planes, lines_of, length, images, experts, inner):
    rows, width = x.shape
    outs = [
        shape_of(rows, width, LOW),
        shape_of(rows, 3 * width, LOW),
        shape_of(rows, width, LOW),
        shape_of(rows, width, FULL),
    ]
    own = vec is None
    if own:
        outs += [shape_of(32, width, FULL), shape_of(1, inner, FULL), shape_of(width, 128, LOW)]
    return run_kernel(
        partial(attend_forward_kernel, length, images, lines_of, own, experts),
        outs,
        [x] if own else [x, vec],
        11,
        scalars=[place],
        far=pieces,
        scratch=weight_scratch(width, pieces, planes),
    )


def attend_backward_kernel(length, images, lines_of, own, experts, place_ref, up_ref, x_ref, vec_ref, qkv_ref, *refs):
    gain = lines_of[0]
    if own:
        (
            feed_ref, moe_ref, gate_ref, wide_ref, router_ref, near_ref, other_ref,
            din_ref, mine_ref, away_ref, low_mine_ref, low_away_ref, small_ref,
            dol_ref, mix_ref, grad_ref, sums_ref, w_ref, sems,
        ) = refs
    else:
        (
            near_ref, other_ref, din_ref, mine_ref, away_ref, low_mine_ref, low_away_ref, sums_ref,
            dol_ref, mix_ref, grad_ref, w_ref, sems,
        ) = refs
    copies = near_copies(place_ref, near_ref, other_ref, w_ref, sems)
    for copy in copies:
        copy.start()
    rows, width = x_ref.shape
    block = rows // images
    pairs = width // 128
    side = place_ref[1]
    dol_ref[...] = up_ref[...].astype(LOW)
    for copy in copies:
        copy.wait()
    for at in range(width // TILE):
        cols = span(at, TILE)
        mix_ref[:, cols] = mul_turned(dol_ref[...], w_ref[cols, 3 * width : 4 * width]).astype(LOW)

    first, second = head_masks()
    keep = lax.broadcasted_iota(jnp.int32, (block, 1), 0) < length
    for image in range(images):
        for pair in range(pairs):
            lines = span(image, block)
            query = qkv_ref[lines, span(pair, 128)]
            key = qkv_ref[lines, span(pair + pairs, 128)]
            value = qkv_ref[lines, span(pair + 2 * pairs, 128)]
            mix = mix_ref[lines, span(pair, 128)]
            grads = []
            for mask in (first, second):
                scores = mul_turned(key * (0.125 * mask).astype(LOW), query)
                scores = jnp.where(keep, scores, -1e30)
                raised = jnp.exp(scores - jnp.max(scores, axis=0, keepdims=True))
                prob = raised * (1.0 / jnp.sum(raised, axis=0, keepdims=True))
                slope = mul_turned(value * mask.astype(LOW), mix)
                inner = jnp.sum(slope * prob, axis=0, keepdims=True)
                change = (prob * (slope - inner)).astype(LOW)
                grads.append(
                    (turned_mul(change, key), mul(change, query), mul(prob.astype(LOW), mix))
                )
            for part, rate in ((0, 0.125), (1, 0.125), (2, 1.0)):
                both = grads[0][part] * (rate * first) + grads[1][part] * (rate * second)
                grad_ref[lines, span(pair + part * pairs, 128)] = both.astype(LOW)

    for at in range(width // TILE):
        cols = span(at, TILE)
        din_ref[:, cols] = mul_turned(grad_ref[...], w_ref[cols, 0 : 3 * width])

    grad, gain_sum, shift_sum = norm_back(x_ref[...], vec_ref[gain : gain + 1, :], din_ref[...])
    din_ref[...] = up_ref[...] + grad
    sums_ref[0:1, :] = gain_sum
    sums_ref[1:2, :] = shift_sum
    sums_ref[2:3, :] = jnp.sum(grad_ref[:, 0:width].astype(FULL), axis=0, keepdims=True)
    sums_ref[3:4, :] = jnp.sum(
        grad_ref[:, 2 * width : 3 * width].astype(FULL), axis=0, keepdims=True
    )
    sums_ref[4:5, :] = jnp.sum(dol_ref[...].astype(FULL), axis=0, keepdims=True)
    sums_ref[5:8, :] = jnp.zeros((3, width), FULL)
    mine_ref[...] = grad_ref[:, span(side, 3 * width // 2)]
    away_ref[...] = grad_ref[:, span(1 - side, 3 * width // 2)]
    low_mine_ref[...] = dol_ref[:, span(side, width // 2)]
    low_away_ref[...] = dol_ref[:, span(1 - side, width // 2)]
    if not own:
        return
    depth = wide_ref.shape[1] // width
    line = lax.broadcasted_iota(jnp.int32, (8, 128 * depth), 0)
    place = lax.broadcasted_iota(jnp.int32, (8, 128 * depth), 1)
    near = lax.broadcasted_iota(jnp.int32, (128 * depth, 128), 1)
    spot = lax.broadcasted_iota(jnp.int32, (128 * depth, 128), 0)
    collect = jnp.where(spot // depth == near, 1.0, 0.0).astype(LOW)
    pieces = []
    for at in range(width // 128):
        many = jnp.where(place % depth == line, wide_ref[:, span(at, 128 * depth)], 0.0)
        high, rest = split_low(many)
        pieces.append(mul(high, collect) + mul(rest, collect))
    wide_rows = jnp.concatenate(pieces, axis=1)
    order = (
        (sums_ref, 0), (feed_ref, 0), (sums_ref, 1), (feed_ref, 1), (sums_ref, 2), (sums_ref, 3),
        (sums_ref, 4), (feed_ref, 2), (moe_ref, 0), (gate_ref, 0), (moe_ref, 1), (gate_ref, 1),
        (moe_ref, 2), (moe_ref, 3), (moe_ref, 4),
    )
    row = lax.broadcasted_iota(jnp.int32, (128, 1), 0)
    total = jnp.zeros((128, width), FULL)
    for at, (source, spot_line) in enumerate(order):
        total = jnp.where(row == at, source[spot_line : spot_line + 1, :], total)
    for at in range(depth):
        total = jnp.where(row == 15 + experts + at, wide_rows[at : at + 1, :], total)
    small_ref[...] = total.T + router_ref[...]


def attend_backward(place, up, x, vec, qkv, pieces, planes, gain, length, images, experts=0, more=()):
    rows, width = x.shape
    own = len(more) > 0
    return run_kernel(
        partial(attend_backward_kernel, length, images, (gain,), own, experts),
        [
            shape_of(rows, width, FULL),
            shape_of(rows, 3 * width // 2, LOW),
            shape_of(rows, 3 * width // 2, LOW),
            shape_of(rows, width // 2, LOW),
            shape_of(rows, width // 2, LOW),
            shape_of(width, 128, FULL) if own else shape_of(8, width, FULL),
        ],
        [up, x, vec, qkv] + list(more),
        19,
        scalars=[place],
        far=pieces,
        scratch=[
            pltpu.VMEM((rows, width), LOW),
            pltpu.VMEM((rows, width), LOW),
            pltpu.VMEM((rows, 3 * width), LOW),
        ]
        + ([pltpu.VMEM((8, width), FULL)] if own else [])
        + weight_scratch(width, pieces, planes),
    )


def unfold(source, target):
    groups, _, lines, wide = source.shape
    width = target.shape[1]
    fold = wide // width
    for group in range(groups):
        for at in range(fold):
            start = (group * fold + at) * lines
            target[start : start + lines, :] = source[group, 0, :, span(at, width)]


def feed_forward_kernel(
    lines_of, x_ref, vec_ref, bias_ref, in_ref, pack_ref, hn_ref, act_ref, slope_ref, out_ref, out_w_ref
):
    gain, shift, last = lines_of
    step = pl.program_id(0)

    @pl.when(step == 0)
    def _():
        hn_ref[...] = norm_low(
            x_ref[...], vec_ref[gain : gain + 1, :], vec_ref[shift : shift + 1, :]
        )
        out_ref[...] = x_ref[...] + vec_ref[last : last + 1, :]

    unfold(pack_ref, out_w_ref)
    for at in range(act_ref.shape[1] // TILE):
        cols = span(at, TILE)
        weight = in_ref[:, 0, :, cols].reshape(x_ref.shape[1], TILE)
        act, slope = gelu_parts(mul(hn_ref[...], weight) + bias_ref[:, cols])
        act_ref[:, cols] = act
        slope_ref[:, cols] = slope
    for at in range(out_ref.shape[1] // TILE):
        cols = span(at, TILE)
        out_ref[:, cols] += mul(act_ref[...], out_w_ref[:, cols])


def pack_blocks(pack, part, inner):
    groups, _, lines, _ = pack.shape
    return [
        pl.BlockSpec((groups, 1, lines, part), lambda at: (0, 0, 0, at)),
        pl.BlockSpec((part * groups // inner, 1, lines, inner), lambda at: (at, 1, 0, 0)),
    ]


def feed_forward(x, vec, bias, pack, lines_of):
    rows, width = x.shape
    inner = bias.shape[1]
    part = 768
    return run_kernel(
        partial(feed_forward_kernel, lines_of),
        [
            shape_of(rows, width, LOW),
            shape_of(rows, inner, LOW),
            shape_of(rows, inner, LOW),
            shape_of(rows, width, FULL),
        ],
        [x, vec, bias, pack, pack],
        11,
        scratch=[pltpu.VMEM((part, width), LOW)],
        grid=(inner // part,),
        in_blocks=[
            whole((rows, width)),
            whole(vec.shape),
            pl.BlockSpec((1, part), lambda at: (0, at)),
        ]
        + pack_blocks(pack, part, inner),
        out_blocks=[
            whole((rows, width)),
            pl.BlockSpec((rows, part), lambda at: (0, at)),
            pl.BlockSpec((rows, part), lambda at: (0, at)),
            whole((rows, width)),
        ],
    )


def feed_backward_kernel(
    gain, place_ref, up_ref, x_ref, vec_ref, slope_ref, in_ref, pack_ref,
    down_ref, mine_ref, away_ref, low_mine_ref, low_away_ref, sums_ref, bias_ref,
    dml_ref, du_ref, out_w_ref,
):
    step = pl.program_id(0)
    last = pl.num_programs(0) - 1
    width = x_ref.shape[1]
    part_cols = slope_ref.shape[1]

    @pl.when(step == 0)
    def _():
        dml_ref[...] = up_ref[...].astype(LOW)
        down_ref[...] = jnp.zeros(down_ref.shape, FULL)

    unfold(pack_ref, out_w_ref)
    for at in range(part_cols // TILE):
        cols = span(at, TILE)
        part = (
            mul_turned(dml_ref[...], out_w_ref[cols, :]) * slope_ref[:, cols].astype(FULL)
        ).astype(LOW)
        du_ref[step, :, cols] = part
        bias_ref[:, cols] = jnp.sum(part.astype(FULL), axis=0, keepdims=True)
    groups = in_ref.shape[0] // 2
    for at in range(2):
        weight = in_ref[span(at, groups), 0, :, :].reshape(width // 2, part_cols)
        down_ref[:, span(at, width // 2)] += mul_turned(du_ref[step, :, :], weight)

    @pl.when(step == last)
    def _():
        side = place_ref[1]
        grad, gain_sum, shift_sum = norm_back(x_ref[...], vec_ref[gain : gain + 1, :], down_ref[...])
        down_ref[...] = up_ref[...] + grad
        sums_ref[0:1, :] = gain_sum
        sums_ref[1:2, :] = shift_sum
        sums_ref[2:3, :] = jnp.sum(dml_ref[...].astype(FULL), axis=0, keepdims=True)
        sums_ref[3:8, :] = jnp.zeros((5, width), FULL)
        half = du_ref.shape[0] // 2
        for at in range(half):
            mine_ref[:, span(at, part_cols)] = du_ref[side * half + at, :, :]
            away_ref[:, span(at, part_cols)] = du_ref[(1 - side) * half + at, :, :]
        low_mine_ref[...] = dml_ref[:, span(side, width // 2)]
        low_away_ref[...] = dml_ref[:, span(1 - side, width // 2)]


def feed_backward(place, up, x, vec, slope, pack, gain):
    rows, width = x.shape
    inner = slope.shape[1]
    part = 768
    return run_kernel(
        partial(feed_backward_kernel, gain),
        [
            shape_of(rows, width, FULL),
            shape_of(rows, inner // 2, LOW),
            shape_of(rows, inner // 2, LOW),
            shape_of(rows, width // 2, LOW),
            shape_of(rows, width // 2, LOW),
            shape_of(8, width, FULL),
            shape_of(1, inner, FULL),
        ],
        [up, x, vec, slope, pack, pack],
        13,
        scalars=[place],
        scratch=[
            pltpu.VMEM((rows, width), LOW),
            pltpu.VMEM((inner // part, rows, part), LOW),
            pltpu.VMEM((part, width), LOW),
        ],
        grid=(inner // part,),
        in_blocks=[
            whole((rows, width)),
            whole((rows, width)),
            whole(vec.shape),
            pl.BlockSpec((rows, part), lambda at: (0, at)),
        ]
        + pack_blocks(pack, part, inner),
        out_blocks=[
            whole((rows, width)),
            whole((rows, inner // 2)),
            whole((rows, inner // 2)),
            whole((rows, width // 2)),
            whole((rows, width // 2)),
            whole((8, width)),
            pl.BlockSpec((1, part), lambda at: (0, at)),
        ],
    )


def product_kernel(counts, *refs):
    out_ref = refs[-1]
    start = 0
    at_ref = 0
    for count in counts:
        size = refs[at_ref + 1].shape[1]
        total = turned_mul(refs[at_ref][...], refs[at_ref + 1][...])
        for more in range(1, count):
            total += turned_mul(refs[at_ref + 2 * more][...], refs[at_ref + 2 * more + 1][...])
        out_ref[:, start : start + size] = total.astype(LOW)
        start += size
        at_ref += 2 * count
    if at_ref < len(refs) - 1:
        extra = refs[at_ref]
        out_ref[:, start : start + extra.shape[1]] = extra[...].astype(LOW)


def products(groups, extra=None, part=256):
    counts = [len(group) for group in groups]
    arrays = [array for group in groups for pair in group for array in pair]
    blocks = []
    for group in groups:
        for left, right in group:
            blocks += [pl.BlockSpec((left.shape[0], part), lambda at: (0, at)), whole(right.shape)]
    cols = sum(group[0][1].shape[1] for group in groups)
    if extra is not None:
        arrays.append(extra)
        blocks.append(pl.BlockSpec((part, extra.shape[1]), lambda at: (at, 0)))
        cols += extra.shape[1]
    lines = groups[0][0][0].shape[1]
    return run_kernel(
        partial(product_kernel, counts),
        [shape_of(lines, cols, LOW)],
        arrays,
        7,
        grid=(lines // part,),
        in_blocks=blocks,
        out_blocks=[pl.BlockSpec((part, cols), lambda at: (at, 0))],
    )[0]


def one_hot_rows(target, slots):
    hit = lax.broadcasted_iota(jnp.int32, (slots, target.shape[1]), 0) == target
    return jnp.where(hit, 1.0, 0.0).astype(LOW)


def one_hot_cols(target, slots):
    hit = lax.broadcasted_iota(jnp.int32, (target.shape[0], slots), 1) == target
    return jnp.where(hit, 1.0, 0.0).astype(LOW)


def slot_lanes(expert, slots, capacity):
    line = lax.broadcasted_iota(jnp.int32, (slots, 128), 0)
    lane = lax.broadcasted_iota(jnp.int32, (slots, 128), 1)
    return jnp.where((line == lane + expert * capacity) & (lane < capacity), 1.0, 0.0).astype(LOW)


def dispatch_kernel(
    experts, lines_of, x_ref, vec_ref, router_ref, route_ref, target_ref,
    mn_ref, gate_ref, pick_ref, out_ref, spot_ref,
):
    gain, shift = lines_of
    slots = out_ref.shape[0]
    capacity = slots // experts
    mn_ref[...] = norm_low(x_ref[...], vec_ref[gain : gain + 1, :], vec_ref[shift : shift + 1, :])
    logits = mul(mn_ref[...], router_ref[...])
    lane = lax.broadcasted_iota(jnp.int32, logits.shape, 1)
    logits = jnp.where(lane < experts, logits, -1e30)
    raised = jnp.exp(logits - jnp.max(logits, axis=-1, keepdims=True))
    gate = raised / jnp.sum(raised, axis=-1, keepdims=True)
    gate_ref[...] = gate
    picks = [
        jnp.sum(jnp.where(lane == route_ref[:, k : k + 1], gate, 0.0), axis=-1, keepdims=True)
        for k in range(2)
    ]
    pick = jnp.where(lane == 0, picks[0], jnp.where(lane == 1, picks[1], 0.0))
    pick_ref[...] = pick
    turned = pick.T
    for k in range(2):
        spot_ref[k, :, :] = one_hot_rows(target_ref[k : k + 1, :], slots)
    for at in range(out_ref.shape[1] // TILE):
        cols = span(at, TILE)
        out_ref[:, cols] = mul(spot_ref[0, :, :] + spot_ref[1, :, :], mn_ref[:, cols]).astype(LOW)
    row = lax.broadcasted_iota(jnp.int32, (16, 1), 0)
    weights = jnp.zeros((16, slots), FULL)
    for k in range(2):
        high, rest = split_low(turned[k : k + 1, :])
        both = jnp.where(row == 14, high.astype(FULL), jnp.where(row == 15, rest.astype(FULL), 0.0))
        weights += mul_turned(both.astype(LOW), spot_ref[k, :, :])
    weights = weights.astype(LOW)
    for expert in range(experts):
        lines = slice((expert + 1) * capacity - 16, (expert + 1) * capacity)
        chosen = mul(weights, slot_lanes(expert, slots, capacity))
        out_ref[lines, 0:128] = jnp.where(
            row >= 14, chosen, out_ref[lines, 0:128].astype(FULL)
        ).astype(LOW)


def dispatch(x, vec, router, routes, targets, experts, slots, lines_of):
    rows, width = x.shape
    return run_kernel(
        partial(dispatch_kernel, experts, lines_of),
        [
            shape_of(rows, width, LOW),
            shape_of(rows, 128, FULL),
            shape_of(rows, 128, FULL),
            shape_of(slots, width, LOW),
        ],
        [x, vec, router, routes, targets],
        6,
        scratch=[pltpu.VMEM((2, slots, rows), LOW)],
    )


def restore(place_ref, source, target):
    planes, lines, _ = target.shape
    for mask in range(planes):
        target[place_ref[0] ^ mask, :, :] = source[mask * lines : (mask + 1) * lines, :]


def unfold_lines(place_ref, source, target, lines):
    width = target.shape[1]
    fold = source.shape[1] // width
    many = source.shape[0] // lines
    for mask in range(many):
        group = mask ^ (place_ref[0] % many)
        for at in range(fold):
            start = pl.multiple_of((group * fold + at) * lines, lines)
            target[pl.ds(start, lines), :] = source[
                mask * lines : (mask + 1) * lines, span(at, width)
            ]


def hidden_kernel(
    experts, place_ref, x_ref, bias_ref, pack_ref, up_ref, act_ref, slope_ref, dy_ref, last_ref, w_ref
):
    restore(place_ref, pack_ref, w_ref)

    @pl.when(pl.program_id(0) == 0)
    def _():
        capacity = x_ref.shape[0] // experts
        row = lax.broadcasted_iota(jnp.int32, (128, 1), 0)
        table = jnp.zeros((128, 128), FULL)
        for group in range(experts):
            mark = x_ref[(group + 1) * capacity - 16 : (group + 1) * capacity, 0:128].astype(FULL)
            table = jnp.where(row == group, mark[14:15, :] + mark[15:16, :], table)
        table = table.T
        total = jnp.zeros(last_ref.shape, FULL)
        for group in range(experts):
            spots = slice(group * capacity, (group + 1) * capacity)
            part = (table[0:capacity, group : group + 1] * up_ref[spots, :].astype(FULL)).astype(LOW)
            dy_ref[spots, :] = part
            total += jnp.sum(part.astype(FULL), axis=0, keepdims=True)
        last_ref[...] = total

    for at in range(act_ref.shape[1] // TILE):
        cols = span(at, TILE)
        weight = w_ref[:, :, cols].reshape(x_ref.shape[1], TILE)
        act, slope = gelu_parts(mul(x_ref[...], weight) + bias_ref[:, cols])
        act_ref[:, cols] = act
        slope_ref[:, cols] = slope


def hidden_forward(place, x, bias, weight, up, planes, experts):
    rows, width = x.shape
    inner = bias.shape[1]
    part = 768
    return run_kernel(
        partial(hidden_kernel, experts),
        [
            shape_of(rows, inner, LOW),
            shape_of(rows, inner, LOW),
            shape_of(rows, width, LOW),
            shape_of(1, width, FULL),
        ],
        [x, bias, weight, up],
        11,
        scalars=[place],
        scratch=[pltpu.VMEM((planes, width // planes, part), LOW)],
        grid=(inner // part,),
        in_blocks=[
            whole(x.shape),
            pl.BlockSpec((1, part), lambda at: (0, at)),
            pl.BlockSpec((width, part), lambda at: (0, at)),
            whole(up.shape),
        ],
        out_blocks=[pl.BlockSpec((rows, part), lambda at: (0, at))] * 2
        + [whole((rows, width)), whole((1, width))],
    )


def expert_out_kernel(
    lines, experts, place_ref, act_ref, bias_ref, pack_ref, up_ref, out_ref, dot_ref, sum_ref, w_ref
):
    step = pl.program_id(0)
    unfold_lines(place_ref, pack_ref, w_ref, lines)

    @pl.when(step == 0)
    def _():
        sum_ref[...] = jnp.zeros(sum_ref.shape, FULL) + bias_ref[...]

    for at in range(w_ref.shape[1] // TILE):
        cols = span(at, TILE)
        sum_ref[:, cols] += mul(act_ref[...], w_ref[:, cols])

    @pl.when(step == pl.num_programs(0) - 1)
    def _():
        result = sum_ref[...].astype(LOW)
        out_ref[...] = result
        dots = jnp.sum(result.astype(FULL) * up_ref[...].astype(FULL), axis=-1, keepdims=True)
        capacity = result.shape[0] // experts
        lane = lax.broadcasted_iota(jnp.int32, (capacity, 128), 1)
        table = jnp.zeros((capacity, 128), FULL)
        for group in range(experts):
            table = jnp.where(lane == group, dots[group * capacity : (group + 1) * capacity], table)
        if capacity < 128:
            table = jnp.concatenate([table, jnp.zeros((128 - capacity, 128), FULL)], axis=0)
        table = table.T
        row = lax.broadcasted_iota(jnp.int32, (16, 1), 0)
        for group in range(experts):
            high, rest = split_low(table[group : group + 1, :])
            both = jnp.where(
                row == 14, high.astype(FULL), jnp.where(row == 15, rest.astype(FULL), 0.0)
            )
            dot_ref[group * 16 : (group + 1) * 16, :] = both.astype(LOW)


def expert_out_forward(place, act, bias, weight, up, lines, experts):
    rows, width = act.shape[0], weight.shape[1]
    inner = act.shape[1]
    part = 768
    many = part // lines
    return run_kernel(
        partial(expert_out_kernel, lines, experts),
        [shape_of(rows, width, LOW), shape_of(experts * 16, 128, LOW)],
        [act, bias, weight, up],
        9,
        scalars=[place],
        scratch=[pltpu.VMEM((rows, width), FULL), pltpu.VMEM((part, width), LOW)],
        grid=(inner // part,),
        in_blocks=[
            pl.BlockSpec((rows, part), lambda at, place: (0, at ^ (place[0] // many))),
            pl.BlockSpec(bias.shape, lambda at, place: (0, 0)),
            pl.BlockSpec((part, width), lambda at, place: (at, 0)),
            pl.BlockSpec(up.shape, lambda at, place: (0, 0)),
        ],
        out_blocks=[
            pl.BlockSpec((rows, width), lambda at, place: (0, 0)),
            pl.BlockSpec((experts * 16, 128), lambda at, place: (0, 0)),
        ],
        ahead=True,
    )


def expert_backward_kernel(
    lines, experts, place_ref, dy_ref, slope_ref, pack_ref, in_ref, dot_ref,
    dh_ref, bias_ref, back_ref, sum_ref, out_w_ref, in_w_ref,
):
    step = pl.program_id(0)
    rows = dy_ref.shape[0]
    capacity = rows // experts
    unfold_lines(place_ref, pack_ref, out_w_ref, lines)
    restore(place_ref, in_ref, in_w_ref)

    @pl.when(step == 0)
    def _():
        sum_ref[...] = jnp.zeros(sum_ref.shape, FULL)

    for at in range(slope_ref.shape[1] // TILE):
        cols = span(at, TILE)
        part = (
            mul_turned(dy_ref[...], out_w_ref[cols, :]) * slope_ref[:, cols].astype(FULL)
        ).astype(LOW)
        dh_ref[:, cols] = part
        bias_ref[:, cols] = jnp.sum(part.astype(FULL), axis=0, keepdims=True)
    planes, tall, part_cols = in_w_ref.shape
    for at in range(2):
        weight = in_w_ref[span(at, planes // 2), :, :].reshape(planes * tall // 2, part_cols)
        sum_ref[:, span(at, planes * tall // 2)] += mul_turned(dh_ref[...], weight)

    @pl.when(step == pl.num_programs(0) - 1)
    def _():
        back_ref[...] = sum_ref[...].astype(LOW)
        row = lax.broadcasted_iota(jnp.int32, (16, 1), 0)
        for group in range(experts):
            spots = slice((group + 1) * capacity - 16, (group + 1) * capacity)
            back_ref[spots, 0:128] = jnp.where(
                row >= 14,
                dot_ref[group * 16 : (group + 1) * 16, :].astype(FULL),
                sum_ref[spots, 0:128],
            ).astype(LOW)


def expert_backward(place, dy, slope, w_out, w_in, dots, lines, experts):
    rows, width = dy.shape
    inner = slope.shape[1]
    planes = inner // lines
    part = 768
    many = part // lines

    def moved(at, place):
        return (0, at ^ (place[0] // many))

    def fixed(at, place):
        return (0, 0)

    return run_kernel(
        partial(expert_backward_kernel, lines, experts),
        [
            shape_of(rows, inner, LOW),
            shape_of(1, inner, FULL),
            shape_of(rows, width, LOW),
        ],
        [dy, slope, w_out, w_in, dots],
        15,
        scalars=[place],
        scratch=[
            pltpu.VMEM((rows, width), FULL),
            pltpu.VMEM((part, width), LOW),
            pltpu.VMEM((planes, width // planes, part), LOW),
        ],
        grid=(inner // part,),
        in_blocks=[
            pl.BlockSpec((rows, width), fixed),
            pl.BlockSpec((rows, part), moved),
            pl.BlockSpec((part, width), lambda at, place: (at, 0)),
            pl.BlockSpec((width, part), moved),
            pl.BlockSpec(dots.shape, fixed),
        ],
        out_blocks=[
            pl.BlockSpec((rows, part), moved),
            pl.BlockSpec((1, part), moved),
            pl.BlockSpec((rows, width), fixed),
        ],
        ahead=True,
    )


def output_kernel(x_ref, home_ref, pick_ref, target_ref, live_ref, out_ref, spot_ref):
    slots = home_ref.shape[0]
    for k in range(2):
        spot_ref[k, :, :] = one_hot_cols(target_ref[:, k : k + 1], slots)
    for at in range(x_ref.shape[1] // TILE):
        cols = span(at, TILE)
        total = x_ref[:, cols]
        for k in range(2):
            total += pick_ref[:, k : k + 1] * mul(spot_ref[k, :, :], home_ref[:, cols])
        out_ref[:, cols] = (total * live_ref[...]).astype(LOW)


def output_rows(x, home, pick, targets, live):
    rows, width = x.shape
    return run_kernel(
        output_kernel,
        [shape_of(rows, width, LOW)],
        [x, home, pick, targets, live],
        7,
        scratch=[pltpu.VMEM((2, rows, home.shape[0]), LOW)],
    )[0]


def return_kernel(
    gain, experts, x_ref, vec_ref, home_ref, gate_ref, route_ref, target_ref, up_ref, mn_ref,
    router_ref, out_ref, sums_ref, router_grad_ref, spot_ref,
):
    rows, width = x_ref.shape
    slots = home_ref.shape[0]
    capacity = slots // experts
    for k in range(2):
        spot_ref[k, :, :] = one_hot_cols(target_ref[:, k : k + 1], slots)
    line = jnp.zeros((16, slots), FULL)
    for expert in range(experts):
        marks = home_ref[(expert + 1) * capacity - 16 : (expert + 1) * capacity, 0:128]
        line += mul_turned(marks, slot_lanes(expert, slots, capacity))
    line = line.astype(LOW)
    lane = lax.broadcasted_iota(jnp.int32, (rows, 128), 1)
    gate = gate_ref[...]
    spread = jnp.zeros((rows, 128), FULL)
    for k in range(2):
        dots = mul_turned(spot_ref[k, :, :], line)
        spread += jnp.where(lane == route_ref[:, k : k + 1], dots[:, 14:15] + dots[:, 15:16], 0.0)
    logit = gate * (spread - jnp.sum(gate * spread, axis=-1, keepdims=True))
    high, rest = split_low(pltpu.roll(logit, 15, 1))
    router_grad_ref[...] = turned_mul(mn_ref[...], high) + turned_mul(mn_ref[...], rest)
    high, rest = split_low(logit)
    for at in range(width // TILE):
        cols = span(at, TILE)
        out_ref[:, cols] = (
            mul_turned(high, router_ref[cols, :])
            + mul_turned(rest, router_ref[cols, :])
            + mul(spot_ref[0, :, :] + spot_ref[1, :, :], home_ref[:, cols])
        )

    grad, gain_sum, shift_sum = norm_back(x_ref[...], vec_ref[gain : gain + 1, :], out_ref[...])
    out_ref[...] = up_ref[...].astype(FULL) + grad
    sums_ref[0:1, :] = gain_sum
    sums_ref[1:2, :] = shift_sum
    sums_ref[2:8, :] = jnp.zeros((6, width), FULL)


def return_grad(x, vec, home, gate, routes, targets, up, mn, router, gain, experts, after):
    rows, width = x.shape
    slots = home.shape[0]
    return run_kernel(
        partial(return_kernel, gain, experts),
        [shape_of(rows, width, FULL), shape_of(8, width, FULL), shape_of(width, 128, FULL)],
        [x, vec, home, gate, routes, targets, up, mn, router],
        7,
        far=after,
        scratch=[pltpu.VMEM((2, rows, slots), LOW)],
    )


def feed_products_kernel(lines, fold, hn_ref, hn_far_ref, du_ref, du_far_ref, act_ref, act_far_ref, low_ref, low_far_ref, out_ref):
    cols = du_ref.shape[1] // fold
    tall = 2 * fold * lines
    tile = hn_ref.shape[1]
    for at in range(fold):
        part = turned_mul(hn_ref[...], du_ref[:, span(at, cols)])
        part += turned_mul(hn_far_ref[...], du_far_ref[:, span(at, cols)])
        part = part.astype(LOW)
        for spot in range(tile // lines):
            start = spot * tall + at * lines
            out_ref[start : start + lines, :] = part[spot * lines : (spot + 1) * lines, :]
    for at in range(act_ref.shape[1] // tile):
        part = turned_mul(act_ref[:, span(at, tile)], low_ref[...])
        part += turned_mul(act_far_ref[:, span(at, tile)], low_far_ref[...])
        part = part.astype(LOW)
        size = fold * lines
        for spot in range(tile // size):
            start = (at * (tile // size) + spot) * tall + size
            out_ref[start : start + size, :] = part[spot * size : (spot + 1) * size, :]


def feed_products(hn, hn_far, du, du_far, act, act_far, low, low_far, blocks, fold):
    rows, width = hn.shape
    lines = width // blocks
    tall = 2 * fold * lines
    steps = 2
    left = pl.BlockSpec((rows, width // steps), lambda at: (0, at))
    wide = pl.BlockSpec((rows, fold * width // steps), lambda at: (0, at))
    return run_kernel(
        partial(feed_products_kernel, lines, fold),
        [shape_of(blocks * tall, low.shape[1], LOW)],
        [hn, hn_far, du, du_far, act, act_far, low, low_far],
        11,
        grid=(steps,),
        in_blocks=[left, left, whole(du.shape), whole(du.shape), wide, wide, whole(low.shape), whole(low.shape)],
        out_blocks=[pl.BlockSpec((blocks * tall // steps, low.shape[1]), lambda at: (at, 0))],
    )[0]


def expert_products_kernel(lines, x_ref, dh_ref, in_bias_ref, out_bias_ref, out_ref):
    width = out_bias_ref.shape[1]
    planes = width // lines
    tall = lines + 16
    step = pl.program_id(0)
    row = lax.broadcasted_iota(jnp.int32, (16, 1), 0)
    last = jnp.where(step == 0, 1.0, 0.0) * out_bias_ref[...]
    both = jnp.where(row == 0, in_bias_ref[...], jnp.where(row == 1, last, 0.0)).astype(LOW)
    many = max(1, 384 // lines)
    for at in range(planes // many):
        part = turned_mul(x_ref[:, span(at, many * lines)], dh_ref[...]).astype(LOW)
        for spot in range(many):
            start = (at * many + spot) * tall
            out_ref[start : start + lines, :] = part[spot * lines : (spot + 1) * lines, :]
            out_ref[start + lines : start + tall, :] = both


def expert_products(x, dh, in_bias, out_bias, planes):
    slots, width = x.shape
    inner = dh.shape[1]
    lines = width + 16 * planes
    return run_kernel(
        partial(expert_products_kernel, width // planes),
        [shape_of(lines, inner, LOW)],
        [x, dh, in_bias, out_bias],
        8,
        grid=(inner // width,),
        in_blocks=[
            whole(x.shape),
            pl.BlockSpec((slots, width), lambda at: (0, at)),
            pl.BlockSpec((1, width), lambda at: (0, at)),
            whole(out_bias.shape),
        ],
        out_blocks=[pl.BlockSpec((lines, width), lambda at: (0, at))],
    )[0]


def spread_kernel(target_ref, up_ref, out_ref, spot_ref):
    slots = out_ref.shape[0]
    spot_ref[...] = one_hot_rows(target_ref[0:1, :], slots) + one_hot_rows(target_ref[1:2, :], slots)
    for at in range(out_ref.shape[1] // TILE):
        cols = span(at, TILE)
        out_ref[:, cols] = mul(spot_ref[...], up_ref[:, cols]).astype(LOW)


def spread_up(targets, up, slots):
    rows, width = up.shape
    return run_kernel(
        spread_kernel,
        [shape_of(slots, width, LOW)],
        [targets, up],
        4,
        scratch=[pltpu.VMEM((slots, rows), LOW)],
    )[0]


tie = lax.optimization_barrier


def trade(value, axis_name, mask):
    count = lax.axis_size(axis_name)
    return lax.ppermute(value, axis_name, [(place, place ^ mask) for place in range(count)])


def in_order(pieces, place):
    level = 0
    while len(pieces) > 1:
        flip = ((place >> level) & 1) == 1
        pieces = [
            jnp.where(
                flip,
                jnp.concatenate([pieces[at + 1], pieces[at]], axis=0),
                jnp.concatenate([pieces[at], pieces[at + 1]], axis=0),
            )
            for at in range(0, len(pieces), 2)
        ]
        level += 1
    return pieces[0]


def core_side():
    return lax.axis_index("expert") % 2


def core_half(shard):
    side = core_side()
    half = shard.shape[1] // 2
    mine = lax.dynamic_slice_in_dim(shard, side * half, half, 1)
    away = lax.dynamic_slice_in_dim(shard, (1 - side) * half, half, 1)
    return in_order([mine, trade(away, "expert", 1)], side)


def layer_gather(shard):
    layers = lax.axis_size("expert") // 2
    stacked = [shard] + [trade(shard, "expert", 2 * mask) for mask in range(1, layers)]
    return in_order(stacked, lax.axis_index("expert") // 2)


def plane_near(piece):
    count = lax.axis_size("fsdp")
    masks = (1, 2) if count == 4 else range(1, count)
    return [trade(piece, "fsdp", mask) for mask in masks]


def plane_far(near):
    if lax.axis_size("fsdp") != 4:
        return []
    half = near[0].shape[0] // 2
    return [trade(near[1][:half], "fsdp", 1), trade(near[0][half:], "fsdp", 2)]


def both_cores(own, near, far):
    held = jnp.concatenate([own] + near + far, axis=0)
    return held, trade(held, "expert", 1)


def sum_first(blocks):
    count = lax.axis_size("fsdp")
    place = lax.axis_index("fsdp")
    parts = [
        lax.dynamic_index_in_dim(blocks, place ^ mask, 0, keepdims=False) for mask in range(count)
    ]
    if count != 4:
        return parts, []
    half = blocks.shape[1] // 2
    return parts[:3], [
        trade(parts[3][:half], "fsdp", 1),
        trade(parts[3][half:], "fsdp", 2),
    ]


def added(left, right):
    return (left.astype(FULL) + right.astype(FULL)).astype(LOW)


def sum_second(parts, got):
    if not got:
        return [trade(part, "fsdp", mask) for mask, part in enumerate(parts) if mask > 0]
    half = parts[1].shape[0] // 2
    send_x = jnp.concatenate([parts[1][:half], added(parts[1][half:], got[1])], axis=0)
    send_y = jnp.concatenate([added(parts[2][:half], got[0]), parts[2][half:]], axis=0)
    return [trade(send_x, "fsdp", 1), trade(send_y, "fsdp", 2)]


def sum_total(own, arrived):
    total = own.astype(FULL)
    for term in arrived:
        total = total + term.astype(FULL)
    return total


def layer_first(held):
    layer = lax.axis_index("expert") // 2
    layers = lax.axis_size("expert") // 2
    parts = [
        lax.dynamic_index_in_dim(held, layer ^ mask, 0, keepdims=False) for mask in range(layers)
    ]
    return parts[0], [trade(parts[mask], "expert", 2 * mask) for mask in range(1, layers)]


def core_last(total):
    side = core_side()
    rows = total.shape[0] // 2
    mine = lax.dynamic_slice_in_dim(total, side * rows, rows, 0)
    away = lax.dynamic_slice_in_dim(total, (1 - side) * rows, rows, 0).astype(LOW)
    came = trade(away, "expert", 1).astype(FULL)
    return jnp.where(side == 0, mine, came), jnp.where(side == 0, came, mine)


def feed_half(fc_in, fc_out):
    side = core_side()
    lines, inner = fc_in.shape
    fold = inner // fc_out.shape[1]
    blocks = [fc_out[at * lines : (at + 1) * lines] for at in range(fold)]
    folded = jnp.concatenate(blocks, axis=1)
    came = trade(jnp.where(side == 0, folded, fc_in), "expert", 1)
    width = fc_out.shape[1]
    rows_came = [came[:, at * width : (at + 1) * width] for at in range(fold)]
    stacked = [
        jnp.concatenate([group[at], group[at + 1]], axis=0)
        for group in (rows_came, blocks)
        for at in range(0, fold, 2)
    ]
    return jnp.where(
        side == 0, jnp.concatenate([fc_in, came], axis=0), jnp.concatenate(stacked, axis=1)
    )


def feed_last(total, fold):
    side = core_side()
    cols = total.shape[1]
    size = total.shape[0] // 2
    inside = total[:size].reshape(fold, 2, -1, cols)
    outside = total[size:].reshape(2, -1, cols)

    def part(core):
        return jnp.concatenate(
            [
                lax.dynamic_index_in_dim(inside, core, 1, keepdims=False).reshape(-1, cols),
                lax.dynamic_index_in_dim(outside, core, 0, keepdims=False),
            ],
            axis=0,
        )

    mine = part(side)
    came = trade(part(1 - side).astype(LOW), "expert", 1).astype(FULL)
    return jnp.where(side == 0, mine, came), jnp.where(side == 0, came, mine)


def in_blocks(half_grad):
    planes = lax.axis_size("fsdp")
    layers = lax.axis_size("expert") // 2
    return half_grad.reshape(planes, layers, -1, half_grad.shape[-1])


def per_device(
    patches,
    dense_gains,
    dense_shifts,
    dense_qkv,
    dense_proj,
    dense_fc_in,
    dense_fc_bias,
    dense_fc_out,
    moe_gains,
    moe_shifts,
    moe_qkv,
    moe_proj,
    router,
    expert_in,
    expert_in_bias,
    expert_out,
    expert_out_bias,
    routes,
    slot_pos,
    image_counts,
    cotangent,
):
    images, length, width = patches.shape
    shard_rows = dense_qkv.shape[0]
    inner = dense_fc_in.shape[1]
    local_experts = expert_in.shape[0]
    experts = local_experts * lax.axis_size("expert")
    planes = lax.axis_size("fsdp")
    plane = lax.axis_index("fsdp")
    place = jnp.stack([plane, core_side()]).astype(jnp.int32)
    block = fit(length, 16)
    rows = images * block
    lowest = (images + 1) // 2
    capacity = fit(5 * (images + lowest) * length // (4 * experts) + 4, 16)
    slots = experts * capacity

    def padded(array, fill=0):
        return jnp.pad(
            array, ((0, 0), (0, block - length), (0, 0)), constant_values=fill
        ).reshape(rows, array.shape[-1])

    def trimmed(array):
        return array.reshape(images, block, array.shape[-1])[:, :length]

    def far(array):
        return trade(array, "expert", 1)

    layers = lax.axis_size("expert") // 2
    fold = inner // width
    small_rows = jnp.concatenate(
        [
            dense_gains.T,
            dense_shifts.T,
            moe_gains.T,
            moe_shifts.T,
            router,
            dense_fc_bias.reshape(shard_rows, -1),
        ],
        axis=1,
    )
    small_cols = small_rows.shape[1]
    small_rows = jnp.pad(small_rows, ((0, 0), (0, 256 - small_cols)))
    first_half = core_half(jnp.concatenate([dense_qkv, dense_proj, small_rows], axis=1))
    moe_half = core_half(jnp.concatenate([moe_qkv, moe_proj], axis=1))
    if (2 * shard_rows) % 16 == 0:
        later = feed_half(dense_fc_in, dense_fc_out)
        pack = lax.all_gather(later, ("fsdp", "expert"), axis=0, tiled=True)
        pack = pack.reshape(planes * layers, 2, 2 * shard_rows, later.shape[1])
    else:
        groups = width // 48
        whole_in = lax.all_gather(dense_fc_in, ("fsdp", "expert"), axis=0, tiled=True)
        whole_out = lax.all_gather(dense_fc_out, ("fsdp", "expert"), axis=0, tiled=True)
        folded = whole_out.reshape(groups, fold, 48, width).swapaxes(1, 2).reshape(groups, 48, inner)
        pack = jnp.stack([whole_in.reshape(groups, 48, inner), folded], axis=1)
    dense_own = layer_gather(first_half)
    expert_bias = jnp.concatenate([expert_in_bias[0], expert_out_bias[0]])
    other_bias = [trade(expert_bias, "fsdp", mask) for mask in range(1, planes)]
    dense_own, other_bias = tie((dense_own, other_bias))
    expert_bias = in_order([part[None] for part in [expert_bias] + other_bias], plane).astype(FULL)
    dense_own, moe_half = tie((dense_own, moe_half))
    dense_near = plane_near(dense_own)
    moe_own = layer_gather(moe_half)
    dense_near, moe_own = tie((dense_near, moe_own))
    dense_far = plane_far(dense_near)
    moe_near = plane_near(moe_own)
    dense_pieces = both_cores(dense_own, dense_near, dense_far)

    live_images = jnp.arange(images) < image_counts[0]
    live_rows = jnp.repeat(live_images, block).astype(FULL)[:, None]
    up = padded(jnp.where(live_images[:, None, None], cotangent, jnp.zeros_like(cotangent)))
    route_cols = padded(routes)
    target_cols = padded(jnp.where(slot_pos >= 0, routes * capacity + slot_pos, -1), -1)
    target_rows = target_cols.T

    def exchange(array):
        return lax.all_to_all(
            array.reshape(experts, capacity, width), "expert", split_axis=0, concat_axis=0, tiled=True
        ).reshape(slots, width)

    x0, up_spread = tie((padded(patches).astype(FULL), spread_up(target_rows, up, slots)))
    up_slots = exchange(up_spread)
    an, qkv, mixed, x1, vec, fc_bias, router_full = attend_forward(
        place, x0, None, dense_pieces, planes, (0, 2, 4, 5, 6), length, images, experts, inner
    )
    x1, moe_near, in_own, out_own = tie((x1, moe_near, expert_in[0], expert_out[0]))
    moe_pieces = both_cores(moe_own, moe_near, plane_far(moe_near))
    in_near = plane_near(in_own)
    out_near = plane_near(out_own)
    hidden_part = expert_in_bias.shape[1]
    in_bias = expert_bias[:, :hidden_part].reshape(1, -1)
    out_bias = expert_bias[:, hidden_part:].reshape(1, -1)

    hn, act, slope, x2 = feed_forward(x1, vec, fc_bias, pack, (1, 3, 7))
    an2, qkv2, mixed2, x3 = attend_forward(
        place, x2, vec, moe_pieces, planes, (8, 10, 12, 13, 14), length, images, experts, inner
    )
    x3, up_slots = tie((x3, up_slots))
    in_far = plane_far(in_near)
    out_far = plane_far(out_near)
    w_in = jnp.concatenate([in_own] + in_near + in_far, axis=0)
    w_out = jnp.concatenate([out_own] + out_near + out_far, axis=0)
    mn, gate, pick, outgoing = dispatch(
        x3, vec, router_full, route_cols, target_rows, experts, slots, (9, 11)
    )
    arrived = exchange(outgoing)
    e_act, e_slope, dy, out_bias_grad = hidden_forward(
        place, arrived, in_bias, w_in, up_slots, planes, experts
    )
    out_grad = products([[(e_act, dy)]], part=768)
    out_grad, e_act, w_out = tie((out_grad, e_act, w_out))
    expert_out_sum = lax.psum_scatter(out_grad, "fsdp", scatter_dimension=0, tiled=True)
    hidden_rows = inner // planes
    result, dots = expert_out_forward(
        place, e_act, out_bias, w_out, up_slots, hidden_rows, experts
    )
    dh, in_bias_grad, back = expert_backward(
        place, dy, e_slope, w_out, w_in, dots, hidden_rows, experts
    )
    back = exchange(back)
    expert_grad = expert_products(arrived, dh, in_bias_grad, out_bias_grad, planes)
    lefts = [far(array) for array in (hn, act, an, mixed, an2, mixed2)]
    expert_grad, back, result, expert_out_sum, lefts = tie(
        (expert_grad, back, result, expert_out_sum, lefts)
    )
    hn_far, act_far, an_far, mixed_far, an2_far, mixed2_far = lefts
    expert_sum = lax.psum_scatter(expert_grad, "fsdp", scatter_dimension=0, tiled=True)
    home = exchange(result)
    dx3, gate_sums, router_grad = return_grad(
        x3, vec, back, gate, route_cols, target_cols, up, mn, router_full, 9, experts, []
    )
    dx2, mine2, away2, low_mine2, low_away2, moe_sums = attend_backward(
        place, dx3, x2, vec, qkv2, moe_pieces, planes, 8, length, images
    )
    dx1, mine1, away1, low_mine1, low_away1, feed_sums, fc_bias_grad = feed_backward(
        place, dx2, x1, vec, slope, pack, 1
    )
    away2, low_away2, away1, low_away1, dx1 = tie(
        (far(away2), far(low_away2), far(away1), far(low_away1), dx1)
    )
    moe_grad = products(
        [
            [(an2, mine2), (an2_far, away2)],
            [(mixed2, low_mine2), (mixed2_far, low_away2)],
        ]
    )
    moe_parts, moe_got = sum_first(in_blocks(moe_grad))
    if (2 * shard_rows) % 16 == 0:
        feed_grad = feed_products(
            hn, hn_far, mine1, away1, act, act_far, low_mine1, low_away1,
            planes * layers, fold,
        )
    else:
        in_part = products([[(hn, mine1), (hn_far, away1)]])
        out_part = products([[(act, low_mine1), (act_far, low_away1)]], part=768)
        in_part = in_blocks(in_part)
        in_part = in_part.reshape(in_part.shape[:3] + (fold, -1)).swapaxes(2, 3)
        in_part = in_part.reshape(planes, layers, -1, in_part.shape[-1])
        feed_grad = jnp.concatenate([in_part, in_blocks(out_part)], axis=2)
        feed_grad = feed_grad.reshape(-1, feed_grad.shape[-1])
    feed_grad, dx1, moe_got = tie((feed_grad, dx1, moe_got))
    feed_parts, feed_got = sum_first(in_blocks(feed_grad))
    moe_came = sum_second(moe_parts, moe_got)
    dx0, mine0, away0, low_mine0, low_away0, vectors = attend_backward(
        place, dx1, x0, vec, qkv, dense_pieces, planes, 0, length, images, experts,
        [feed_sums, moe_sums, gate_sums, fc_bias_grad, router_grad],
    )
    feed_got, mine0, expert_sum, moe_came = tie((feed_got, mine0, expert_sum, moe_came))
    feed_came = sum_second(feed_parts, feed_got)
    moe_mine, moe_layers = layer_first(sum_total(moe_parts[0], moe_came).astype(LOW))
    dense_grad = products(
        [
            [(an, mine0), (an_far, far(away0))],
            [(mixed, low_mine0), (mixed_far, far(low_away0))],
        ],
        vectors,
    )
    dense_parts, dense_got = sum_first(in_blocks(dense_grad))
    dense_got, home, dx0, feed_came, moe_layers, expert_sum, expert_out_sum = tie(
        (dense_got, home, dx0, feed_came, moe_layers, expert_sum, expert_out_sum)
    )
    dense_came = sum_second(dense_parts, dense_got)
    feed_mine, feed_layers = layer_first(sum_total(feed_parts[0], feed_came).astype(LOW))
    output = output_rows(x3, home, pick, target_cols, live_rows)
    moe_left, moe_right = core_last(sum_total(moe_mine, moe_layers))
    dense_came, feed_layers, output = tie((dense_came, feed_layers, output))
    dense_mine, dense_layers = layer_first(sum_total(dense_parts[0], dense_came).astype(LOW))
    feed_left, feed_right = feed_last(sum_total(feed_mine, feed_layers), fold)
    dense_left, dense_right = core_last(sum_total(dense_mine, dense_layers))
    third = 3 * width // 2

    def split(left, right):
        return (
            jnp.concatenate([left[:, :third], right[:, :third]], axis=1),
            jnp.concatenate([left[:, third : 2 * width], right[:, third : 2 * width]], axis=1),
        )

    dense_qkv_sum, dense_proj_sum = split(dense_left, dense_right)
    moe_qkv_sum, moe_proj_sum = split(moe_left, moe_right)
    small_sum = dense_left[:, 2 * width :] + dense_right[:, 2 * width :]
    feed_in_sum = jnp.concatenate(
        [
            half[at * shard_rows : (at + 1) * shard_rows]
            for half in (feed_left, feed_right)
            for at in range(fold)
        ],
        axis=1,
    )
    feed_out_sum = jnp.concatenate(
        [feed_left[fold * shard_rows :], feed_right[fold * shard_rows :]], axis=1
    )
    expert_rows = width // planes
    expert_in_sum = expert_sum[:expert_rows].astype(FULL)[None]
    expert_out_sum = expert_out_sum.astype(FULL)[None]
    bias_rows = expert_sum[expert_rows:].astype(FULL)
    in_bias_sum = lax.dynamic_slice(bias_rows, (0, plane * hidden_part), (1, hidden_part))
    out_bias_sum = lax.dynamic_slice(bias_rows, (1, plane * expert_rows), (1, expert_rows))
    small_turn = small_sum[:, :15].T
    return (
        trimmed(output),
        trimmed(dx0),
        small_turn[0:2],
        small_turn[2:8],
        dense_qkv_sum,
        dense_proj_sum,
        feed_in_sum,
        small_sum[:, 15 + experts : small_cols].reshape(-1),
        feed_out_sum,
        small_turn[8:10],
        small_turn[10:15],
        moe_qkv_sum,
        moe_proj_sum,
        small_sum[:, 15 : 15 + experts],
        expert_in_sum,
        in_bias_sum,
        expert_out_sum,
        out_bias_sum,
    )


def solution(mesh):
    return jax.shard_map(
        per_device,
        mesh=mesh,
        in_specs=(
            P(("fsdp", "expert"), None, None),
            P(None, ("fsdp", "expert")),
            P(None, ("fsdp", "expert")),
            P(("fsdp", "expert"), None),
            P(("fsdp", "expert"), None),
            P(("fsdp", "expert"), None),
            P(("fsdp", "expert")),
            P(("fsdp", "expert"), None),
            P(None, ("fsdp", "expert")),
            P(None, ("fsdp", "expert")),
            P(("fsdp", "expert"), None),
            P(("fsdp", "expert"), None),
            P(("fsdp", "expert"), None),
            P("expert", "fsdp", None),
            P("expert", "fsdp"),
            P("expert", "fsdp", None),
            P("expert", "fsdp"),
            P(("fsdp", "expert"), None, None),
            P(("fsdp", "expert"), None, None),
            P(("fsdp", "expert")),
            P(("fsdp", "expert"), None, None),
        ),
        out_specs=(
            P(("fsdp", "expert"), None, None),
            P(("fsdp", "expert"), None, None),
            P(None, ("fsdp", "expert")),
            P(None, ("fsdp", "expert")),
            P(("fsdp", "expert"), None),
            P(("fsdp", "expert"), None),
            P(("fsdp", "expert"), None),
            P(("fsdp", "expert")),
            P(("fsdp", "expert"), None),
            P(None, ("fsdp", "expert")),
            P(None, ("fsdp", "expert")),
            P(("fsdp", "expert"), None),
            P(("fsdp", "expert"), None),
            P(("fsdp", "expert"), None),
            P("expert", "fsdp", None),
            P("expert", "fsdp"),
            P("expert", "fsdp", None),
            P("expert", "fsdp"),
        ),
        check_vma=False,
    )
```
